32 devices in a mesh: dp: 4 (over y, core), frame: 2 (over x), lon: 4 (over z).
Axes of the slice: x: 2, y: 2, z: 4, core: 2. Of those that a mesh axis runs over, the one named last changes fastest.
Arguments:
- fields: bfloat16 [4, 2, 4, 1440, 1024], P('dp', 'frame', None, 'lon'), may hold values from -6 to 6
- band_rows: int32 [4, 4], P('dp'), may hold values from 0 to 719
- earliest_past_snapshot: int32 [4], P('dp'), may hold values from 0 to 1
- lat_table: bfloat16 [720, 1024], replicated, may hold values from -3 to 3
- norm_gain: float32 [1024], replicated, may hold values from 0.5 to 1.5
- w_in1: bfloat16 [2, 16, 64, 64], P(None, 'lon'), may hold values from -0.5 to 0.5
- b_in1: float32 [2, 1024], P(None, 'lon'), may hold values from -1.5 to 1.5
- w_out2: bfloat16 [2, 16, 64, 64], P(None, 'lon'), may hold values from -0.5 to 0.5
- b_out2: float32 [2, 1024], P(None, 'lon'), may hold values from -0.25 to 0.25
- w_query: bfloat16 [1024, 1024], replicated, may hold values from -0.1875 to 0.1875
- w_keyval: bfloat16 [1024, 512], replicated, may hold values from -0.1875 to 0.1875
- w_output: bfloat16 [1024, 1024], replicated, may hold values from -0.1875 to 0.1875
- score_scale: float32 [16], replicated, may hold values from 0.5 to 100
- spec_cot: bfloat16 [4, 2, 4, 2, 368, 1024], P('dp', 'frame', None, None, None, 'lon'), may hold values from -0.05517578 to 0.05517578
Outputs:
- predicted_output_fields: bfloat16 [4, 2, 4, 1440, 1024], P('dp', 'frame', None, 'lon')
- mask_coefficient2_derivative: float32 [2, 16, 64, 64], P(None, 'lon')
- mask_offset2_derivative: float32 [2, 1024], P(None, 'lon')
The draws below stay inside these ranges and needn't reach their ends.
All inputs are finite; a program needn't handle non-finite values.
Results may differ from the reference program's by a relative error of at most 0.03.
Values may be sent and summed in bfloat16 or wider, within the bound.
No kernel may reach another device: no remote copies, remote signals or barrier semaphores. Data moves between devices by JAX's collectives and lax.ppermute only.
A program may use at most 64 MiB of HBM per device.

```python
import math
import jax
import jax.numpy as jnp
from jax import lax

D = 1024
LON = 1440
MODES = 368
LAT_ALL = 720
BLK = 64
HD = 64
KVH = 4
LAT_DEV = 4
BATCH = 4
FRAMES = 2
NBLK = 16
HEADS = 16


def draw_band_rows(key, part):
    picked = jax.random.randint(key, (BATCH, LAT_DEV), 0, LAT_ALL, dtype=jnp.int32)
    picked = picked.at[0, 0].set(LAT_ALL - 1)
    return picked.at[0, 1].set(0)


def draw_earliest_past_snapshot(key, part):
    picked = jax.random.randint(key, (BATCH,), 0, FRAMES, dtype=jnp.int32)
    picked = picked.at[0].set(FRAMES - 1)
    return picked.at[1].set(0)


def draw_score_scale(key, part):
    key_base = jax.random.fold_in(key, 0)
    scales = jnp.exp(jax.random.uniform(key_base, (HEADS,), jnp.float32, math.log(0.5), math.log(4.0)))
    return scales.astype(jnp.float32)


def block_levels(stream_key, shape, cuts, low, largest):
    def one(dim, blocks):
        draws = jax.random.uniform(jax.random.fold_in(jax.random.fold_in(stream_key, 6), dim), (blocks,), jnp.float32, low / len(cuts), largest / len(cuts))
        return jnp.repeat(jnp.exp(draws), shape[dim] // blocks).reshape((-1,) + (1,) * (len(shape) - dim - 1))

    level = one(*cuts[0])
    for cut in cuts[1:]:
        level = level * one(*cut)
    return level


def scatter_about(rng, extent, deviation, most, cuts=(), kind=jnp.bfloat16):
    level = block_levels(rng, extent, cuts, -0.22, 0.18) if cuts else 1.0
    result = jax.random.normal(rng, extent, jnp.float32) * deviation * level
    return jnp.minimum(jnp.maximum(result, -most), most).astype(kind)


def setup_inputs(seed: int = 0) -> dict:
    splits = jax.random.split(jax.random.key(seed), 15)
    return {
        "fields": scatter_about(splits[0], (BATCH, FRAMES, LAT_DEV, LON, D), 1.0, 6.0, ((0, 4), (1, 2), (3, 4))),
        "band_rows": draw_band_rows(jax.random.fold_in(splits[14], 71), 0),
        "earliest_past_snapshot": draw_earliest_past_snapshot(jax.random.fold_in(splits[14], 71), 0),
        "lat_table": scatter_about(splits[3], (LAT_ALL, D), 0.5, 3.0),
        "norm_gain": jnp.clip(1.0 + 0.1 * jax.random.normal(splits[4], (D,), jnp.float32), 0.5, 1.5),
        "w_in1": scatter_about(splits[5], (2, NBLK, BLK, BLK), (2 * BLK) ** -0.5, 0.5, ((1, 4),)),
        "b_in1": scatter_about(splits[6], (2, D), 0.3, 1.5, ((1, 4),), jnp.float32),
        "w_out2": scatter_about(splits[7], (2, NBLK, BLK, BLK), (2 * BLK) ** -0.5, 0.5, ((1, 4),)),
        "b_out2": scatter_about(splits[8], (2, D), 0.05, 0.25, ((1, 4),), jnp.float32),
        "w_query": scatter_about(splits[9], (D, D), D ** -0.5, 0.1875),
        "w_keyval": scatter_about(splits[10], (D, 2 * KVH * HD), D ** -0.5, 0.1875),
        "w_output": scatter_about(splits[11], (D, D), D ** -0.5, 0.1875),
        "score_scale": draw_score_scale(jax.random.fold_in(splits[14], 71), 0),
        "spec_cot": scatter_about(splits[13], (BATCH, FRAMES, LAT_DEV, 2, MODES, D), (1.0 / (BATCH * FRAMES * LAT_DEV * MODES) ** 0.5), 0.05517578, ((0, 4), (1, 2), (5, 4))),
    }


def transform_table():
    longitude = jnp.arange(LON, dtype=jnp.int32)
    zonal_wavenumber = jnp.arange(MODES, dtype=jnp.int32)
    turns_mod = longitude[:, None] * zonal_wavenumber[None, :] % LON
    angles = turns_mod.astype(jnp.float32) * (2.0 * math.pi / LON)
    return jnp.concatenate([jnp.cos(angles), -jnp.sin(angles)], axis=1).astype(jnp.bfloat16)

def inverse_table(forward):
    zonal_wavenumber = jnp.arange(MODES, dtype=jnp.int32)
    factor = jnp.where(zonal_wavenumber == 0, 1.0, 2.0).astype(jnp.float32)
    factor = jnp.concatenate([factor, factor])
    return (forward.astype(jnp.float32) * factor[None, :]).astype(jnp.bfloat16)

def block_mix(left, weight):
    return jnp.einsum('rmgc,gce->rmge', left.astype(jnp.float32), weight.astype(jnp.float32))

def filter_modes(spectrum, w_in1, b_in1, w_out2, b_out2):
    spectral_real = spectrum[:, 0]
    spec_im = spectrum[:, 1]
    first_re = jax.nn.relu(block_mix(spectral_real, w_in1[0]) - block_mix(spec_im, w_in1[1]) + b_in1[0]).astype(jnp.bfloat16)
    first_im = jax.nn.relu(block_mix(spectral_real, w_in1[1]) + block_mix(spec_im, w_in1[0]) + b_in1[1]).astype(jnp.bfloat16)
    second_re = (block_mix(first_re, w_out2[0]) - block_mix(first_im, w_out2[1]) + b_out2[0]).astype(jnp.bfloat16)
    second_im = (block_mix(first_re, w_out2[1]) + block_mix(first_im, w_out2[0]) + b_out2[1]).astype(jnp.bfloat16)
    return (first_re, first_im, jnp.concatenate([second_re, second_im], axis=1))

def head_norm(values_in):
    return values_in * lax.rsqrt(lax.optimization_barrier(jnp.mean(values_in * values_in, axis=-1, keepdims=True)) + 1e-06)

def reference(fields, band_rows, earliest_past_snapshot, lat_table, norm_gain, w_in1, b_in1, w_out2, b_out2, w_query, w_keyval, w_output, score_scale, spec_cot):
    forward = transform_table()
    backward = inverse_table(forward)
    scale_t = 1.0 / math.sqrt(LON)
    groups = HEADS // KVH
    onehot = (band_rows[:, :, None] == jnp.arange(LAT_ALL, dtype=jnp.int32)[None, None, :]).astype(jnp.float32)
    embedding = jnp.einsum('blt,td->bld', onehot, lat_table.astype(jnp.float32))
    embed_flat = jnp.broadcast_to(embedding[:, None], (BATCH, FRAMES, LAT_DEV, D)).reshape(BATCH * FRAMES, LAT_DEV, D)
    fields_flat = fields.reshape(BATCH * FRAMES, LAT_DEV, LON, D)
    cot_flat = spec_cot.reshape(BATCH * FRAMES, LAT_DEV, 2, MODES, D)
    offset_first_layer = b_in1.reshape(2, NBLK, BLK)
    bias_two = b_out2.reshape(2, NBLK, BLK)

    def spectral_step(packed):
        snapshot_state, frame_embed, frame_cot = packed
        inputs = snapshot_state.astype(jnp.float32) + frame_embed[:, None, :]
        center = lax.optimization_barrier(jnp.mean(inputs, axis=-1, keepdims=True))
        spread = lax.optimization_barrier(jnp.mean(jnp.square(inputs - center), axis=-1, keepdims=True))
        normed = ((inputs - center) * lax.rsqrt(spread + 1e-05) * norm_gain.astype(jnp.float32)).astype(jnp.bfloat16)
        spectrum = (jnp.einsum('lnd,nk->lkd', normed.astype(jnp.float32), forward.astype(jnp.float32)) * scale_t).astype(jnp.bfloat16)
        spectrum = spectrum.reshape(LAT_DEV, 2, MODES, NBLK, BLK)
        first_re, first_im, mixed = filter_modes(spectrum, w_in1, offset_first_layer, w_out2, bias_two)
        mixed = mixed.reshape(LAT_DEV, 2 * MODES, D)
        grid_part = (jnp.einsum('lkd,nk->lnd', mixed.astype(jnp.float32), backward.astype(jnp.float32)) * scale_t).astype(jnp.bfloat16)
        hidden = (inputs + grid_part.astype(jnp.float32)).astype(jnp.bfloat16)
        cotangent = frame_cot.reshape(LAT_DEV, 2, MODES, NBLK, BLK).astype(jnp.float32)
        real_first = first_re.astype(jnp.float32)
        imag_first = first_im.astype(jnp.float32)
        grad_re = jnp.einsum('lmgc,lmge->gce', real_first, cotangent[:, 0]) + jnp.einsum('lmgc,lmge->gce', imag_first, cotangent[:, 1])
        grad_im = jnp.einsum('lmgc,lmge->gce', real_first, cotangent[:, 1]) - jnp.einsum('lmgc,lmge->gce', imag_first, cotangent[:, 0])
        bias_grad = lax.optimization_barrier(jnp.sum(cotangent, axis=(0, 2))).reshape(2, D)
        return (hidden, jnp.stack([grad_re, grad_im]), bias_grad)
    latent_entire_activation, grad_stack, bias_stack = lax.map(spectral_step, (fields_flat, embed_flat, cot_flat))
    mask_coefficient2_derivative = lax.optimization_barrier(jnp.sum(grad_stack, axis=0))
    mask_offset2_derivative = lax.optimization_barrier(jnp.sum(bias_stack, axis=0))
    latent_entire_activation = latent_entire_activation.reshape(BATCH, FRAMES, LAT_DEV * LON, D)
    site_total = LAT_DEV * LON
    frame_ids = jnp.arange(FRAMES, dtype=jnp.int32)

    def per_example_softmax_mixing(packed):
        hidden_b, first_b = packed
        tokens = hidden_b.reshape(FRAMES * site_total, D)
        query = jnp.dot(tokens, w_query, preferred_element_type=jnp.float32).reshape(FRAMES, site_total, HEADS, HD)
        qnorm = head_norm(query).astype(jnp.bfloat16)
        keyval = jnp.dot(tokens, w_keyval, preferred_element_type=jnp.float32)
        knorm = head_norm(keyval[:, :KVH * HD].reshape(FRAMES, site_total, KVH, HD)).astype(jnp.bfloat16)
        values = keyval[:, KVH * HD:].astype(jnp.bfloat16).reshape(FRAMES, site_total, KVH, HD)
        q_five = qnorm.reshape(FRAMES, site_total, KVH, groups, HD).astype(jnp.float32)
        scores = jnp.einsum('qskgd,tskd->skgqt', q_five, knorm.astype(jnp.float32))
        scores = scores * (score_scale.reshape(KVH, groups, 1, 1) / math.sqrt(HD))
        later = frame_ids[None, :] <= frame_ids[:, None]
        seen = later & ((frame_ids[None, :] >= first_b) | (frame_ids[None, :] == frame_ids[:, None]))
        scores = jnp.where(seen, scores, -1e+30)
        top_score = lax.optimization_barrier(jnp.max(scores, axis=-1, keepdims=True))
        weights = jnp.exp(scores - top_score)
        probs = (weights / lax.optimization_barrier(jnp.sum(weights, axis=-1, keepdims=True))).astype(jnp.bfloat16)
        attended = jnp.einsum('skgqt,tskd->qskgd', probs.astype(jnp.float32), values.astype(jnp.float32)).astype(jnp.bfloat16)
        output = jnp.dot(attended.reshape(FRAMES * site_total, D), w_output, preferred_element_type=jnp.float32)
        return (tokens.astype(jnp.float32) + output).astype(jnp.bfloat16).reshape(FRAMES, LAT_DEV, LON, D)
    predicted_output_fields = lax.map(per_example_softmax_mixing, (latent_entire_activation, earliest_past_snapshot))
    return (predicted_output_fields, mask_coefficient2_derivative, mask_offset2_derivative)
```

```python
import functools
import math

import jax
import jax.numpy as jnp
import ml_dtypes
import numpy as np
from jax import lax
from jax.experimental import pallas as pl
from jax.experimental.pallas import tpu as pltpu
from jax.sharding import PartitionSpec as P


def window_basis(window, length, modes, rank):
    band = 2 * modes - 1
    site = np.arange(window)
    step = np.arange(1, window)
    diagonal = -np.cos(np.pi * (window - 1 - 2 * site) / length) * np.cos(np.pi * band / length)
    beside = np.sin(np.pi * step / length) * np.sin(np.pi * (window - step) / length)
    _, vectors = np.linalg.eigh(np.diag(diagonal) + np.diag(beside, 1) + np.diag(beside, -1))
    basis = vectors[:, ::-1][:, :rank]
    lead = np.argmax(np.abs(basis) > 1e-3, axis=0)
    return basis * np.sign(basis[lead, np.arange(rank)])[None, :]


def window_tables(window, length, modes, rank):
    basis = window_basis(window, length, modes, rank)
    turns = np.arange(length)[:, None] * np.arange(modes)[None, :] % length
    angles = 2.0 * np.pi * turns / length
    table = np.concatenate([np.cos(angles), -np.sin(angles)], axis=1)
    factor = np.where(np.arange(2 * modes) % modes == 0, 1.0, 2.0)
    parts = table.reshape(length // window, window, 2 * modes)
    spread = np.einsum("pnj,nr->prj", parts, basis) / math.sqrt(length)
    fold = np.transpose(spread, (2, 0, 1)).reshape(2 * modes, -1)
    unfold = spread * factor

    def small(array):
        return (np.round(array * 2.0**16) / 2.0**16).astype(ml_dtypes.bfloat16)

    return small(basis), small(fold), small(unfold)


LANES = 256
F32 = jnp.float32
BF16 = jnp.bfloat16


def dot(left, right):
    return jnp.dot(left, right, preferred_element_type=F32)


def row_tiles(rows, size):
    return [(low, min(low + size, rows)) for low in range(0, rows, size)]


def latitude_row(band, block):
    rows = block.astype(F32)
    place = lax.broadcasted_iota(jnp.int32, rows.shape, 0)
    return jnp.sum(jnp.where(place == band % rows.shape[0], rows, 0.0), axis=0, keepdims=True)


def compress_kernel(row, me_ref, band_ref, x_ref, lat_ref, gain_ref, basis_ref, *rest):
    outs, (normed_ref,) = rest[:-1], rest[-1:]
    count = len(outs)
    rows, width = x_ref.shape
    embed = latitude_row(band_ref[0, row], lat_ref[...])
    gain = gain_ref[...]
    for low, high in row_tiles(rows, 16):
        inputs = x_ref[low:high].astype(F32) + embed
        center = jnp.sum(inputs, axis=-1, keepdims=True) * (1.0 / width)
        inputs = inputs - center
        spread = jnp.sum(inputs * inputs, axis=-1, keepdims=True) * (1.0 / width)
        normed_ref[low:high] = (inputs * lax.rsqrt(spread + 1e-05) * gain).astype(BF16)
    for shift, out in enumerate(outs):
        block = lax.rem(me_ref[0] + shift, count)
        columns = pl.ds(pl.multiple_of(block * out.shape[1], out.shape[1]), out.shape[1])
        out[...] = dot(basis_ref[...], normed_ref[:, columns]).astype(BF16)


def filter_kernel(count, me_ref, *refs):
    parts, refs = refs[:count], refs[count:]
    fold_ref, w1_ref, b1_ref, w2_ref, b2_ref, unfold_ref = refs[:6]
    outs, first_ref, whole_ref, mixed_ref = refs[6 : 6 + count], *refs[6 + count :]
    rank, width = parts[0].shape
    modes = first_ref.shape[0] // 2
    me = me_ref[0]
    for shift, part in enumerate(parts):
        owner = lax.rem(me + count - shift, count)
        whole_ref[pl.ds(pl.multiple_of(owner * rank, 16), rank)] = part[...]
    spectrum = dot(fold_ref[...], whole_ref[...]).astype(BF16)
    first = (
        dot(spectrum[:modes], w1_ref[:width])
        + dot(spectrum[modes:], w1_ref[width:])
        + b1_ref[...]
    )
    first = jnp.maximum(first, 0.0).astype(BF16)
    first_ref[:modes] = first[:, :width]
    first_ref[modes:] = first[:, width:]
    mixed = (dot(first, w2_ref[...]) + b2_ref[...]).astype(BF16)
    mixed_ref[:modes] = mixed[:, :width]
    mixed_ref[modes:] = mixed[:, width:]
    for shift, out in enumerate(outs):
        out[...] = dot(unfold_ref[lax.rem(me + shift, count)], mixed_ref[...]).astype(BF16)


def gradient_kernel(*refs):
    *firsts, cot_ref, weight_ref, bias_ref = refs
    modes, width = cot_ref.shape[2:]
    blocks, size = weight_ref.shape[1:3]
    contract = (((0,), (0,)), ((), ()))
    total, bias = 0.0, 0.0
    for row, first_ref in enumerate(firsts):
        real, imag = cot_ref[row, 0], cot_ref[row, 1]
        both = jnp.concatenate([real, imag], axis=1)
        turned = jnp.concatenate([imag, -real], axis=1)
        total += lax.dot_general(first_ref[:modes], both, contract, preferred_element_type=F32)
        total += lax.dot_general(first_ref[modes:], turned, contract, preferred_element_type=F32)
        bias += jnp.sum(both.astype(F32), axis=0, keepdims=True)
    bias_ref[...] = bias
    for part in range(2):
        for block in range(blocks):
            low = block * size
            weight_ref[part, block] = total[low : low + size, part * width + low : part * width + low + size]


def head_scale(values, ones):
    squares = (values * values).astype(BF16)
    return values * lax.rsqrt(dot(squares, ones) + 1e-06)


def head_ones(head_size, value):
    row = lax.broadcasted_iota(jnp.int32, (LANES, LANES), 0) // head_size
    column = lax.broadcasted_iota(jnp.int32, (LANES, LANES), 1) // head_size
    return jnp.where(row == column, value, 0.0).astype(BF16)


def expand_kernel(row, count, head_size, me_ref, band_ref, x_ref, lat_ref, *refs):
    parts, refs = refs[:count], refs[count:]
    basis_ref, w_keyval_ref, hidden_ref, keyval_ref, whole_ref = refs
    width = parts[0].shape[1]
    me = me_ref[0]
    for shift, part in enumerate(parts):
        whole_ref[lax.rem(me + count - shift, count)] = part[...]
    embed = latitude_row(band_ref[0, row], lat_ref[...])
    for block in range(count):
        columns = slice(block * width, block * width + width)
        grid = dot(basis_ref[...], whole_ref[block]).astype(BF16).astype(F32)
        inputs = x_ref[:, columns].astype(F32) + embed[:, columns]
        hidden_ref[:, columns] = (inputs + grid).astype(BF16)
    keyval = dot(hidden_ref[...], w_keyval_ref[...])
    ones = head_ones(head_size, 1.0 / head_size)
    half = keyval.shape[1] // 2
    for low in range(0, half, LANES):
        keyval_ref[:, low : low + LANES] = head_scale(keyval[:, low : low + LANES], ones).astype(BF16)
    keyval_ref[:, half:] = keyval[:, half:].astype(BF16)


def query_kernel(head_size, hidden_ref, w_query_ref, query_ref):
    ones = head_ones(head_size, 1.0 / head_size)
    for low in range(0, query_ref.shape[1], LANES):
        columns = slice(low, low + LANES)
        query = dot(hidden_ref[...], w_query_ref[:, columns])
        query_ref[:, columns] = head_scale(query, ones).astype(BF16)


def repeat_head(pair, upper, head_size):
    lane = lax.broadcasted_iota(jnp.int32, pair.shape, 1)
    rolled = pltpu.roll(pair, head_size, 1)
    first_half = (lane < head_size) != upper
    return jnp.where(first_half, pair, rolled)


def attend_kernel(head_size, seen_ref, query_ref, own_ref, other_ref, hidden_ref, scale_ref, w_ref, *rest):
    out_ref, attended_ref = rest[-2:]
    half = own_ref.shape[1] // 2
    pair_width = 2 * head_size
    ones = head_ones(head_size, 1.0)
    seen = seen_ref[0] > 0
    for head in range(half // head_size):
        pair = slice(head // 2 * pair_width, (head // 2 + 1) * pair_width)
        value_pair = slice(half + pair.start, half + pair.stop)
        upper = head % 2 == 1
        own_key, other_key = own_ref[:, pair].astype(F32), other_ref[:, pair].astype(F32)
        own_value, other_value = own_ref[:, value_pair].astype(F32), other_ref[:, value_pair].astype(F32)
        key_step = repeat_head(other_key - own_key, upper, head_size)
        value = repeat_head(own_value, upper, head_size)
        value_step = repeat_head(other_value - own_value, upper, head_size)
        columns = slice(head * LANES, head * LANES + LANES)
        twice = lambda part: jnp.concatenate([part, part], axis=1)
        product = query_ref[:, columns].astype(F32) * twice(key_step) * scale_ref[:, columns]
        high = product.astype(BF16)
        low = (product - high.astype(F32)).astype(BF16)
        lead = dot(high, ones) + dot(low, ones)
        prob = 1.0 / (1.0 + jnp.exp(-lead))
        prob = jnp.where(seen, prob, 0.0)
        attended_ref[:, columns] = (twice(value) + prob * twice(value_step)).astype(BF16)
    for low in range(0, out_ref.shape[1], LANES):
        columns = slice(low, low + LANES)
        output = dot(attended_ref[...], w_ref[:, columns])
        out_ref[:, columns] = (hidden_ref[:, columns].astype(F32) + output).astype(BF16)


def whole(array):
    return pl.BlockSpec(array.shape, lambda *_, rank=array.ndim: (0,) * rank)


def call(kernel, prefetch, args, specs, outs, scratch, flops, grid=(1,), alias=None, out_specs=None):
    moved = sum(math.prod(a.shape) * a.dtype.itemsize for a in outs) * 2
    return pl.pallas_call(
        kernel,
        grid_spec=pltpu.PrefetchScalarGridSpec(
            num_scalar_prefetch=len(prefetch),
            grid=grid,
            in_specs=specs,
            out_specs=out_specs or [whole(out) for out in outs],
            scratch_shapes=scratch,
        ),
        out_shape=outs,
        input_output_aliases=alias or {},
        compiler_params=pltpu.CompilerParams(vmem_limit_bytes=40 * 1024 * 1024),
        cost_estimate=pl.CostEstimate(flops=flops, bytes_accessed=moved, transcendentals=0),
    )(*prefetch, *args)


def block_diagonal(weight):
    _, blocks, size, _ = weight.shape
    width = blocks * size
    tiled = jnp.tile(weight.reshape(2, width, size), (1, 1, blocks))
    row = lax.broadcasted_iota(jnp.int32, (width, width), 0) // size
    column = lax.broadcasted_iota(jnp.int32, (width, width), 1) // size
    real, imag = jnp.where((row == column)[None], tiled, 0)
    return jnp.concatenate(
        [jnp.concatenate([real, imag], axis=1), jnp.concatenate([-imag, real], axis=1)], axis=0
    )


def swap_blocks(parts, count):
    moved = [
        lax.ppermute(part, "lon", [(i, (i + shift) % count) for i in range(count)])
        for shift, part in enumerate(parts)
        if shift
    ]
    return [parts[0], *moved]


def sum_over(array, axis):
    size = lax.axis_size(axis)
    if size & (size - 1):
        return lax.psum(array, axis)
    step = 1
    while step < size:
        array = array + lax.ppermute(array, axis, [(i, i ^ step) for i in range(size)])
        step *= 2
    return array


def fused_body(
    fields,
    band_rows,
    earliest_past_snapshot,
    lat_table,
    norm_gain,
    w_in1,
    b_in1,
    w_out2,
    b_out2,
    w_query,
    w_keyval,
    w_output,
    score_scale,
    spec_cot,
):
    _, _, lat_rows, window, width = fields.shape
    count = lax.axis_size("lon")
    length = window * count
    modes, local_width = spec_cot.shape[4:]
    _, blocks, block_size, _ = w_in1.shape
    head_size = width // score_scale.shape[0]
    keyval_width = w_keyval.shape[1]
    rank = basis_rank(window, length, modes)
    basis, fold, unfold = (jnp.asarray(a) for a in window_tables(window, length, modes, rank))
    me = jnp.reshape(lax.axis_index("lon"), (1,)).astype(jnp.int32)
    frame = lax.axis_index("frame")
    seen = ((frame == 1) & (earliest_past_snapshot <= 0)).astype(jnp.int32)
    scale_lanes = jnp.repeat(score_scale / math.sqrt(head_size), head_size).reshape(1, width)
    gain = norm_gain.reshape(1, width)
    mix1, mix2 = block_diagonal(w_in1), block_diagonal(w_out2)
    bias1, bias2 = b_in1.reshape(1, -1), b_out2.reshape(1, -1)

    part_shape = jax.ShapeDtypeStruct((rank, local_width), BF16)
    lat_block = 16

    def row_specs(row):
        return [
            pl.BlockSpec((None, None, None, window, width), lambda *_: (0, 0, row, 0, 0)),
            pl.BlockSpec((lat_block, width), lambda _, me, band: (band[0, row] // lat_block, 0)),
        ]

    def compress(row):
        return call(
            functools.partial(compress_kernel, row),
            (me, band_rows),
            (fields, lat_table, gain, basis.T),
            [*row_specs(row), whole(gain), whole(basis.T)],
            [part_shape] * count,
            [pltpu.VMEM((window, width), BF16)],
            2 * rank * window * width,
        )

    def mix(parts):
        args = (*parts, fold, mix1, bias1, mix2, bias2, unfold)
        return call(
            functools.partial(filter_kernel, count),
            (me,),
            args,
            [whole(a) for a in args],
            [*[part_shape] * count, jax.ShapeDtypeStruct((2 * modes, local_width), BF16)],
            [pltpu.VMEM((count * rank, local_width), BF16), pltpu.VMEM((2 * modes, local_width), BF16)],
            16 * modes * local_width * local_width + 8 * modes * local_width * rank * count,
        )

    def expand(row, parts):
        args = (*parts, basis, w_keyval)
        return call(
            functools.partial(expand_kernel, row, count, head_size),
            (me, band_rows),
            (fields, lat_table, *args),
            [*row_specs(row), *[whole(a) for a in args]],
            [
                jax.ShapeDtypeStruct((window, width), BF16),
                jax.ShapeDtypeStruct((window, keyval_width), BF16),
            ],
            [pltpu.VMEM((count, rank, local_width), BF16)],
            2 * window * width * (rank + keyval_width),
        )

    def project(hidden):
        return call(
            functools.partial(query_kernel, head_size),
            (),
            (hidden, w_query),
            [whole(hidden), whole(w_query)],
            [jax.ShapeDtypeStruct(hidden.shape, BF16)],
            [],
            2 * window * width * width,
        )[0]

    def attention(row, query, own, other, hidden, filled):
        args = (query, own, other, hidden, scale_lanes, w_output)
        specs = [whole(a) for a in args]
        alias = None
        if filled is not None:
            alias = {1 + len(args): 0}
            args, specs = (*args, filled), [*specs, pl.BlockSpec(memory_space=pl.ANY)]
        return call(
            functools.partial(attend_kernel, head_size),
            (seen,),
            args,
            specs,
            [jax.ShapeDtypeStruct(fields.shape, BF16)],
            [pltpu.VMEM((window, width), BF16)],
            4 * window * width * width,
            alias=alias,
            out_specs=[pl.BlockSpec((None, None, None, window, width), lambda *_: (0, 0, row, 0, 0))],
        )[0]

    outward = [swap_blocks(compress(row), count) for row in range(lat_rows)]
    homeward, firsts = [], []
    for row in range(lat_rows):
        *parts, first = mix(outward[row])
        homeward.append(swap_blocks(parts, count))
        firsts.append(first)
    cells = []
    for row in range(lat_rows):
        hidden, keyval = expand(row, homeward[row])
        earlier = lax.ppermute(keyval, "frame", [(0, 1)])
        cells.append((project(hidden), keyval, earlier, hidden))

    cotangent = spec_cot.reshape(spec_cot.shape[2:])
    args = (*firsts, cotangent)
    weight, bias = call(
        gradient_kernel,
        (),
        args,
        [whole(a) for a in args],
        [
            jax.ShapeDtypeStruct((2, blocks, block_size, block_size), F32),
            jax.ShapeDtypeStruct((1, 2 * local_width), F32),
        ],
        [],
        8 * lat_rows * modes * local_width * local_width,
    )
    packed = jnp.concatenate([weight.reshape(-1), bias.reshape(-1)]).reshape(-1, 128)
    packed = sum_over(sum_over(packed, "frame"), "dp").reshape(-1)
    cut = weight.size
    filled = None
    for row in range(lat_rows):
        filled = attention(row, *cells[row], filled)
    return (filled, packed[:cut].reshape(weight.shape), packed[cut:].reshape(2, local_width))


def transform_table(length, modes):
    longitude = jnp.arange(length, dtype=jnp.int32)
    zonal_wavenumber = jnp.arange(modes, dtype=jnp.int32)
    turns_mod = longitude[:, None] * zonal_wavenumber[None, :] % length
    angles = turns_mod.astype(jnp.float32) * (2.0 * math.pi / length)
    return jnp.concatenate([jnp.cos(angles), -jnp.sin(angles)], axis=1).astype(jnp.bfloat16)


def inverse_table(forward, modes):
    zonal_wavenumber = jnp.arange(modes, dtype=jnp.int32)
    factor = jnp.where(zonal_wavenumber == 0, 1.0, 2.0).astype(jnp.float32)
    factor = jnp.concatenate([factor, factor])
    return (forward.astype(jnp.float32) * factor[None, :]).astype(jnp.bfloat16)


def block_mix(left, weight):
    return jnp.einsum("rmgc,gce->rmge", left, weight, preferred_element_type=jnp.float32)


def filter_modes(spectrum, w_in1, b_in1, w_out2, b_out2):
    spectral_real = spectrum[:, 0]
    spec_im = spectrum[:, 1]
    first_re = jax.nn.relu(
        block_mix(spectral_real, w_in1[0]) - block_mix(spec_im, w_in1[1]) + b_in1[0]
    ).astype(jnp.bfloat16)
    first_im = jax.nn.relu(
        block_mix(spectral_real, w_in1[1]) + block_mix(spec_im, w_in1[0]) + b_in1[1]
    ).astype(jnp.bfloat16)
    second_re = (
        block_mix(first_re, w_out2[0]) - block_mix(first_im, w_out2[1]) + b_out2[0]
    ).astype(jnp.bfloat16)
    second_im = (
        block_mix(first_re, w_out2[1]) + block_mix(first_im, w_out2[0]) + b_out2[1]
    ).astype(jnp.bfloat16)
    return (first_re, first_im, jnp.concatenate([second_re, second_im], axis=1))


def head_norm(values_in):
    return values_in * lax.rsqrt(jnp.mean(values_in * values_in, axis=-1, keepdims=True) + 1e-06)


def attend(
    queries, keys_all, value_rows_full, query_frame, first_seen, score_scale, kv_heads, head_size
):
    site_count, query_frames, width = queries.shape
    key_frames = keys_all.shape[1]
    groups = width // head_size // kv_heads
    q_five = queries.reshape(site_count, query_frames, kv_heads, groups, head_size)
    k_four = keys_all.reshape(site_count, key_frames, kv_heads, head_size)
    v_four = value_rows_full.reshape(site_count, key_frames, kv_heads, head_size)
    scores = jnp.einsum("sqkgd,stkd->kgqts", q_five, k_four, preferred_element_type=jnp.float32)
    scores = scores * (score_scale.reshape(kv_heads, groups, 1, 1, 1) / math.sqrt(head_size))
    key_ids = jnp.arange(key_frames, dtype=jnp.int32)[None, :, None]
    query_ids = query_frame[:, None, None]
    seen = (key_ids <= query_ids) & (
        (key_ids >= first_seen[None, None, :]) | (key_ids == query_ids)
    )
    scores = jnp.where(seen[None, None], scores, -1e30)
    top_score = jnp.max(scores, axis=-2, keepdims=True)
    weights = jnp.exp(scores - top_score)
    probs = (weights / jnp.sum(weights, axis=-2, keepdims=True)).astype(jnp.bfloat16)
    attended = jnp.einsum("kgqts,stkd->sqkgd", probs, v_four, preferred_element_type=jnp.float32)
    return attended.astype(jnp.bfloat16).reshape(site_count, query_frames, width)


def plain_body(
    fields,
    band_rows,
    earliest_past_snapshot,
    lat_table,
    norm_gain,
    w_in1,
    b_in1,
    w_out2,
    b_out2,
    w_query,
    w_keyval,
    w_output,
    score_scale,
    spec_cot,
):
    samples, _, lat_rows, lon_local, width = fields.shape
    grid_rows = samples * lat_rows
    length = lon_local * lax.axis_size("lon")
    modes = spec_cot.shape[4]
    local_width = spec_cot.shape[5]
    blocks = w_in1.shape[1]
    block_size = w_in1.shape[2]
    forward = transform_table(length, modes)
    backward = inverse_table(forward, modes)
    scale_t = 1.0 / math.sqrt(length)
    lat_count = lat_table.shape[0]
    onehot = (
        band_rows[:, :, None] == jnp.arange(lat_count, dtype=jnp.int32)[None, None, :]
    ).astype(jnp.bfloat16)
    embedding = jnp.dot(
        onehot.reshape(grid_rows, lat_count), lat_table, preferred_element_type=jnp.float32
    )
    inputs = fields[:, 0].astype(jnp.float32) + embedding.reshape(samples, lat_rows, 1, width)
    center = jnp.mean(inputs, axis=-1, keepdims=True)
    spread = jnp.mean(jnp.square(inputs - center), axis=-1, keepdims=True)
    normed = ((inputs - center) * lax.rsqrt(spread + 1e-05) * norm_gain).astype(jnp.bfloat16)
    gathered = lax.all_to_all(
        normed.reshape(grid_rows, lon_local, width), "lon", split_axis=2, concat_axis=1, tiled=True
    )
    spectrum = (
        jnp.einsum("rnc,nk->rkc", gathered, forward, preferred_element_type=jnp.float32) * scale_t
    ).astype(jnp.bfloat16)
    spectrum = spectrum.reshape(grid_rows, 2, modes, blocks, block_size)
    first_re, first_im, mixed = filter_modes(
        spectrum,
        w_in1,
        b_in1.reshape(2, blocks, block_size),
        w_out2,
        b_out2.reshape(2, blocks, block_size),
    )
    mixed = mixed.reshape(grid_rows, 2 * modes, local_width)
    grid_part = (
        jnp.einsum("rkc,nk->rnc", mixed, backward, preferred_element_type=jnp.float32) * scale_t
    ).astype(jnp.bfloat16)
    returned = lax.all_to_all(grid_part, "lon", split_axis=1, concat_axis=2, tiled=True)
    hidden = (
        inputs + returned.reshape(samples, lat_rows, lon_local, width).astype(jnp.float32)
    ).astype(jnp.bfloat16)
    cotangent = spec_cot.reshape(grid_rows, 2, modes, blocks, block_size)
    grad_re = jnp.einsum(
        "rmgc,rmge->gce", first_re, cotangent[:, 0], preferred_element_type=jnp.float32
    )
    grad_re = grad_re + jnp.einsum(
        "rmgc,rmge->gce", first_im, cotangent[:, 1], preferred_element_type=jnp.float32
    )
    grad_im = jnp.einsum(
        "rmgc,rmge->gce", first_re, cotangent[:, 1], preferred_element_type=jnp.float32
    )
    grad_im = grad_im - jnp.einsum(
        "rmgc,rmge->gce", first_im, cotangent[:, 0], preferred_element_type=jnp.float32
    )
    bias_terms = jnp.sum(cotangent.astype(jnp.float32), axis=(0, 2)).reshape(2, local_width)
    mask_coefficient2_derivative, mask_offset2_derivative = lax.psum(
        (jnp.stack([grad_re, grad_im]), bias_terms), ("dp", "frame")
    )
    site_count = grid_rows * lon_local
    tokens = hidden.reshape(site_count, width)
    head_count = score_scale.shape[0]
    head_size = width // head_count
    kv_width = w_keyval.shape[1] // 2
    kv_heads = kv_width // head_size
    query = jnp.dot(tokens, w_query, preferred_element_type=jnp.float32).reshape(
        site_count, head_count, head_size
    )
    qnorm = head_norm(query).astype(jnp.bfloat16).reshape(site_count, 1, width)
    keyval = jnp.dot(tokens, w_keyval, preferred_element_type=jnp.float32)
    knorm = (
        head_norm(keyval[:, :kv_width].reshape(site_count, kv_heads, head_size))
        .astype(jnp.bfloat16)
        .reshape(site_count, 1, kv_width)
    )
    values = keyval[:, kv_width:].astype(jnp.bfloat16).reshape(site_count, 1, kv_width)
    first_seen = jnp.broadcast_to(
        earliest_past_snapshot[:, None], (samples, lat_rows * lon_local)
    ).reshape(site_count)
    own_frame = lax.axis_index("frame")
    keys_all, value_rows_full = (
        lax.all_gather(knorm, "frame", axis=1, tiled=True),
        lax.all_gather(values, "frame", axis=1, tiled=True),
    )
    query_frame = jnp.reshape(own_frame, (1,))
    attended = attend(
        qnorm, keys_all, value_rows_full, query_frame, first_seen, score_scale, kv_heads, head_size
    )
    output = jnp.dot(
        attended.reshape(site_count, width), w_output, preferred_element_type=jnp.float32
    )
    predicted_output_fields = (
        (tokens.astype(jnp.float32) + output)
        .astype(jnp.bfloat16)
        .reshape(samples, 1, lat_rows, lon_local, width)
    )
    return (predicted_output_fields, mask_coefficient2_derivative, mask_offset2_derivative)


def basis_rank(window, length, modes):
    return -(-(window * (2 * modes - 1) // length + 24) // 16) * 16


def body(fields, *rest):
    width, local_width = fields.shape[-1], rest[-1].shape[-1]
    head_size = width // rest[-2].shape[0]
    fits = (
        fields.shape[0] == 1
        and lax.axis_size("frame") == 2
        and local_width % LANES == 0
        and 2 * head_size == 128
        and rest[-4].shape[1] * 2 == width
    )
    return (fused_body if fits else plain_body)(fields, *rest)


def solution(mesh):
    placed = (
        P("dp", "frame", None, "lon", None),
        P("dp", None),
        P("dp"),
        P(),
        P(),
        P(None, "lon", None, None),
        P(None, "lon"),
        P(None, "lon", None, None),
        P(None, "lon"),
        P(),
        P(),
        P(),
        P(),
        P("dp", "frame", None, None, None, "lon"),
    )
    return jax.shard_map(
        body,
        mesh=mesh,
        in_specs=placed,
        out_specs=(P("dp", "frame", None, "lon", None), P(None, "lon", None, None), P(None, "lon")),
        check_vma=False,
    )
```

```python
import functools
import math

import jax
import jax.numpy as jnp
import ml_dtypes
import numpy as np
from jax import lax
from jax.experimental import pallas as pl
from jax.experimental.pallas import tpu as pltpu
from jax.sharding import PartitionSpec as P


def window_basis(window, length, modes, rank):
    band = 2 * modes - 1
    site = np.arange(window)
    step = np.arange(1, window)
    diagonal = -np.cos(np.pi * (window - 1 - 2 * site) / length) * np.cos(np.pi * band / length)
    beside = np.sin(np.pi * step / length) * np.sin(np.pi * (window - step) / length)
    _, vectors = np.linalg.eigh(np.diag(diagonal) + np.diag(beside, 1) + np.diag(beside, -1))
    basis = vectors[:, ::-1][:, :rank]
    lead = np.argmax(np.abs(basis) > 1e-3, axis=0)
    return basis * np.sign(basis[lead, np.arange(rank)])[None, :]


def window_tables(window, length, modes, rank):
    basis = window_basis(window, length, modes, rank)
    turns = np.arange(length)[:, None] * np.arange(modes)[None, :] % length
    angles = 2.0 * np.pi * turns / length
    table = np.concatenate([np.cos(angles), -np.sin(angles)], axis=1)
    factor = np.where(np.arange(2 * modes) % modes == 0, 1.0, 2.0)
    parts = table.reshape(length // window, window, 2 * modes)
    spread = np.einsum("pnj,nr->prj", parts, basis) / math.sqrt(length)
    fold = np.transpose(spread, (2, 0, 1)).reshape(2 * modes, -1)
    unfold = spread * factor

    def small(array):
        return (np.round(array * 2.0**16) / 2.0**16).astype(ml_dtypes.bfloat16)

    return small(basis), small(basis.T), small(fold), small(unfold)


LANES = 256
F32 = jnp.float32
BF16 = jnp.bfloat16


def dot(left, right):
    return jnp.dot(left, right, preferred_element_type=F32)


def row_tiles(rows, size):
    return [(low, min(low + size, rows)) for low in range(0, rows, size)]


def latitude_row(band, block):
    rows = block.astype(F32)
    place = lax.broadcasted_iota(jnp.int32, rows.shape, 0)
    return jnp.sum(jnp.where(place == band % rows.shape[0], rows, 0.0), axis=0, keepdims=True)


def compress_kernel(start, band_ref, x_ref, lat_ref, gain_ref, basis_ref, *rest):
    *outs, normed_ref = rest
    rows, width = x_ref.shape
    embed = latitude_row(band_ref[0, start + pl.program_id(0)], lat_ref[...])
    gain = gain_ref[...]
    for low, high in row_tiles(rows, 16):
        inputs = x_ref[low:high].astype(F32) + embed
        center = jnp.sum(inputs, axis=-1, keepdims=True) * (1.0 / width)
        inputs = inputs - center
        spread = jnp.sum(inputs * inputs, axis=-1, keepdims=True) * (1.0 / width)
        normed_ref[low:high] = (inputs * lax.rsqrt(spread + 1e-05) * gain).astype(BF16)
    size = width // lax.axis_size("lon")
    for block, store in outgoing(outs):
        columns = pl.ds(pl.multiple_of(block * size, size), size)
        store(dot(basis_ref[...], normed_ref[:, columns]).astype(BF16))


def outgoing(outs):
    count = lax.axis_size("lon")
    if len(outs) == 1:
        return [(block, functools.partial(outs[0].__setitem__, block)) for block in range(count)]
    me = lax.axis_index("lon")
    return [
        (lax.rem(me + shift, count), functools.partial(out.__setitem__, ...))
        for shift, out in enumerate(outs)
    ]


def incoming(parts):
    count = lax.axis_size("lon")
    if len(parts) == 1:
        return [(owner, parts[0][owner]) for owner in range(count)]
    me = lax.axis_index("lon")
    return [(lax.rem(me + count - shift, count), part[...]) for shift, part in enumerate(parts)]


def blocks_kernel(w1_ref, w2_ref, mix1_ref, mix2_ref):
    _, blocks, size, _ = w1_ref.shape
    width = blocks * size
    for weight, mix in ((w1_ref, mix1_ref), (w2_ref, mix2_ref)):
        mix[...] = jnp.zeros(mix.shape, mix.dtype)
        for block in range(blocks):
            low = block * size
            here, there = slice(low, low + size), slice(width + low, width + low + size)
            real, imag = weight[0, block], weight[1, block]
            mix[here, here] = real
            mix[here, there] = imag
            mix[there, here] = -imag
            mix[there, there] = real


def filter_kernel(taken, *refs):
    parts, refs = refs[:taken], refs[taken:]
    fold_ref, w1_ref, b1_ref, w2_ref, b2_ref, unfold_ref = refs[:6]
    *outs, first_ref, whole_ref, mixed_ref = refs[6:]
    rank, width = parts[0].shape[-2:]
    modes = first_ref.shape[0] // 2
    for owner, part in incoming(parts):
        whole_ref[pl.ds(pl.multiple_of(owner * rank, 16), rank)] = part
    spectrum = dot(fold_ref[...], whole_ref[...]).astype(BF16)
    first = dot(spectrum[:modes], w1_ref[:width]) + dot(spectrum[modes:], w1_ref[width:])
    first_re = jnp.maximum(first[:, :width] + b1_ref[0:1], 0.0).astype(BF16)
    first_im = jnp.maximum(first[:, width:] + b1_ref[1:2], 0.0).astype(BF16)
    first_ref[:modes] = first_re
    first_ref[modes:] = first_im
    mixed = dot(first_re, w2_ref[:width]) + dot(first_im, w2_ref[width:])
    mixed_ref[:modes] = (mixed[:, :width] + b2_ref[0:1]).astype(BF16)
    mixed_ref[modes:] = (mixed[:, width:] + b2_ref[1:2]).astype(BF16)
    for block, store in outgoing(outs):
        store(dot(unfold_ref[block], mixed_ref[...]).astype(BF16))


def gradient_kernel(size, *refs):
    *firsts, cot_ref, packed_ref = refs
    modes, width = cot_ref.shape[2:]
    contract = (((0,), (0,)), ((), ()))
    total, bias, row = 0.0, 0.0, 0
    for first_ref in firsts:
        for piece in range(first_ref.shape[0]):
            real, imag = cot_ref[row, 0], cot_ref[row, 1]
            both = jnp.concatenate([real, imag], axis=1)
            turned = jnp.concatenate([imag, -real], axis=1)
            first_re, first_im = first_ref[piece, :modes], first_ref[piece, modes:]
            total += lax.dot_general(first_re, both, contract, preferred_element_type=F32)
            total += lax.dot_general(first_im, turned, contract, preferred_element_type=F32)
            bias += jnp.sum(both.astype(F32), axis=0, keepdims=True)
            row += 1
    pair = 2 * size
    lane = lax.broadcasted_iota(jnp.int32, (size, pair), 1)
    out = 0
    for low in range(0, 2 * width, pair):
        left = low % width
        even = total[left : left + size, low : low + pair]
        odd = total[left + size : left + pair, low : low + pair]
        packed_ref[out : out + size] = jnp.where(lane < size, even, odd)
        out += size
    packed_ref[out:] = jnp.zeros((packed_ref.shape[0] - out, pair), F32)
    for place, low in enumerate(range(0, 2 * width, pair)):
        packed_ref[out + place : out + place + 1] = bias[:, low : low + pair]


def unpack_kernel(summed_ref, weight_ref, bias_ref):
    _, blocks, size, _ = weight_ref.shape
    total = summed_ref[...]
    out = 0
    for part in range(2):
        for block in range(0, blocks, 2):
            weight_ref[part, block] = total[out : out + size, :size]
            weight_ref[part, block + 1] = total[out : out + size, size:]
            out += size
    for part in range(2):
        for low in range(0, bias_ref.shape[1], 2 * size):
            bias_ref[part : part + 1, low : low + 2 * size] = total[out : out + 1]
            out += 1


def head_scale(values, ones):
    squares = (values * values).astype(BF16)
    return values * lax.rsqrt(dot(squares, ones) + 1e-06)


def head_ones(head_size, value):
    row = lax.broadcasted_iota(jnp.int32, (LANES, LANES), 0) // head_size
    column = lax.broadcasted_iota(jnp.int32, (LANES, LANES), 1) // head_size
    return jnp.where(row == column, value, 0.0).astype(BF16)


def expand_kernel(start, taken, head_size, band_ref, x_ref, lat_ref, *refs):
    parts, refs = refs[:taken], refs[taken:]
    basis_ref, w_keyval_ref, hidden_ref, keyval_ref, whole_ref = refs
    count, _, width = whole_ref.shape
    for owner, part in incoming(parts):
        whole_ref[owner] = part
    embed = latitude_row(band_ref[0, start + pl.program_id(0)], lat_ref[...])
    for block in range(count):
        columns = slice(block * width, block * width + width)
        grid = dot(basis_ref[...], whole_ref[block]).astype(BF16).astype(F32)
        inputs = x_ref[:, columns].astype(F32) + embed[:, columns]
        hidden_ref[:, columns] = (inputs + grid).astype(BF16)
    keyval = dot(hidden_ref[...], w_keyval_ref[...])
    ones = head_ones(head_size, 1.0 / head_size)
    half = keyval.shape[1] // 2
    for low in range(0, half, LANES):
        keyval_ref[:, low : low + LANES] = head_scale(keyval[:, low : low + LANES], ones).astype(BF16)
    keyval_ref[:, half:] = keyval[:, half:].astype(BF16)


def query_kernel(head_size, hidden_ref, w_query_ref, query_ref):
    ones = head_ones(head_size, 1.0 / head_size)
    for low in range(0, query_ref.shape[1], LANES):
        columns = slice(low, low + LANES)
        query = dot(hidden_ref[...], w_query_ref[:, columns])
        query_ref[:, columns] = head_scale(query, ones).astype(BF16)


def repeat_head(pair, upper, head_size):
    lane = lax.broadcasted_iota(jnp.int32, pair.shape, 1)
    rolled = pltpu.roll(pair, head_size, 1)
    return jnp.where((lane < head_size) != upper, pair, rolled)


def twice(part):
    return jnp.concatenate([part, part], axis=1)


def attend_kernel(head_size, past_ref, scale_ref, query_ref, own_ref, other_ref, hidden_ref, w_ref, *rest):
    out_ref, attended_ref = rest[-2:]
    half = own_ref.shape[1] // 2
    pair_width = 2 * head_size
    group = LANES // head_size
    ones = head_ones(head_size, 1.0)
    lane_head = lax.broadcasted_iota(jnp.int32, (1, LANES), 1) // head_size
    seen = jnp.logical_and(lax.axis_index("frame") == 1, past_ref[0] <= 0)
    for head in range(half // head_size):
        pair = slice(head // 2 * pair_width, (head // 2 + 1) * pair_width)
        value_pair = slice(half + pair.start, half + pair.stop)
        upper = head % 2 == 1
        own_key, other_key = own_ref[:, pair].astype(F32), other_ref[:, pair].astype(F32)
        own_value, other_value = own_ref[:, value_pair].astype(F32), other_ref[:, value_pair].astype(F32)
        key_step = repeat_head(other_key - own_key, upper, head_size)
        value = repeat_head(own_value, upper, head_size)
        value_step = repeat_head(other_value - own_value, upper, head_size)
        columns = slice(head * LANES, head * LANES + LANES)
        scale = jnp.zeros((1, LANES), F32)
        for place in range(group):
            scale = jnp.where(lane_head == place, scale_ref[head * group + place], scale)
        scale = scale * (1.0 / math.sqrt(head_size))
        product = query_ref[:, columns].astype(F32) * twice(key_step) * scale
        high = product.astype(BF16)
        low = (product - high.astype(F32)).astype(BF16)
        lead = dot(high, ones) + dot(low, ones)
        prob = jnp.where(seen, 1.0 / (1.0 + jnp.exp(-lead)), 0.0)
        attended_ref[:, columns] = (twice(value) + prob * twice(value_step)).astype(BF16)
    for low in range(0, out_ref.shape[1], LANES):
        columns = slice(low, low + LANES)
        output = dot(attended_ref[...], w_ref[:, columns])
        out_ref[:, columns] = (hidden_ref[:, columns].astype(F32) + output).astype(BF16)


def fixed(array):
    return pl.BlockSpec(array.shape, lambda *_, rank=len(array.shape): (0,) * rank)


def by_row(array, low=0, lead=0):
    before, after = array.shape[:lead], array.shape[lead + 1 :]
    return pl.BlockSpec(
        (*before, None, *after), lambda i, *_: (0,) * len(before) + (low + i,) + (0,) * len(after)
    )


class Order:
    def __init__(self):
        self.last = None

    def __call__(self, kernel, prefetch, args, specs, outs, out_specs, scratch, flops, grid=(1,), alias=None):
        anywhere = pl.BlockSpec(memory_space=pl.ANY)
        token = jax.ShapeDtypeStruct((8, 128), F32)
        taken = [] if self.last is None else [self.last]
        skip, count = len(prefetch) + len(args), len(outs)

        def ordered(*refs):
            refs = refs[:skip] + refs[skip + len(taken) :]
            give = len(prefetch) + len(args) + count
            kernel(*refs[:give], *refs[give + 1 :])

        *results, self.last = call(
            ordered,
            prefetch,
            (*args, *taken),
            [*specs, *[anywhere] * len(taken)],
            [*outs, token],
            [*out_specs, anywhere],
            scratch,
            flops,
            grid,
            alias,
        )
        return results


def call(kernel, prefetch, args, specs, outs, out_specs, scratch, flops, grid=(1,), alias=None):
    moved = 2 * sum(math.prod(out.shape) * out.dtype.itemsize for out in outs)
    return pl.pallas_call(
        kernel,
        grid_spec=pltpu.PrefetchScalarGridSpec(
            num_scalar_prefetch=len(prefetch),
            grid=grid,
            in_specs=specs,
            out_specs=out_specs,
            scratch_shapes=scratch,
        ),
        out_shape=outs,
        input_output_aliases=alias or {},
        compiler_params=pltpu.CompilerParams(vmem_limit_bytes=VMEM_BYTES),
        cost_estimate=pl.CostEstimate(flops=1024, bytes_accessed=1024, transcendentals=0),
    )(*prefetch, *args)


VMEM_BYTES = 36 * 1024 * 1024


def held(array):
    return pltpu.with_memory_space_constraint(array, pltpu.HBM)


def swap_blocks(parts, count):
    if len(parts) == 1:
        return [lax.all_to_all(parts[0], "lon", 0, 0, tiled=True)]
    moved = [
        lax.ppermute(part, "lon", [(i, (i + shift) % count) for i in range(count)])
        for shift, part in enumerate(parts)
        if shift
    ]
    return [parts[0], *moved]


def exchanges(axis):
    size = lax.axis_size(axis)
    step = 1
    while step < size:
        yield axis, [(i, i ^ step) for i in range(size)]
        step *= 2


def fused_body(
    fields,
    band_rows,
    earliest_past_snapshot,
    lat_table,
    norm_gain,
    w_in1,
    b_in1,
    w_out2,
    b_out2,
    w_query,
    w_keyval,
    w_output,
    score_scale,
    spec_cot,
):
    _, _, lat_rows, window, width = fields.shape
    count = lax.axis_size("lon")
    length = window * count
    modes, local_width = spec_cot.shape[4:]
    _, blocks, block_size, _ = w_in1.shape
    head_size = width // score_scale.shape[0]
    keyval_width = w_keyval.shape[1]
    rank = basis_rank(window, length, modes)
    basis, basis_t, fold, unfold = window_tables(window, length, modes, rank)
    gain = norm_gain.reshape(1, width)

    run = Order()

    def struct(*shape, dtype=BF16):
        return jax.ShapeDtypeStruct(shape, dtype)

    def row_specs(start):
        return [
            pl.BlockSpec((None, None, None, window, width), lambda i, *_: (0, 0, start + i, 0, 0)),
            pl.BlockSpec((16, width), lambda i, band: (band[0, start + i] // 16, 0)),
        ]

    def part_outs(rows, at_once):
        if at_once:
            return [struct(count, rows, rank, local_width)]
        return [struct(rows, rank, local_width)] * count

    def compress(start, rows, at_once):
        outs = part_outs(rows, at_once)
        return run(
            functools.partial(compress_kernel, start),
            (band_rows,),
            (held(fields), held(lat_table), gain, basis_t),
            [*row_specs(start), fixed(gain), fixed(basis_t)],
            outs,
            [by_row(out, lead=len(out.shape) - 3) for out in outs],
            [pltpu.VMEM((window, width), BF16)],
            2 * rows * rank * window * width,
            grid=(rows,),
        )

    def mix(parts, low, rows, at_once):
        args = (fold, mix1, b_in1, mix2, b_out2, unfold)
        outs = [*part_outs(rows, at_once), struct(rows, 2 * modes, local_width)]
        return run(
            functools.partial(filter_kernel, len(parts)),
            (),
            (*parts, *args),
            [*[by_row(part, low, part.ndim - 3) for part in parts], *[fixed(a) for a in args]],
            outs,
            [by_row(out, lead=len(out.shape) - 3) for out in outs],
            [pltpu.VMEM((count * rank, local_width), BF16), pltpu.VMEM((2 * modes, local_width), BF16)],
            rows * (16 * modes * local_width * local_width + 8 * modes * local_width * rank * count),
            grid=(rows,),
        )

    def expand(start, parts, low, rows):
        args = (basis, w_keyval)
        outs = [struct(rows, window, width), struct(rows, window, keyval_width)]
        return run(
            functools.partial(expand_kernel, start, len(parts), head_size),
            (band_rows,),
            (held(fields), held(lat_table), *parts, *args),
            [*row_specs(start), *[by_row(part, low, part.ndim - 3) for part in parts], *[fixed(a) for a in args]],
            outs,
            [by_row(out) for out in outs],
            [pltpu.VMEM((count, rank, local_width), BF16)],
            2 * rows * window * width * (rank + keyval_width),
            grid=(rows,),
        )

    def gradient(firsts):
        args = (*firsts, spec_cot.reshape(spec_cot.shape[2:]))
        packed = struct(blocks * block_size + 8, 2 * block_size, dtype=F32)
        return call(
            functools.partial(gradient_kernel, block_size),
            (),
            args,
            [fixed(a) for a in args],
            [packed],
            [fixed(packed)],
            [],
            8 * lat_rows * modes * local_width * local_width,
        )[0]

    def unpack(summed):
        outs = [struct(*w_out2.shape, dtype=F32), struct(*b_out2.shape, dtype=F32)]
        specs = [fixed(out) for out in outs]
        return call(unpack_kernel, (), (summed,), [fixed(summed)], outs, specs, [], 0)

    def project(hidden):
        return run(
            functools.partial(query_kernel, head_size),
            (),
            (hidden, w_query),
            [by_row(hidden), fixed(w_query)],
            [struct(*hidden.shape)],
            [by_row(hidden)],
            [],
            2 * hidden.size * width,
            grid=(hidden.shape[0],),
        )[0]

    def attention(start, query, own, other, hidden, filled):
        args = (query, own, other, hidden, w_output)
        first_frame = pl.BlockSpec((None, None, *own.shape[1:]), lambda i, *_: (0, i, 0, 0))
        specs = [
            by_row(query),
            by_row(own),
            first_frame if other.ndim > own.ndim else by_row(other),
            by_row(hidden),
            fixed(w_output),
        ]
        alias = None
        if filled is not None:
            alias = {2 + len(args): 0}
            args, specs = (*args, filled), [*specs, pl.BlockSpec(memory_space=pl.ANY)]
        return run(
            functools.partial(attend_kernel, head_size),
            (earliest_past_snapshot, score_scale),
            args,
            specs,
            [struct(*fields.shape)],
            [pl.BlockSpec((None, None, None, window, width), lambda i, *_: (0, 0, start + i, 0, 0))],
            [pltpu.VMEM((window, width), BF16)],
            4 * hidden.size * width,
            grid=(hidden.shape[0],),
            alias=alias,
        )[0]

    received, firsts, homeward, cells = {}, [], {}, {}
    filled = gradients = None
    for step, start, rows, at_once in PLAN:
        if step == "compress":
            parts = swap_blocks(compress(start, rows, at_once), count)
            received.update({start + low: (parts, low) for low in range(rows)})
        elif step == "blocks":
            mixes = [w_in1, w_out2]
            mix_shape = struct(2 * local_width, 2 * local_width)
            mix1, mix2 = run(
                blocks_kernel, (), mixes, [fixed(a) for a in mixes], [mix_shape] * 2, [fixed(mix_shape)] * 2, [], 0
            )
        elif step == "mix":
            *back, first = mix(*received[start], rows, at_once)
            parts = swap_blocks(back, count)
            homeward.update({start + low: (parts, low) for low in range(rows)})
            firsts.append(first)
        elif step == "expand":
            hidden, keyval = expand(start, *homeward[start], rows)
            earlier = lax.all_gather(keyval, "frame") if at_once else lax.ppermute(keyval, "frame", [(0, 1)])
            cells[start] = (keyval, earlier, hidden)
        elif step == "query":
            cells[start] = (project(cells[start][-1]), *cells[start])
        elif step == "attend":
            filled = attention(start, *cells[start], filled)
        elif step == "gradient":
            summed = gradient(firsts)
            for axis, pairs in (*exchanges("frame"), *exchanges("dp")):
                summed = summed + lax.ppermute(summed, axis, pairs)
        elif step == "sum":
            gradients = unpack(summed)
    return (filled, *gradients)


PLAN = (
    ("compress", 0, 2, False),
    ("compress", 2, 2, False),
    ("blocks", 0, 0, False),
    ("mix", 0, 2, False),
    ("mix", 2, 2, False),
    ("expand", 0, 2, False),
    ("query", 0, 2, False),
    ("gradient", 0, 0, False),
    ("expand", 2, 1, False),
    ("query", 2, 1, False),
    ("expand", 3, 1, False),
    ("query", 3, 1, False),
    ("attend", 0, 2, False),
    ("attend", 2, 1, False),
    ("attend", 3, 1, False),
    ("sum", 0, 0, False),
)


def transform_table(length, modes):
    longitude = jnp.arange(length, dtype=jnp.int32)
    zonal_wavenumber = jnp.arange(modes, dtype=jnp.int32)
    turns_mod = longitude[:, None] * zonal_wavenumber[None, :] % length
    angles = turns_mod.astype(jnp.float32) * (2.0 * math.pi / length)
    return jnp.concatenate([jnp.cos(angles), -jnp.sin(angles)], axis=1).astype(jnp.bfloat16)


def inverse_table(forward, modes):
    zonal_wavenumber = jnp.arange(modes, dtype=jnp.int32)
    factor = jnp.where(zonal_wavenumber == 0, 1.0, 2.0).astype(jnp.float32)
    factor = jnp.concatenate([factor, factor])
    return (forward.astype(jnp.float32) * factor[None, :]).astype(jnp.bfloat16)


def block_mix(left, weight):
    return jnp.einsum("rmgc,gce->rmge", left, weight, preferred_element_type=jnp.float32)


def filter_modes(spectrum, w_in1, b_in1, w_out2, b_out2):
    spectral_real = spectrum[:, 0]
    spec_im = spectrum[:, 1]
    first_re = jax.nn.relu(
        block_mix(spectral_real, w_in1[0]) - block_mix(spec_im, w_in1[1]) + b_in1[0]
    ).astype(jnp.bfloat16)
    first_im = jax.nn.relu(
        block_mix(spectral_real, w_in1[1]) + block_mix(spec_im, w_in1[0]) + b_in1[1]
    ).astype(jnp.bfloat16)
    second_re = (
        block_mix(first_re, w_out2[0]) - block_mix(first_im, w_out2[1]) + b_out2[0]
    ).astype(jnp.bfloat16)
    second_im = (
        block_mix(first_re, w_out2[1]) + block_mix(first_im, w_out2[0]) + b_out2[1]
    ).astype(jnp.bfloat16)
    return (first_re, first_im, jnp.concatenate([second_re, second_im], axis=1))


def head_norm(values_in):
    return values_in * lax.rsqrt(jnp.mean(values_in * values_in, axis=-1, keepdims=True) + 1e-06)


def attend(
    queries, keys_all, value_rows_full, query_frame, first_seen, score_scale, kv_heads, head_size
):
    site_count, query_frames, width = queries.shape
    key_frames = keys_all.shape[1]
    groups = width // head_size // kv_heads
    q_five = queries.reshape(site_count, query_frames, kv_heads, groups, head_size)
    k_four = keys_all.reshape(site_count, key_frames, kv_heads, head_size)
    v_four = value_rows_full.reshape(site_count, key_frames, kv_heads, head_size)
    scores = jnp.einsum("sqkgd,stkd->kgqts", q_five, k_four, preferred_element_type=jnp.float32)
    scores = scores * (score_scale.reshape(kv_heads, groups, 1, 1, 1) / math.sqrt(head_size))
    key_ids = jnp.arange(key_frames, dtype=jnp.int32)[None, :, None]
    query_ids = query_frame[:, None, None]
    seen = (key_ids <= query_ids) & (
        (key_ids >= first_seen[None, None, :]) | (key_ids == query_ids)
    )
    scores = jnp.where(seen[None, None], scores, -1e30)
    top_score = jnp.max(scores, axis=-2, keepdims=True)
    weights = jnp.exp(scores - top_score)
    probs = (weights / jnp.sum(weights, axis=-2, keepdims=True)).astype(jnp.bfloat16)
    attended = jnp.einsum("kgqts,stkd->sqkgd", probs, v_four, preferred_element_type=jnp.float32)
    return attended.astype(jnp.bfloat16).reshape(site_count, query_frames, width)


def plain_body(
    fields,
    band_rows,
    earliest_past_snapshot,
    lat_table,
    norm_gain,
    w_in1,
    b_in1,
    w_out2,
    b_out2,
    w_query,
    w_keyval,
    w_output,
    score_scale,
    spec_cot,
):
    samples, _, lat_rows, lon_local, width = fields.shape
    grid_rows = samples * lat_rows
    length = lon_local * lax.axis_size("lon")
    modes = spec_cot.shape[4]
    local_width = spec_cot.shape[5]
    blocks = w_in1.shape[1]
    block_size = w_in1.shape[2]
    forward = transform_table(length, modes)
    backward = inverse_table(forward, modes)
    scale_t = 1.0 / math.sqrt(length)
    lat_count = lat_table.shape[0]
    onehot = (
        band_rows[:, :, None] == jnp.arange(lat_count, dtype=jnp.int32)[None, None, :]
    ).astype(jnp.bfloat16)
    embedding = jnp.dot(
        onehot.reshape(grid_rows, lat_count), lat_table, preferred_element_type=jnp.float32
    )
    inputs = fields[:, 0].astype(jnp.float32) + embedding.reshape(samples, lat_rows, 1, width)
    center = jnp.mean(inputs, axis=-1, keepdims=True)
    spread = jnp.mean(jnp.square(inputs - center), axis=-1, keepdims=True)
    normed = ((inputs - center) * lax.rsqrt(spread + 1e-05) * norm_gain).astype(jnp.bfloat16)
    gathered = lax.all_to_all(
        normed.reshape(grid_rows, lon_local, width), "lon", split_axis=2, concat_axis=1, tiled=True
    )
    spectrum = (
        jnp.einsum("rnc,nk->rkc", gathered, forward, preferred_element_type=jnp.float32) * scale_t
    ).astype(jnp.bfloat16)
    spectrum = spectrum.reshape(grid_rows, 2, modes, blocks, block_size)
    first_re, first_im, mixed = filter_modes(
        spectrum,
        w_in1,
        b_in1.reshape(2, blocks, block_size),
        w_out2,
        b_out2.reshape(2, blocks, block_size),
    )
    mixed = mixed.reshape(grid_rows, 2 * modes, local_width)
    grid_part = (
        jnp.einsum("rkc,nk->rnc", mixed, backward, preferred_element_type=jnp.float32) * scale_t
    ).astype(jnp.bfloat16)
    returned = lax.all_to_all(grid_part, "lon", split_axis=1, concat_axis=2, tiled=True)
    hidden = (
        inputs + returned.reshape(samples, lat_rows, lon_local, width).astype(jnp.float32)
    ).astype(jnp.bfloat16)
    cotangent = spec_cot.reshape(grid_rows, 2, modes, blocks, block_size)
    grad_re = jnp.einsum(
        "rmgc,rmge->gce", first_re, cotangent[:, 0], preferred_element_type=jnp.float32
    )
    grad_re = grad_re + jnp.einsum(
        "rmgc,rmge->gce", first_im, cotangent[:, 1], preferred_element_type=jnp.float32
    )
    grad_im = jnp.einsum(
        "rmgc,rmge->gce", first_re, cotangent[:, 1], preferred_element_type=jnp.float32
    )
    grad_im = grad_im - jnp.einsum(
        "rmgc,rmge->gce", first_im, cotangent[:, 0], preferred_element_type=jnp.float32
    )
    bias_terms = jnp.sum(cotangent.astype(jnp.float32), axis=(0, 2)).reshape(2, local_width)
    mask_coefficient2_derivative, mask_offset2_derivative = lax.psum(
        (jnp.stack([grad_re, grad_im]), bias_terms), ("dp", "frame")
    )
    site_count = grid_rows * lon_local
    tokens = hidden.reshape(site_count, width)
    head_count = score_scale.shape[0]
    head_size = width // head_count
    kv_width = w_keyval.shape[1] // 2
    kv_heads = kv_width // head_size
    query = jnp.dot(tokens, w_query, preferred_element_type=jnp.float32).reshape(
        site_count, head_count, head_size
    )
    qnorm = head_norm(query).astype(jnp.bfloat16).reshape(site_count, 1, width)
    keyval = jnp.dot(tokens, w_keyval, preferred_element_type=jnp.float32)
    knorm = (
        head_norm(keyval[:, :kv_width].reshape(site_count, kv_heads, head_size))
        .astype(jnp.bfloat16)
        .reshape(site_count, 1, kv_width)
    )
    values = keyval[:, kv_width:].astype(jnp.bfloat16).reshape(site_count, 1, kv_width)
    first_seen = jnp.broadcast_to(
        earliest_past_snapshot[:, None], (samples, lat_rows * lon_local)
    ).reshape(site_count)
    own_frame = lax.axis_index("frame")
    keys_all, value_rows_full = (
        lax.all_gather(knorm, "frame", axis=1, tiled=True),
        lax.all_gather(values, "frame", axis=1, tiled=True),
    )
    query_frame = jnp.reshape(own_frame, (1,))
    attended = attend(
        qnorm, keys_all, value_rows_full, query_frame, first_seen, score_scale, kv_heads, head_size
    )
    output = jnp.dot(
        attended.reshape(site_count, width), w_output, preferred_element_type=jnp.float32
    )
    predicted_output_fields = (
        (tokens.astype(jnp.float32) + output)
        .astype(jnp.bfloat16)
        .reshape(samples, 1, lat_rows, lon_local, width)
    )
    return (predicted_output_fields, mask_coefficient2_derivative, mask_offset2_derivative)


def basis_rank(window, length, modes):
    return -(-(window * (2 * modes - 1) // length + 24) // 16) * 16


def body(fields, *rest):
    width, local_width = fields.shape[-1], rest[-1].shape[-1]
    head_size = width // rest[-2].shape[0]
    fits = (
        fields.shape[0] == 1
        and lax.axis_size("frame") == 2
        and local_width % LANES == 0
        and fields.shape[2] == sum(rows for step, _, rows, _ in PLAN if step == "compress")
        and 2 * head_size == 128
        and 2 * rest[4].shape[2] == 128
        and rest[-4].shape[1] * 2 == width
    )
    sizes = [lax.axis_size(axis) for axis in ("frame", "dp")]
    fits = fits and all(size & (size - 1) == 0 for size in sizes)
    return (fused_body if fits else plain_body)(fields, *rest)


def solution(mesh):
    placed = (
        P("dp", "frame", None, "lon", None),
        P("dp", None),
        P("dp"),
        P(),
        P(),
        P(None, "lon", None, None),
        P(None, "lon"),
        P(None, "lon", None, None),
        P(None, "lon"),
        P(),
        P(),
        P(),
        P(),
        P("dp", "frame", None, None, None, "lon"),
    )
    return jax.shard_map(
        body,
        mesh=mesh,
        in_specs=placed,
        out_specs=(P("dp", "frame", None, "lon", None), P(None, "lon", None, None), P(None, "lon")),
        check_vma=False,
    )
```

```python
import functools
import math

import jax
import jax.numpy as jnp
import ml_dtypes
import numpy as np
from jax import lax
from jax.experimental import pallas as pl
from jax.experimental.pallas import tpu as pltpu
from jax.sharding import PartitionSpec as P


def window_basis(window, length, modes, rank):
    band = 2 * modes - 1
    site = np.arange(window)
    step = np.arange(1, window)
    diagonal = -np.cos(np.pi * (window - 1 - 2 * site) / length) * np.cos(np.pi * band / length)
    beside = np.sin(np.pi * step / length) * np.sin(np.pi * (window - step) / length)
    _, vectors = np.linalg.eigh(np.diag(diagonal) + np.diag(beside, 1) + np.diag(beside, -1))
    basis = vectors[:, ::-1][:, :rank]
    lead = np.argmax(np.abs(basis) > 1e-3, axis=0)
    return basis * np.sign(basis[lead, np.arange(rank)])[None, :]


def window_tables(window, length, modes, rank):
    basis = window_basis(window, length, modes, rank)
    turns = np.arange(length)[:, None] * np.arange(modes)[None, :] % length
    angles = 2.0 * np.pi * turns / length
    table = np.concatenate([np.cos(angles), -np.sin(angles)], axis=1)
    factor = np.where(np.arange(2 * modes) % modes == 0, 1.0, 2.0)
    parts = table.reshape(length // window, window, 2 * modes)
    spread = np.einsum("pnj,nr->prj", parts, basis) / math.sqrt(length)
    fold = np.transpose(spread, (2, 0, 1)).reshape(2 * modes, -1)
    unfold = spread * factor

    def small(array):
        return (np.round(array * 2.0**16) / 2.0**16).astype(ml_dtypes.bfloat16)

    return small(basis), small(basis.T), small(fold), small(unfold)


LANES = 256
F32 = jnp.float32
BF16 = jnp.bfloat16


def dot(left, right):
    return jnp.dot(left, right, preferred_element_type=F32)


def row_tiles(rows, size):
    return [(low, min(low + size, rows)) for low in range(0, rows, size)]


def latitude_row(band, block):
    rows = block.astype(F32)
    place = lax.broadcasted_iota(jnp.int32, rows.shape, 0)
    return jnp.sum(jnp.where(place == band % rows.shape[0], rows, 0.0), axis=0, keepdims=True)


def compress_kernel(start, band_ref, x_ref, lat_ref, gain_ref, basis_ref, *rest):
    *outs, normed_ref = rest
    rows, width = x_ref.shape
    embed = latitude_row(band_ref[0, start + pl.program_id(0)], lat_ref[...])
    gain = gain_ref[...]
    for low, high in row_tiles(rows, 16):
        inputs = x_ref[low:high].astype(F32) + embed
        center = jnp.sum(inputs, axis=-1, keepdims=True) * (1.0 / width)
        inputs = inputs - center
        spread = jnp.sum(inputs * inputs, axis=-1, keepdims=True) * (1.0 / width)
        normed_ref[low:high] = (inputs * lax.rsqrt(spread + 1e-05) * gain).astype(BF16)
    size = width // lax.axis_size("lon")
    for block, store in outgoing(outs):
        columns = pl.ds(pl.multiple_of(block * size, size), size)
        store(dot(basis_ref[...], normed_ref[:, columns]).astype(BF16))


def outgoing(outs):
    count = lax.axis_size("lon")
    if len(outs) == 1:
        return [(block, functools.partial(outs[0].__setitem__, block)) for block in range(count)]
    me = lax.axis_index("lon")
    return [
        (lax.rem(me + shift, count), functools.partial(out.__setitem__, ...))
        for shift, out in enumerate(outs)
    ]


def incoming(parts):
    count = lax.axis_size("lon")
    if len(parts) == 1:
        return [(owner, parts[0][owner]) for owner in range(count)]
    me = lax.axis_index("lon")
    return [(lax.rem(me + count - shift, count), part[...]) for shift, part in enumerate(parts)]


def blocks_kernel(w1_ref, w2_ref, mix1_ref, mix2_ref):
    _, blocks, size, _ = w1_ref.shape
    width = blocks * size
    for weight, mix in ((w1_ref, mix1_ref), (w2_ref, mix2_ref)):
        mix[...] = jnp.zeros(mix.shape, mix.dtype)
        for block in range(blocks):
            low = block * size
            here, there = slice(low, low + size), slice(width + low, width + low + size)
            real, imag = weight[0, block], weight[1, block]
            mix[here, here] = real
            mix[here, there] = imag
            mix[there, here] = -imag
            mix[there, there] = real


def filter_kernel(taken, *refs):
    parts, refs = refs[:taken], refs[taken:]
    fold_ref, w1_ref, b1_ref, w2_ref, b2_ref, unfold_ref = refs[:6]
    *outs, first_ref, whole_ref, mixed_ref = refs[6:]
    rank, width = parts[0].shape[-2:]
    modes = first_ref.shape[0] // 2
    for owner, part in incoming(parts):
        whole_ref[pl.ds(pl.multiple_of(owner * rank, 16), rank)] = part
    spectrum = dot(fold_ref[...], whole_ref[...]).astype(BF16)
    first = dot(spectrum[:modes], w1_ref[:width]) + dot(spectrum[modes:], w1_ref[width:])
    first_re = jnp.maximum(first[:, :width] + b1_ref[0:1], 0.0).astype(BF16)
    first_im = jnp.maximum(first[:, width:] + b1_ref[1:2], 0.0).astype(BF16)
    first_ref[:modes] = first_re
    first_ref[modes:] = first_im
    mixed = dot(first_re, w2_ref[:width]) + dot(first_im, w2_ref[width:])
    mixed_ref[:modes] = (mixed[:, :width] + b2_ref[0:1]).astype(BF16)
    mixed_ref[modes:] = (mixed[:, width:] + b2_ref[1:2]).astype(BF16)
    for block, store in outgoing(outs):
        store(dot(unfold_ref[block], mixed_ref[...]).astype(BF16))


def gradient_kernel(size, *refs):
    *firsts, cot_ref, packed_ref = refs
    modes, width = cot_ref.shape[2:]
    contract = (((0,), (0,)), ((), ()))
    total, bias, row = 0.0, 0.0, 0
    for first_ref in firsts:
        for piece in range(first_ref.shape[0]):
            real, imag = cot_ref[row, 0], cot_ref[row, 1]
            both = jnp.concatenate([real, imag], axis=1)
            turned = jnp.concatenate([imag, -real], axis=1)
            first_re, first_im = first_ref[piece, :modes], first_ref[piece, modes:]
            total += lax.dot_general(first_re, both, contract, preferred_element_type=F32)
            total += lax.dot_general(first_im, turned, contract, preferred_element_type=F32)
            bias += jnp.sum(both.astype(F32), axis=0, keepdims=True)
            row += 1
    pair = 2 * size
    lane = lax.broadcasted_iota(jnp.int32, (size, pair), 1)
    out = 0
    for low in range(0, 2 * width, pair):
        left = low % width
        even = total[left : left + size, low : low + pair]
        odd = total[left + size : left + pair, low : low + pair]
        packed_ref[out : out + size] = jnp.where(lane < size, even, odd)
        out += size
    packed_ref[out:] = jnp.zeros((packed_ref.shape[0] - out, pair), F32)
    for place, low in enumerate(range(0, 2 * width, pair)):
        packed_ref[out + place : out + place + 1] = bias[:, low : low + pair]


def unpack_kernel(summed_ref, weight_ref, bias_ref):
    _, blocks, size, _ = weight_ref.shape
    total = summed_ref[...]
    out = 0
    for part in range(2):
        for block in range(0, blocks, 2):
            weight_ref[part, block] = total[out : out + size, :size]
            weight_ref[part, block + 1] = total[out : out + size, size:]
            out += size
    for part in range(2):
        for low in range(0, bias_ref.shape[1], 2 * size):
            bias_ref[part : part + 1, low : low + 2 * size] = total[out : out + 1]
            out += 1


def head_scale(values, ones):
    squares = (values * values).astype(BF16)
    return values * lax.rsqrt(dot(squares, ones) + 1e-06)


def head_ones(head_size, value):
    row = lax.broadcasted_iota(jnp.int32, (LANES, LANES), 0) // head_size
    column = lax.broadcasted_iota(jnp.int32, (LANES, LANES), 1) // head_size
    return jnp.where(row == column, value, 0.0).astype(BF16)


def expand_kernel(start, taken, head_size, band_ref, x_ref, lat_ref, *refs):
    parts, refs = refs[:taken], refs[taken:]
    basis_ref, w_keyval_ref, hidden_ref, *keyval_refs, whole_ref = refs
    count, _, width = whole_ref.shape
    for owner, part in incoming(parts):
        whole_ref[owner] = part
    embed = latitude_row(band_ref[0, start + pl.program_id(0)], lat_ref[...])
    for block in range(count):
        columns = slice(block * width, block * width + width)
        grid = dot(basis_ref[...], whole_ref[block]).astype(BF16).astype(F32)
        inputs = x_ref[:, columns].astype(F32) + embed[:, columns]
        hidden_ref[:, columns] = (inputs + grid).astype(BF16)
    keyval = dot(hidden_ref[...], w_keyval_ref[...])
    ones = head_ones(head_size, 1.0 / head_size)
    half = keyval.shape[1] // 2
    keys = [head_scale(keyval[:, low : low + LANES], ones) for low in range(0, half, LANES)]
    keyval = jnp.concatenate([*keys, keyval[:, half:]], axis=1).astype(BF16)
    low = 0
    for out in keyval_refs:
        out[...] = keyval[:, low : low + out.shape[1]]
        low += out.shape[1]


def query_kernel(head_size, hidden_ref, w_query_ref, query_ref):
    ones = head_ones(head_size, 1.0 / head_size)
    for low in range(0, query_ref.shape[1], LANES):
        columns = slice(low, low + LANES)
        query = dot(hidden_ref[...], w_query_ref[:, columns])
        query_ref[:, columns] = head_scale(query, ones).astype(BF16)


def repeat_head(pair, upper, head_size):
    lane = lax.broadcasted_iota(jnp.int32, pair.shape, 1)
    rolled = pltpu.roll(pair, head_size, 1)
    return jnp.where((lane < head_size) != upper, pair, rolled)


def twice(part):
    return jnp.concatenate([part, part], axis=1)


def attend_kernel(head_size, taken, past_ref, scale_ref, query_ref, *refs):
    own_refs, other_refs, refs = refs[:taken], refs[taken : 2 * taken], refs[2 * taken :]
    hidden_ref, w_ref, *_, out_ref, attended_ref = refs
    half = sum(ref.shape[1] for ref in own_refs) // 2
    pair_width = 2 * head_size
    group = LANES // head_size
    ones = head_ones(head_size, 1.0)
    ones = jnp.concatenate([ones, ones], axis=0)
    lane_head = lax.broadcasted_iota(jnp.int32, (1, LANES), 1) // head_size
    seen = jnp.logical_and(lax.axis_index("frame") == 1, past_ref[0] <= 0)

    def load(refs, low):
        size = refs[0].shape[1]
        return refs[low // size][:, low % size : low % size + pair_width].astype(F32)

    for pair in range(0, half, pair_width):
        key_step = load(other_refs, pair) - load(own_refs, pair)
        own_value = load(own_refs, half + pair)
        reach = jnp.where(seen, 0.5 * (load(other_refs, half + pair) - own_value), 0.0)
        middle = own_value + reach
        for upper in (False, True):
            head = pair // head_size + upper
            columns = slice(head * LANES, head * LANES + LANES)
            scale = jnp.zeros((1, LANES), F32)
            for place in range(group):
                scale = jnp.where(lane_head == place, scale_ref[head * group + place], scale)
            scale = scale * (0.5 / math.sqrt(head_size))
            step = repeat_head(key_step, upper, head_size)
            product = query_ref[:, columns].astype(F32) * twice(step)
            high = product.astype(BF16)
            low = (product - high.astype(F32)).astype(BF16)
            lead = dot(jnp.concatenate([high, low], axis=1), ones)
            share = jnp.tanh(lead * scale)
            middles, reaches = (twice(repeat_head(part, upper, head_size)) for part in (middle, reach))
            attended_ref[:, columns] = (middles + reaches * share).astype(BF16)
    for low in range(0, out_ref.shape[1], LANES):
        columns = slice(low, low + LANES)
        output = dot(attended_ref[...], w_ref[:, columns])
        out_ref[:, columns] = (hidden_ref[:, columns].astype(F32) + output).astype(BF16)


def fixed(array):
    return pl.BlockSpec(array.shape, lambda *_, rank=len(array.shape): (0,) * rank)


def by_row(array, low=0, lead=0):
    before, after = array.shape[:lead], array.shape[lead + 1 :]
    return pl.BlockSpec(
        (*before, None, *after), lambda i, *_: (0,) * len(before) + (low + i,) + (0,) * len(after)
    )


class Order:
    def __init__(self):
        self.last = None

    def __call__(self, kernel, prefetch, args, specs, outs, out_specs, scratch, flops, grid=(1,), alias=None):
        anywhere = pl.BlockSpec(memory_space=pl.ANY)
        token = jax.ShapeDtypeStruct((8, 128), F32)
        taken = [] if self.last is None else [self.last]
        skip, count = len(prefetch) + len(args), len(outs)

        def ordered(*refs):
            refs = refs[:skip] + refs[skip + len(taken) :]
            give = len(prefetch) + len(args) + count
            kernel(*refs[:give], *refs[give + 1 :])

        *results, self.last = call(
            ordered,
            prefetch,
            (*args, *taken),
            [*specs, *[anywhere] * len(taken)],
            [*outs, token],
            [*out_specs, anywhere],
            scratch,
            flops,
            grid,
            alias,
        )
        return results


def call(kernel, prefetch, args, specs, outs, out_specs, scratch, flops, grid=(1,), alias=None):
    moved = 2 * sum(math.prod(out.shape) * out.dtype.itemsize for out in outs)
    return pl.pallas_call(
        kernel,
        grid_spec=pltpu.PrefetchScalarGridSpec(
            num_scalar_prefetch=len(prefetch),
            grid=grid,
            in_specs=specs,
            out_specs=out_specs,
            scratch_shapes=scratch,
        ),
        out_shape=outs,
        input_output_aliases=alias or {},
        compiler_params=pltpu.CompilerParams(vmem_limit_bytes=VMEM_BYTES),
        cost_estimate=pl.CostEstimate(flops=1024, bytes_accessed=1024, transcendentals=0),
    )(*prefetch, *args)


VMEM_BYTES = 36 * 1024 * 1024


def held(array):
    return pltpu.with_memory_space_constraint(array, pltpu.HBM)


def swap_blocks(parts, count):
    if len(parts) == 1:
        return [lax.all_to_all(parts[0], "lon", 0, 0, tiled=True)]
    moved = [
        lax.ppermute(part, "lon", [(i, (i + shift) % count) for i in range(count)])
        for shift, part in enumerate(parts)
        if shift
    ]
    return [parts[0], *moved]


def exchanges(axis):
    size = lax.axis_size(axis)
    step = 1
    while step < size:
        yield axis, [(i, i ^ step) for i in range(size)]
        step *= 2


def fused_body(
    fields,
    band_rows,
    earliest_past_snapshot,
    lat_table,
    norm_gain,
    w_in1,
    b_in1,
    w_out2,
    b_out2,
    w_query,
    w_keyval,
    w_output,
    score_scale,
    spec_cot,
):
    _, _, lat_rows, window, width = fields.shape
    count = lax.axis_size("lon")
    length = window * count
    modes, local_width = spec_cot.shape[4:]
    _, blocks, block_size, _ = w_in1.shape
    head_size = width // score_scale.shape[0]
    keyval_width = w_keyval.shape[1]
    rank = basis_rank(window, length, modes)
    basis, basis_t, fold, unfold = window_tables(window, length, modes, rank)
    gain = norm_gain.reshape(1, width)

    run = Order()

    def struct(*shape, dtype=BF16):
        return jax.ShapeDtypeStruct(shape, dtype)

    def row_specs(start):
        return [
            pl.BlockSpec((None, None, None, window, width), lambda i, *_: (0, 0, start + i, 0, 0)),
            pl.BlockSpec((16, width), lambda i, band: (band[0, start + i] // 16, 0)),
        ]

    def part_outs(rows, at_once):
        if at_once:
            return [struct(count, rows, rank, local_width)]
        return [struct(rows, rank, local_width)] * count

    def compress(start, rows, at_once):
        outs = part_outs(rows, at_once)
        return run(
            functools.partial(compress_kernel, start),
            (band_rows,),
            tuple(held(a) for a in (fields, lat_table, gain, basis_t)),
            [*row_specs(start), fixed(gain), fixed(basis_t)],
            outs,
            [by_row(out, lead=len(out.shape) - 3) for out in outs],
            [pltpu.VMEM((window, width), BF16)],
            2 * rows * rank * window * width,
            grid=(rows,),
        )

    def mix(parts, low, rows, at_once):
        args = (fold, mix1, b_in1, mix2, b_out2, unfold)
        outs = [*part_outs(rows, at_once), struct(rows, 2 * modes, local_width)]
        return run(
            functools.partial(filter_kernel, len(parts)),
            (),
            (*parts, *args),
            [*[by_row(part, low, part.ndim - 3) for part in parts], *[fixed(a) for a in args]],
            outs,
            [by_row(out, lead=len(out.shape) - 3) for out in outs],
            [pltpu.VMEM((count * rank, local_width), BF16), pltpu.VMEM((2 * modes, local_width), BF16)],
            rows * (16 * modes * local_width * local_width + 8 * modes * local_width * rank * count),
            grid=(rows,),
        )

    def expand(start, parts, low, rows, split):
        args = (basis, w_keyval)
        pieces = 2 if split else 1
        outs = [struct(rows, window, width), *[struct(rows, window, keyval_width // pieces)] * pieces]
        return run(
            functools.partial(expand_kernel, start, len(parts), head_size),
            (band_rows,),
            (held(fields), held(lat_table), *parts, *args),
            [*row_specs(start), *[by_row(part, low, part.ndim - 3) for part in parts], *[fixed(a) for a in args]],
            outs,
            [by_row(out) for out in outs],
            [pltpu.VMEM((count, rank, local_width), BF16)],
            2 * rows * window * width * (rank + keyval_width),
            grid=(rows,),
        )

    def gradient(firsts):
        args = (*firsts, spec_cot.reshape(spec_cot.shape[2:]))
        packed = struct(blocks * block_size + 8, 2 * block_size, dtype=F32)
        return call(
            functools.partial(gradient_kernel, block_size),
            (),
            args,
            [fixed(a) for a in args],
            [packed],
            [fixed(packed)],
            [],
            8 * lat_rows * modes * local_width * local_width,
        )[0]

    def unpack(summed):
        outs = [struct(*w_out2.shape, dtype=F32), struct(*b_out2.shape, dtype=F32)]
        specs = [fixed(out) for out in outs]
        return run(unpack_kernel, (), (summed,), [fixed(summed)], outs, specs, [], 0)

    def project(hidden):
        return run(
            functools.partial(query_kernel, head_size),
            (),
            (hidden, w_query),
            [by_row(hidden), fixed(w_query)],
            [struct(*hidden.shape)],
            [by_row(hidden)],
            [],
            2 * hidden.size * width,
            grid=(hidden.shape[0],),
        )[0]

    def attention(start, query, own, other, hidden, filled):
        by_rows = (query, *own, *other, hidden)
        args = (*by_rows, w_output)
        specs = [*[by_row(a) for a in by_rows], fixed(w_output)]
        alias = None
        if filled is not None:
            alias = {2 + len(args): 0}
            args, specs = (*args, filled), [*specs, pl.BlockSpec(memory_space=pl.ANY)]
        return run(
            functools.partial(attend_kernel, head_size, len(own)),
            (earliest_past_snapshot, score_scale),
            args,
            specs,
            [struct(*fields.shape)],
            [pl.BlockSpec((None, None, None, window, width), lambda i, *_: (0, 0, start + i, 0, 0))],
            [pltpu.VMEM((window, width), BF16)],
            4 * hidden.size * width,
            grid=(hidden.shape[0],),
            alias=alias,
        )[0]

    received, firsts, homeward, cells = {}, [], {}, {}
    filled = gradients = None
    for step, start, rows, at_once in PLAN:
        if step == "compress":
            parts = swap_blocks(compress(start, rows, at_once), count)
            received.update({start + low: (parts, low) for low in range(rows)})
        elif step == "blocks":
            mixes = [w_in1, w_out2]
            mix_shape = struct(2 * local_width, 2 * local_width)
            mix1, mix2 = run(
                blocks_kernel, (), mixes, [fixed(a) for a in mixes], [mix_shape] * 2, [fixed(mix_shape)] * 2, [], 0
            )
        elif step == "mix":
            *back, first = mix(*received[start], rows, at_once)
            parts = swap_blocks(back, count)
            homeward.update({start + low: (parts, low) for low in range(rows)})
            firsts.append(first)
        elif step == "expand":
            hidden, *keyval = expand(start, *homeward[start], rows, at_once)
            earlier = [lax.ppermute(part, "frame", [(0, 1)]) for part in keyval]
            cells[start] = (keyval, earlier, hidden)
        elif step == "query":
            cells[start] = (project(cells[start][-1]), *cells[start])
        elif step == "attend":
            filled = attention(start, *cells[start], filled)
        elif step == "gradient":
            summed = gradient(firsts)
            for axis, pairs in (*exchanges("frame"), *exchanges("dp")):
                summed = summed + lax.ppermute(summed, axis, pairs)
        elif step == "sum":
            gradients = unpack(summed)
    return (filled, *gradients)


PLAN = (
    ("compress", 0, 2, False),
    ("compress", 2, 2, False),
    ("blocks", 0, 0, False),
    ("mix", 0, 2, False),
    ("mix", 2, 2, False),
    ("expand", 0, 2, True),
    ("query", 0, 2, False),
    ("gradient", 0, 0, False),
    ("expand", 2, 1, False),
    ("expand", 3, 1, False),
    ("query", 2, 1, False),
    ("query", 3, 1, False),
    ("attend", 0, 2, False),
    ("attend", 2, 1, False),
    ("attend", 3, 1, False),
    ("sum", 0, 0, False),
)


def transform_table(length, modes):
    longitude = jnp.arange(length, dtype=jnp.int32)
    zonal_wavenumber = jnp.arange(modes, dtype=jnp.int32)
    turns_mod = longitude[:, None] * zonal_wavenumber[None, :] % length
    angles = turns_mod.astype(jnp.float32) * (2.0 * math.pi / length)
    return jnp.concatenate([jnp.cos(angles), -jnp.sin(angles)], axis=1).astype(jnp.bfloat16)


def inverse_table(forward, modes):
    zonal_wavenumber = jnp.arange(modes, dtype=jnp.int32)
    factor = jnp.where(zonal_wavenumber == 0, 1.0, 2.0).astype(jnp.float32)
    factor = jnp.concatenate([factor, factor])
    return (forward.astype(jnp.float32) * factor[None, :]).astype(jnp.bfloat16)


def block_mix(left, weight):
    return jnp.einsum("rmgc,gce->rmge", left, weight, preferred_element_type=jnp.float32)


def filter_modes(spectrum, w_in1, b_in1, w_out2, b_out2):
    spectral_real = spectrum[:, 0]
    spec_im = spectrum[:, 1]
    first_re = jax.nn.relu(
        block_mix(spectral_real, w_in1[0]) - block_mix(spec_im, w_in1[1]) + b_in1[0]
    ).astype(jnp.bfloat16)
    first_im = jax.nn.relu(
        block_mix(spectral_real, w_in1[1]) + block_mix(spec_im, w_in1[0]) + b_in1[1]
    ).astype(jnp.bfloat16)
    second_re = (
        block_mix(first_re, w_out2[0]) - block_mix(first_im, w_out2[1]) + b_out2[0]
    ).astype(jnp.bfloat16)
    second_im = (
        block_mix(first_re, w_out2[1]) + block_mix(first_im, w_out2[0]) + b_out2[1]
    ).astype(jnp.bfloat16)
    return (first_re, first_im, jnp.concatenate([second_re, second_im], axis=1))


def head_norm(values_in):
    return values_in * lax.rsqrt(jnp.mean(values_in * values_in, axis=-1, keepdims=True) + 1e-06)


def attend(
    queries, keys_all, value_rows_full, query_frame, first_seen, score_scale, kv_heads, head_size
):
    site_count, query_frames, width = queries.shape
    key_frames = keys_all.shape[1]
    groups = width // head_size // kv_heads
    q_five = queries.reshape(site_count, query_frames, kv_heads, groups, head_size)
    k_four = keys_all.reshape(site_count, key_frames, kv_heads, head_size)
    v_four = value_rows_full.reshape(site_count, key_frames, kv_heads, head_size)
    scores = jnp.einsum("sqkgd,stkd->kgqts", q_five, k_four, preferred_element_type=jnp.float32)
    scores = scores * (score_scale.reshape(kv_heads, groups, 1, 1, 1) / math.sqrt(head_size))
    key_ids = jnp.arange(key_frames, dtype=jnp.int32)[None, :, None]
    query_ids = query_frame[:, None, None]
    seen = (key_ids <= query_ids) & (
        (key_ids >= first_seen[None, None, :]) | (key_ids == query_ids)
    )
    scores = jnp.where(seen[None, None], scores, -1e30)
    top_score = jnp.max(scores, axis=-2, keepdims=True)
    weights = jnp.exp(scores - top_score)
    probs = (weights / jnp.sum(weights, axis=-2, keepdims=True)).astype(jnp.bfloat16)
    attended = jnp.einsum("kgqts,stkd->sqkgd", probs, v_four, preferred_element_type=jnp.float32)
    return attended.astype(jnp.bfloat16).reshape(site_count, query_frames, width)


def plain_body(
    fields,
    band_rows,
    earliest_past_snapshot,
    lat_table,
    norm_gain,
    w_in1,
    b_in1,
    w_out2,
    b_out2,
    w_query,
    w_keyval,
    w_output,
    score_scale,
    spec_cot,
):
    samples, _, lat_rows, lon_local, width = fields.shape
    grid_rows = samples * lat_rows
    length = lon_local * lax.axis_size("lon")
    modes = spec_cot.shape[4]
    local_width = spec_cot.shape[5]
    blocks = w_in1.shape[1]
    block_size = w_in1.shape[2]
    forward = transform_table(length, modes)
    backward = inverse_table(forward, modes)
    scale_t = 1.0 / math.sqrt(length)
    lat_count = lat_table.shape[0]
    onehot = (
        band_rows[:, :, None] == jnp.arange(lat_count, dtype=jnp.int32)[None, None, :]
    ).astype(jnp.bfloat16)
    embedding = jnp.dot(
        onehot.reshape(grid_rows, lat_count), lat_table, preferred_element_type=jnp.float32
    )
    inputs = fields[:, 0].astype(jnp.float32) + embedding.reshape(samples, lat_rows, 1, width)
    center = jnp.mean(inputs, axis=-1, keepdims=True)
    spread = jnp.mean(jnp.square(inputs - center), axis=-1, keepdims=True)
    normed = ((inputs - center) * lax.rsqrt(spread + 1e-05) * norm_gain).astype(jnp.bfloat16)
    gathered = lax.all_to_all(
        normed.reshape(grid_rows, lon_local, width), "lon", split_axis=2, concat_axis=1, tiled=True
    )
    spectrum = (
        jnp.einsum("rnc,nk->rkc", gathered, forward, preferred_element_type=jnp.float32) * scale_t
    ).astype(jnp.bfloat16)
    spectrum = spectrum.reshape(grid_rows, 2, modes, blocks, block_size)
    first_re, first_im, mixed = filter_modes(
        spectrum,
        w_in1,
        b_in1.reshape(2, blocks, block_size),
        w_out2,
        b_out2.reshape(2, blocks, block_size),
    )
    mixed = mixed.reshape(grid_rows, 2 * modes, local_width)
    grid_part = (
        jnp.einsum("rkc,nk->rnc", mixed, backward, preferred_element_type=jnp.float32) * scale_t
    ).astype(jnp.bfloat16)
    returned = lax.all_to_all(grid_part, "lon", split_axis=1, concat_axis=2, tiled=True)
    hidden = (
        inputs + returned.reshape(samples, lat_rows, lon_local, width).astype(jnp.float32)
    ).astype(jnp.bfloat16)
    cotangent = spec_cot.reshape(grid_rows, 2, modes, blocks, block_size)
    grad_re = jnp.einsum(
        "rmgc,rmge->gce", first_re, cotangent[:, 0], preferred_element_type=jnp.float32
    )
    grad_re = grad_re + jnp.einsum(
        "rmgc,rmge->gce", first_im, cotangent[:, 1], preferred_element_type=jnp.float32
    )
    grad_im = jnp.einsum(
        "rmgc,rmge->gce", first_re, cotangent[:, 1], preferred_element_type=jnp.float32
    )
    grad_im = grad_im - jnp.einsum(
        "rmgc,rmge->gce", first_im, cotangent[:, 0], preferred_element_type=jnp.float32
    )
    bias_terms = jnp.sum(cotangent.astype(jnp.float32), axis=(0, 2)).reshape(2, local_width)
    mask_coefficient2_derivative, mask_offset2_derivative = lax.psum(
        (jnp.stack([grad_re, grad_im]), bias_terms), ("dp", "frame")
    )
    site_count = grid_rows * lon_local
    tokens = hidden.reshape(site_count, width)
    head_count = score_scale.shape[0]
    head_size = width // head_count
    kv_width = w_keyval.shape[1] // 2
    kv_heads = kv_width // head_size
    query = jnp.dot(tokens, w_query, preferred_element_type=jnp.float32).reshape(
        site_count, head_count, head_size
    )
    qnorm = head_norm(query).astype(jnp.bfloat16).reshape(site_count, 1, width)
    keyval = jnp.dot(tokens, w_keyval, preferred_element_type=jnp.float32)
    knorm = (
        head_norm(keyval[:, :kv_width].reshape(site_count, kv_heads, head_size))
        .astype(jnp.bfloat16)
        .reshape(site_count, 1, kv_width)
    )
    values = keyval[:, kv_width:].astype(jnp.bfloat16).reshape(site_count, 1, kv_width)
    first_seen = jnp.broadcast_to(
        earliest_past_snapshot[:, None], (samples, lat_rows * lon_local)
    ).reshape(site_count)
    own_frame = lax.axis_index("frame")
    keys_all, value_rows_full = (
        lax.all_gather(knorm, "frame", axis=1, tiled=True),
        lax.all_gather(values, "frame", axis=1, tiled=True),
    )
    query_frame = jnp.reshape(own_frame, (1,))
    attended = attend(
        qnorm, keys_all, value_rows_full, query_frame, first_seen, score_scale, kv_heads, head_size
    )
    output = jnp.dot(
        attended.reshape(site_count, width), w_output, preferred_element_type=jnp.float32
    )
    predicted_output_fields = (
        (tokens.astype(jnp.float32) + output)
        .astype(jnp.bfloat16)
        .reshape(samples, 1, lat_rows, lon_local, width)
    )
    return (predicted_output_fields, mask_coefficient2_derivative, mask_offset2_derivative)


def basis_rank(window, length, modes):
    return -(-(window * (2 * modes - 1) // length + 24) // 16) * 16


def body(fields, *rest):
    width, local_width = fields.shape[-1], rest[-1].shape[-1]
    head_size = width // rest[-2].shape[0]
    fits = (
        fields.shape[0] == 1
        and lax.axis_size("frame") == 2
        and local_width % LANES == 0
        and fields.shape[2] == sum(rows for step, _, rows, _ in PLAN if step == "compress")
        and 2 * head_size == 128
        and 2 * rest[4].shape[2] == 128
        and rest[-4].shape[1] * 2 == width
    )
    sizes = [lax.axis_size(axis) for axis in ("frame", "dp")]
    fits = fits and all(size & (size - 1) == 0 for size in sizes)
    return (fused_body if fits else plain_body)(fields, *rest)


def solution(mesh):
    placed = (
        P("dp", "frame", None, "lon", None),
        P("dp", None),
        P("dp"),
        P(),
        P(),
        P(None, "lon", None, None),
        P(None, "lon"),
        P(None, "lon", None, None),
        P(None, "lon"),
        P(),
        P(),
        P(),
        P(),
        P("dp", "frame", None, None, None, "lon"),
    )
    return jax.shard_map(
        body,
        mesh=mesh,
        in_specs=placed,
        out_specs=(P("dp", "frame", None, "lon", None), P(None, "lon", None, None), P(None, "lon")),
        check_vma=False,
    )
```

```python
import functools
import math

import jax
import jax.numpy as jnp
import ml_dtypes
import numpy as np
from jax import lax
from jax.experimental import pallas as pl
from jax.experimental.pallas import tpu as pltpu
from jax.sharding import PartitionSpec as P


def window_basis(window, length, modes, rank):
    band = 2 * modes - 1
    site = np.arange(window)
    step = np.arange(1, window)
    diagonal = -np.cos(np.pi * (window - 1 - 2 * site) / length) * np.cos(np.pi * band / length)
    beside = np.sin(np.pi * step / length) * np.sin(np.pi * (window - step) / length)
    _, vectors = np.linalg.eigh(np.diag(diagonal) + np.diag(beside, 1) + np.diag(beside, -1))
    basis = vectors[:, ::-1][:, :rank]
    lead = np.argmax(np.abs(basis) > 1e-3, axis=0)
    return basis * np.sign(basis[lead, np.arange(rank)])[None, :]


def window_tables(window, length, modes, rank):
    basis = window_basis(window, length, modes, rank)
    turns = np.arange(length)[:, None] * np.arange(modes)[None, :] % length
    angles = 2.0 * np.pi * turns / length
    table = np.concatenate([np.cos(angles), -np.sin(angles)], axis=1)
    factor = np.where(np.arange(2 * modes) % modes == 0, 1.0, 2.0)
    parts = table.reshape(length // window, window, 2 * modes)
    spread = np.einsum("pnj,nr->prj", parts, basis) / math.sqrt(length)
    fold = np.transpose(spread, (2, 0, 1)).reshape(2 * modes, -1)
    unfold = spread * factor

    def small(array):
        return (np.round(array * 2.0**16) / 2.0**16).astype(ml_dtypes.bfloat16)

    return small(basis), small(basis.T), small(fold), small(unfold)


LANES = 256
F32 = jnp.float32
BF16 = jnp.bfloat16


def dot(left, right):
    return jnp.dot(left, right, preferred_element_type=F32)


def row_tiles(rows, size):
    return [(low, min(low + size, rows)) for low in range(0, rows, size)]


def latitude_row(band, block):
    rows = block.astype(F32)
    place = lax.broadcasted_iota(jnp.int32, rows.shape, 0)
    return jnp.sum(jnp.where(place == band % rows.shape[0], rows, 0.0), axis=0, keepdims=True)


def compress_kernel(start, band_ref, x_ref, lat_ref, gain_ref, basis_ref, *rest):
    *outs, normed_ref = rest
    rows, width = x_ref.shape
    embed = latitude_row(band_ref[0, start + pl.program_id(0)], lat_ref[...])
    gain = gain_ref[...]
    for low, high in row_tiles(rows, 16):
        inputs = x_ref[low:high].astype(F32) + embed
        center = jnp.sum(inputs, axis=-1, keepdims=True) * (1.0 / width)
        inputs = inputs - center
        spread = jnp.sum(inputs * inputs, axis=-1, keepdims=True) * (1.0 / width)
        normed_ref[low:high] = (inputs * lax.rsqrt(spread + 1e-05) * gain).astype(BF16)
    size = width // lax.axis_size("lon")
    for block, store in outgoing(outs):
        columns = pl.ds(pl.multiple_of(block * size, size), size)
        store(dot(basis_ref[...], normed_ref[:, columns]).astype(BF16))


def outgoing(outs):
    count = lax.axis_size("lon")
    if len(outs) == 1:
        return [(block, functools.partial(outs[0].__setitem__, block)) for block in range(count)]
    me = lax.axis_index("lon")
    return [
        (lax.rem(me + shift, count), functools.partial(out.__setitem__, ...))
        for shift, out in enumerate(outs)
    ]


def incoming(parts):
    count = lax.axis_size("lon")
    if len(parts) == 1:
        return [(owner, parts[0][owner]) for owner in range(count)]
    me = lax.axis_index("lon")
    return [(lax.rem(me + count - shift, count), part[...]) for shift, part in enumerate(parts)]


def blocks_kernel(w1_ref, w2_ref, mix1_ref, mix2_ref):
    _, blocks, size, _ = w1_ref.shape
    width = blocks * size
    for weight, mix in ((w1_ref, mix1_ref), (w2_ref, mix2_ref)):
        mix[...] = jnp.zeros(mix.shape, mix.dtype)
        for block in range(blocks):
            low = block * size
            here, there = slice(low, low + size), slice(width + low, width + low + size)
            real, imag = weight[0, block], weight[1, block]
            mix[here, here] = real
            mix[here, there] = imag
            mix[there, here] = -imag
            mix[there, there] = real


def filter_kernel(taken, *refs):
    parts, refs = refs[:taken], refs[taken:]
    fold_ref, w1_ref, b1_ref, w2_ref, b2_ref, first_ref, mixed_ref, whole_ref = refs
    rank, width = parts[0].shape[-2:]
    modes = first_ref.shape[0] // 2
    for owner, part in incoming(parts):
        whole_ref[pl.ds(pl.multiple_of(owner * rank, 16), rank)] = part
    spectrum = dot(fold_ref[...], whole_ref[...]).astype(BF16)
    spectrum = jnp.concatenate([spectrum[:modes], spectrum[modes:]], axis=1)
    first = jnp.maximum(dot(spectrum, w1_ref[...]) + both_parts(b1_ref), 0.0).astype(BF16)
    first_ref[:modes] = first[:, :width]
    first_ref[modes:] = first[:, width:]
    mixed = (dot(first, w2_ref[...]) + both_parts(b2_ref)).astype(BF16)
    mixed_ref[:modes] = mixed[:, :width]
    mixed_ref[modes:] = mixed[:, width:]


def both_parts(ref):
    return jnp.concatenate([ref[0:1], ref[1:2]], axis=1)


def unfold_kernel(mixed_ref, unfold_ref, *outs):
    sums = [(store, dot(unfold_ref[block], mixed_ref[...])) for block, store in outgoing(outs)]
    for store, part in sums:
        store(part.astype(BF16))


def gradient_kernel(size, *refs):
    *firsts, cot_ref, packed_ref = refs
    modes, width = cot_ref.shape[2:]
    contract = (((0,), (0,)), ((), ()))
    total, bias, row = 0.0, 0.0, 0
    for first_ref in firsts:
        for piece in range(first_ref.shape[0]):
            real, imag = cot_ref[row, 0], cot_ref[row, 1]
            both = jnp.concatenate([real, imag], axis=1)
            turned = jnp.concatenate([imag, -real], axis=1)
            first_re, first_im = first_ref[piece, :modes], first_ref[piece, modes:]
            total += lax.dot_general(first_re, both, contract, preferred_element_type=F32)
            total += lax.dot_general(first_im, turned, contract, preferred_element_type=F32)
            bias += jnp.sum(both.astype(F32), axis=0, keepdims=True)
            row += 1
    pair = 2 * size
    lane = lax.broadcasted_iota(jnp.int32, (size, pair), 1)
    out = 0
    for low in range(0, 2 * width, pair):
        left = low % width
        even = total[left : left + size, low : low + pair]
        odd = total[left + size : left + pair, low : low + pair]
        packed_ref[out : out + size] = jnp.where(lane < size, even, odd)
        out += size
    packed_ref[out:] = jnp.zeros((packed_ref.shape[0] - out, pair), F32)
    for place, low in enumerate(range(0, 2 * width, pair)):
        packed_ref[out + place : out + place + 1] = bias[:, low : low + pair]


def unpack_kernel(summed_ref, weight_ref, bias_ref):
    _, blocks, size, _ = weight_ref.shape
    total = summed_ref[...]
    out = 0
    for part in range(2):
        for block in range(0, blocks, 2):
            weight_ref[part, block] = total[out : out + size, :size]
            weight_ref[part, block + 1] = total[out : out + size, size:]
            out += size
    for part in range(2):
        for low in range(0, bias_ref.shape[1], 2 * size):
            bias_ref[part : part + 1, low : low + 2 * size] = total[out : out + 1]
            out += 1


def head_scale(values, ones):
    squares = (values * values).astype(BF16)
    return values * lax.rsqrt(dot(squares, ones) + 1e-06)


def head_ones(head_size, value):
    row = lax.broadcasted_iota(jnp.int32, (LANES, LANES), 0) // head_size
    column = lax.broadcasted_iota(jnp.int32, (LANES, LANES), 1) // head_size
    return jnp.where(row == column, value, 0.0).astype(BF16)


def expand_kernel(start, taken, head_size, band_ref, x_ref, lat_ref, *refs):
    parts, refs = refs[:taken], refs[taken:]
    basis_ref, w_keyval_ref, hidden_ref, *keyval_refs, whole_ref = refs
    count, _, width = whole_ref.shape
    for owner, part in incoming(parts):
        whole_ref[owner] = part
    embed = latitude_row(band_ref[0, start + pl.program_id(0)], lat_ref[...])
    grids = [dot(basis_ref[...], whole_ref[block]).astype(BF16) for block in range(count)]
    inputs = x_ref[...].astype(F32) + embed
    hidden = (inputs + jnp.concatenate(grids, axis=1).astype(F32)).astype(BF16)
    hidden_ref[...] = hidden
    keyval = dot(hidden, w_keyval_ref[...])
    ones = head_ones(head_size, 1.0 / head_size)
    half = keyval.shape[1] // 2
    keys = [head_scale(keyval[:, low : low + LANES], ones) for low in range(0, half, LANES)]
    keyval = jnp.concatenate([*keys, keyval[:, half:]], axis=1).astype(BF16)
    low = 0
    for out in keyval_refs:
        out[...] = keyval[:, low : low + out.shape[1]]
        low += out.shape[1]


def query_kernel(head_size, hidden_ref, w_query_ref, query_ref):
    ones = head_ones(head_size, 1.0 / head_size)
    tiles = [slice(low, low + LANES) for low in range(0, query_ref.shape[1], LANES)]
    queries = [dot(hidden_ref[...], w_query_ref[:, columns]) for columns in tiles]
    means = [dot((query * query).astype(BF16), ones) for query in queries]
    for columns, query, mean in zip(tiles, queries, means):
        query_ref[:, columns] = (query * lax.rsqrt(mean + 1e-06)).astype(BF16)


def repeat_head(pair, upper, head_size):
    lane = lax.broadcasted_iota(jnp.int32, pair.shape, 1)
    rolled = pltpu.roll(pair, head_size, 1)
    return jnp.where((lane < head_size) != upper, pair, rolled)


def twice(part):
    return jnp.concatenate([part, part], axis=1)


def attend_kernel(head_size, groups, past_ref, scale_ref, *refs):
    out_ref = refs[-1]
    w_ref = refs[sum(2 + 2 * taken for _, _, taken in groups)]
    for first, last, taken in groups:
        size = 2 + 2 * taken
        mine, refs = refs[:size], refs[size:]
        row = pl.program_id(0)

        @pl.when(jnp.logical_and(row >= first, row < last))
        def _(mine=mine, taken=taken):
            attend_row(head_size, taken, past_ref, scale_ref, *mine, w_ref, out_ref)


def attend_row(head_size, taken, past_ref, scale_ref, query_ref, *refs):
    own_refs, other_refs, refs = refs[:taken], refs[taken : 2 * taken], refs[2 * taken :]
    hidden_ref, w_ref, out_ref = refs
    half = sum(ref.shape[1] for ref in own_refs) // 2
    pair_width = 2 * head_size
    group = LANES // head_size
    ones = head_ones(head_size, 1.0)
    ones = jnp.concatenate([ones, ones], axis=0)
    lane_head = lax.broadcasted_iota(jnp.int32, (1, LANES), 1) // head_size
    seen = jnp.logical_and(lax.axis_index("frame") == 1, past_ref[0] <= 0)

    def load(refs, low):
        size = refs[0].shape[1]
        return refs[low // size][:, low % size : low % size + pair_width].astype(F32)

    leads, attended = [], []
    heads = range(half // head_size)
    for head in heads:
        pair = head // 2 * pair_width
        step = repeat_head(load(other_refs, pair) - load(own_refs, pair), head % 2 == 1, head_size)
        product = query_ref[:, head * LANES : head * LANES + LANES].astype(F32) * twice(step)
        high = product.astype(BF16)
        low = (product - high.astype(F32)).astype(BF16)
        leads.append(dot(jnp.concatenate([high, low], axis=1), ones))
    for head in heads:
        pair = half + head // 2 * pair_width
        value = load(own_refs, pair)
        reach = jnp.where(seen, 0.5 * (load(other_refs, pair) - value), 0.0)
        scale = jnp.zeros((1, LANES), F32)
        for place in range(group):
            scale = jnp.where(lane_head == place, scale_ref[head * group + place], scale)
        share = jnp.tanh(leads[head] * (scale * (0.5 / math.sqrt(head_size))))
        middle, reach = (twice(repeat_head(part, head % 2 == 1, head_size)) for part in (value + reach, reach))
        attended.append((middle + reach * share).astype(BF16))
    output = dot(jnp.concatenate(attended, axis=1), w_ref[...])
    out_ref[...] = (hidden_ref[...].astype(F32) + output).astype(BF16)


def fixed(array):
    return pl.BlockSpec(array.shape, lambda *_, rank=len(array.shape): (0,) * rank)


def by_row(array, low=0, lead=0):
    before, after = array.shape[:lead], array.shape[lead + 1 :]
    return pl.BlockSpec(
        (*before, None, *after), lambda i, *_: (0,) * len(before) + (low + i,) + (0,) * len(after)
    )


def within(array, start):
    rows, *rest = array.shape
    return pl.BlockSpec(
        (None, *rest), lambda i, *_: (jnp.clip(i - start, 0, rows - 1),) + (0,) * len(rest)
    )


class Order:
    def __init__(self):
        self.last = None
        self.after = []

    def __call__(self, kernel, prefetch, args, specs, outs, out_specs, scratch, flops, grid=(1,), alias=None):
        anywhere = pl.BlockSpec(memory_space=pl.ANY)
        token = jax.ShapeDtypeStruct((8, 128), F32)
        taken = self.after + ([] if self.last is None else [self.last])
        self.after = []
        skip, count = len(prefetch) + len(args), len(outs)

        def ordered(*refs):
            refs = refs[:skip] + refs[skip + len(taken) :]
            give = len(prefetch) + len(args) + count
            kernel(*refs[:give], *refs[give + 1 :])

        *results, self.last = call(
            ordered,
            prefetch,
            tuple(args) + tuple(taken),
            [*specs, *[anywhere] * len(taken)],
            [*outs, token],
            [*out_specs, anywhere],
            scratch,
            flops,
            grid,
            alias,
        )
        return results


def call(kernel, prefetch, args, specs, outs, out_specs, scratch, flops, grid=(1,), alias=None):
    moved = 2 * sum(math.prod(out.shape) * out.dtype.itemsize for out in outs)
    return pl.pallas_call(
        kernel,
        grid_spec=pltpu.PrefetchScalarGridSpec(
            num_scalar_prefetch=len(prefetch),
            grid=grid,
            in_specs=specs,
            out_specs=out_specs,
            scratch_shapes=scratch,
        ),
        out_shape=outs,
        input_output_aliases=alias or {},
        compiler_params=pltpu.CompilerParams(vmem_limit_bytes=VMEM_BYTES),
        cost_estimate=pl.CostEstimate(flops=1024, bytes_accessed=1024, transcendentals=0),
    )(*prefetch, *args)


VMEM_BYTES = 36 * 1024 * 1024


def held(array):
    return pltpu.with_memory_space_constraint(array, pltpu.HBM)


def swap_blocks(parts, count):
    if len(parts) == 1:
        return [lax.all_to_all(parts[0], "lon", 0, 0, tiled=True)]
    moved = [
        lax.ppermute(part, "lon", [(i, (i + shift) % count) for i in range(count)])
        for shift, part in enumerate(parts)
        if shift
    ]
    return [parts[0], *moved]


def exchanges(axis):
    size = lax.axis_size(axis)
    step = 1
    while step < size:
        yield axis, [(i, i ^ step) for i in range(size)]
        step *= 2


def fused_body(
    fields,
    band_rows,
    earliest_past_snapshot,
    lat_table,
    norm_gain,
    w_in1,
    b_in1,
    w_out2,
    b_out2,
    w_query,
    w_keyval,
    w_output,
    score_scale,
    spec_cot,
):
    _, _, lat_rows, window, width = fields.shape
    count = lax.axis_size("lon")
    length = window * count
    modes, local_width = spec_cot.shape[4:]
    _, blocks, block_size, _ = w_in1.shape
    head_size = width // score_scale.shape[0]
    keyval_width = w_keyval.shape[1]
    rank = basis_rank(window, length, modes)
    basis, basis_t, fold, unfold = window_tables(window, length, modes, rank)
    gain = norm_gain.reshape(1, width)

    run = Order()

    def struct(*shape, dtype=BF16):
        return jax.ShapeDtypeStruct(shape, dtype)

    def row_specs(start):
        return [
            pl.BlockSpec((None, None, None, window, width), lambda i, *_: (0, 0, start + i, 0, 0)),
            pl.BlockSpec((16, width), lambda i, band: (band[0, start + i] // 16, 0)),
        ]

    def part_outs(rows, at_once):
        if at_once:
            return [struct(count, rows, rank, local_width)]
        return [struct(rows, rank, local_width)] * count

    def compress(start, rows, at_once):
        outs = part_outs(rows, at_once)
        return run(
            functools.partial(compress_kernel, start),
            (band_rows,),
            tuple(held(a) for a in (fields, lat_table, gain, basis_t)),
            [*row_specs(start), fixed(gain), fixed(basis_t)],
            outs,
            [by_row(out, lead=len(out.shape) - 3) for out in outs],
            [pltpu.VMEM((window, width), BF16)],
            2 * rows * rank * window * width,
            grid=(rows,),
        )

    def mix(parts, low, rows):
        args = (fold, mix1, b_in1, mix2, b_out2)
        outs = [struct(rows, 2 * modes, local_width)] * 2
        return run(
            functools.partial(filter_kernel, len(parts)),
            (),
            (*parts, *args),
            [*[by_row(part, low, part.ndim - 3) for part in parts], *[fixed(a) for a in args]],
            outs,
            [by_row(out) for out in outs],
            [pltpu.VMEM((count * rank, local_width), BF16)],
            rows * (16 * modes * local_width * local_width + 4 * modes * local_width * rank * count),
            grid=(rows,),
        )

    def unmix(mixed, at_once):
        rows = mixed.shape[0]
        outs = part_outs(rows, at_once)
        return run(
            unfold_kernel,
            (),
            (mixed, unfold),
            [by_row(mixed), fixed(unfold)],
            outs,
            [by_row(out, lead=len(out.shape) - 3) for out in outs],
            [],
            rows * 4 * modes * local_width * rank * count,
            grid=(rows,),
        )

    def expand(start, parts, low, rows, split):
        args = (basis, w_keyval)
        pieces = 2 if split else 1
        outs = [struct(rows, window, width), *[struct(rows, window, keyval_width // pieces)] * pieces]
        return run(
            functools.partial(expand_kernel, start, len(parts), head_size),
            (band_rows,),
            (fields, held(lat_table), *parts, *args),
            [*row_specs(start), *[by_row(part, low, part.ndim - 3) for part in parts], *[fixed(a) for a in args]],
            outs,
            [by_row(out) for out in outs],
            [pltpu.VMEM((count, rank, local_width), BF16)],
            2 * rows * window * width * (rank + keyval_width),
            grid=(rows,),
        )

    def gradient(firsts):
        args = (*firsts, spec_cot.reshape(spec_cot.shape[2:]))
        packed = struct(blocks * block_size + 8, 2 * block_size, dtype=F32)
        return run(
            functools.partial(gradient_kernel, block_size),
            (),
            args,
            [fixed(a) for a in args],
            [packed],
            [fixed(packed)],
            [],
            8 * lat_rows * modes * local_width * local_width,
        )[0]

    def unpack(summed):
        outs = [struct(*w_out2.shape, dtype=F32), struct(*b_out2.shape, dtype=F32)]
        specs = [fixed(out) for out in outs]
        return run(unpack_kernel, (), (summed,), [fixed(summed)], outs, specs, [], 0)

    def project(hidden):
        return run(
            functools.partial(query_kernel, head_size),
            (),
            (hidden, w_query),
            [by_row(hidden), fixed(w_query)],
            [struct(*hidden.shape)],
            [by_row(hidden)],
            [],
            2 * hidden.size * width,
            grid=(hidden.shape[0],),
        )[0]

    def attention(start, rows, filled):
        args, specs, groups = [], [], []
        for low in sorted(set(cells) & set(range(start, start + rows))):
            query, own, other, hidden = cells[low]
            mine = (query, *own, *other, hidden)
            groups.append((low - start, low - start + query.shape[0], len(own)))
            args += mine
            specs += [within(a, low - start) for a in mine]
        args.append(w_output)
        specs.append(fixed(w_output))
        alias = None
        if filled is not None:
            alias = {2 + len(args): 0}
            args.append(filled)
            specs.append(pl.BlockSpec(memory_space=pl.ANY))
        return run(
            functools.partial(attend_kernel, head_size, groups),
            (earliest_past_snapshot, score_scale),
            args,
            specs,
            [struct(*fields.shape)],
            [pl.BlockSpec((None, None, None, window, width), lambda i, *_: (0, 0, start + i, 0, 0))],
            [],
            4 * rows * window * width * width,
            grid=(rows,),
            alias=alias,
        )[0]

    predicted = None
    received, mixes, firsts, homeward, cells = {}, {}, [], {}, {}
    for step, start, rows, at_once in PLAN:
        if step == "compress":
            parts = swap_blocks(compress(start, rows, at_once), count)
            received.update({start + low: (parts, low) for low in range(rows)})
        elif step == "blocks":
            weights = [w_in1, w_out2]
            mix_shape = struct(2 * local_width, 2 * local_width)
            mix1, mix2 = run(
                blocks_kernel, (), weights, [fixed(a) for a in weights], [mix_shape] * 2, [fixed(mix_shape)] * 2, [], 0
            )
        elif step == "mix":
            first, mixes[start] = mix(*received[start], rows)
            firsts.append(first)
        elif step == "unmix":
            parts = swap_blocks(unmix(mixes[start], at_once), count)
            homeward.update({start + low: (parts, low) for low in range(rows)})
        elif step == "expand":
            hidden, *keyval = expand(start, *homeward[start], rows, at_once)
            earlier = [lax.ppermute(part, "frame", [(0, 1)]) for part in keyval]
            cells[start] = (keyval, earlier, hidden)
        elif step == "received":
            run.after.append(received[start][0][rows])
        elif step == "returned":
            run.after.append(homeward[start][0][rows])
        elif step == "query":
            cells[start] = (project(cells[start][-1]), *cells[start])
        elif step == "attend":
            predicted = attention(start, rows, predicted)
        elif step == "gradient":
            summed = gradient(firsts)
            rounds = [*exchanges("frame"), *exchanges("dp")]
            crossing = lax.ppermute(summed, *rounds.pop(0))
        elif step == "add":
            summed = summed + crossing
            if rounds:
                crossing = lax.ppermute(summed, *rounds.pop(0))
                run.after.append(summed)
        elif step == "sum":
            gradients = unpack(summed)
    return (predicted, *gradients)


PLAN = (
    ("compress", 0, 2, False),
    ("received", 0, 2, False),
    ("compress", 2, 2, False),
    ("blocks", 0, 0, False),
    ("mix", 0, 2, False),
    ("unmix", 0, 2, False),
    ("mix", 2, 2, False),
    ("gradient", 0, 0, False),
    ("returned", 0, 1, False),
    ("unmix", 2, 2, False),
    ("expand", 0, 2, True),
    ("query", 0, 2, False),
    ("expand", 2, 1, False),
    ("expand", 3, 1, False),
    ("add", 0, 0, False),
    ("query", 2, 1, False),
    ("query", 3, 1, False),
    ("add", 0, 0, False),
    ("attend", 0, 2, False),
    ("attend", 2, 1, False),
    ("add", 0, 0, False),
    ("sum", 0, 0, False),
    ("attend", 3, 1, False),
)


def transform_table(length, modes):
    longitude = jnp.arange(length, dtype=jnp.int32)
    zonal_wavenumber = jnp.arange(modes, dtype=jnp.int32)
    turns_mod = longitude[:, None] * zonal_wavenumber[None, :] % length
    angles = turns_mod.astype(jnp.float32) * (2.0 * math.pi / length)
    return jnp.concatenate([jnp.cos(angles), -jnp.sin(angles)], axis=1).astype(jnp.bfloat16)


def inverse_table(forward, modes):
    zonal_wavenumber = jnp.arange(modes, dtype=jnp.int32)
    factor = jnp.where(zonal_wavenumber == 0, 1.0, 2.0).astype(jnp.float32)
    factor = jnp.concatenate([factor, factor])
    return (forward.astype(jnp.float32) * factor[None, :]).astype(jnp.bfloat16)


def block_mix(left, weight):
    return jnp.einsum("rmgc,gce->rmge", left, weight, preferred_element_type=jnp.float32)


def filter_modes(spectrum, w_in1, b_in1, w_out2, b_out2):
    spectral_real = spectrum[:, 0]
    spec_im = spectrum[:, 1]
    first_re = jax.nn.relu(
        block_mix(spectral_real, w_in1[0]) - block_mix(spec_im, w_in1[1]) + b_in1[0]
    ).astype(jnp.bfloat16)
    first_im = jax.nn.relu(
        block_mix(spectral_real, w_in1[1]) + block_mix(spec_im, w_in1[0]) + b_in1[1]
    ).astype(jnp.bfloat16)
    second_re = (
        block_mix(first_re, w_out2[0]) - block_mix(first_im, w_out2[1]) + b_out2[0]
    ).astype(jnp.bfloat16)
    second_im = (
        block_mix(first_re, w_out2[1]) + block_mix(first_im, w_out2[0]) + b_out2[1]
    ).astype(jnp.bfloat16)
    return (first_re, first_im, jnp.concatenate([second_re, second_im], axis=1))


def head_norm(values_in):
    return values_in * lax.rsqrt(jnp.mean(values_in * values_in, axis=-1, keepdims=True) + 1e-06)


def attend(
    queries, keys_all, value_rows_full, query_frame, first_seen, score_scale, kv_heads, head_size
):
    site_count, query_frames, width = queries.shape
    key_frames = keys_all.shape[1]
    groups = width // head_size // kv_heads
    q_five = queries.reshape(site_count, query_frames, kv_heads, groups, head_size)
    k_four = keys_all.reshape(site_count, key_frames, kv_heads, head_size)
    v_four = value_rows_full.reshape(site_count, key_frames, kv_heads, head_size)
    scores = jnp.einsum("sqkgd,stkd->kgqts", q_five, k_four, preferred_element_type=jnp.float32)
    scores = scores * (score_scale.reshape(kv_heads, groups, 1, 1, 1) / math.sqrt(head_size))
    key_ids = jnp.arange(key_frames, dtype=jnp.int32)[None, :, None]
    query_ids = query_frame[:, None, None]
    seen = (key_ids <= query_ids) & (
        (key_ids >= first_seen[None, None, :]) | (key_ids == query_ids)
    )
    scores = jnp.where(seen[None, None], scores, -1e30)
    top_score = jnp.max(scores, axis=-2, keepdims=True)
    weights = jnp.exp(scores - top_score)
    probs = (weights / jnp.sum(weights, axis=-2, keepdims=True)).astype(jnp.bfloat16)
    attended = jnp.einsum("kgqts,stkd->sqkgd", probs, v_four, preferred_element_type=jnp.float32)
    return attended.astype(jnp.bfloat16).reshape(site_count, query_frames, width)


def plain_body(
    fields,
    band_rows,
    earliest_past_snapshot,
    lat_table,
    norm_gain,
    w_in1,
    b_in1,
    w_out2,
    b_out2,
    w_query,
    w_keyval,
    w_output,
    score_scale,
    spec_cot,
):
    samples, _, lat_rows, lon_local, width = fields.shape
    grid_rows = samples * lat_rows
    length = lon_local * lax.axis_size("lon")
    modes = spec_cot.shape[4]
    local_width = spec_cot.shape[5]
    blocks = w_in1.shape[1]
    block_size = w_in1.shape[2]
    forward = transform_table(length, modes)
    backward = inverse_table(forward, modes)
    scale_t = 1.0 / math.sqrt(length)
    lat_count = lat_table.shape[0]
    onehot = (
        band_rows[:, :, None] == jnp.arange(lat_count, dtype=jnp.int32)[None, None, :]
    ).astype(jnp.bfloat16)
    embedding = jnp.dot(
        onehot.reshape(grid_rows, lat_count), lat_table, preferred_element_type=jnp.float32
    )
    inputs = fields[:, 0].astype(jnp.float32) + embedding.reshape(samples, lat_rows, 1, width)
    center = jnp.mean(inputs, axis=-1, keepdims=True)
    spread = jnp.mean(jnp.square(inputs - center), axis=-1, keepdims=True)
    normed = ((inputs - center) * lax.rsqrt(spread + 1e-05) * norm_gain).astype(jnp.bfloat16)
    gathered = lax.all_to_all(
        normed.reshape(grid_rows, lon_local, width), "lon", split_axis=2, concat_axis=1, tiled=True
    )
    spectrum = (
        jnp.einsum("rnc,nk->rkc", gathered, forward, preferred_element_type=jnp.float32) * scale_t
    ).astype(jnp.bfloat16)
    spectrum = spectrum.reshape(grid_rows, 2, modes, blocks, block_size)
    first_re, first_im, mixed = filter_modes(
        spectrum,
        w_in1,
        b_in1.reshape(2, blocks, block_size),
        w_out2,
        b_out2.reshape(2, blocks, block_size),
    )
    mixed = mixed.reshape(grid_rows, 2 * modes, local_width)
    grid_part = (
        jnp.einsum("rkc,nk->rnc", mixed, backward, preferred_element_type=jnp.float32) * scale_t
    ).astype(jnp.bfloat16)
    returned = lax.all_to_all(grid_part, "lon", split_axis=1, concat_axis=2, tiled=True)
    hidden = (
        inputs + returned.reshape(samples, lat_rows, lon_local, width).astype(jnp.float32)
    ).astype(jnp.bfloat16)
    cotangent = spec_cot.reshape(grid_rows, 2, modes, blocks, block_size)
    grad_re = jnp.einsum(
        "rmgc,rmge->gce", first_re, cotangent[:, 0], preferred_element_type=jnp.float32
    )
    grad_re = grad_re + jnp.einsum(
        "rmgc,rmge->gce", first_im, cotangent[:, 1], preferred_element_type=jnp.float32
    )
    grad_im = jnp.einsum(
        "rmgc,rmge->gce", first_re, cotangent[:, 1], preferred_element_type=jnp.float32
    )
    grad_im = grad_im - jnp.einsum(
        "rmgc,rmge->gce", first_im, cotangent[:, 0], preferred_element_type=jnp.float32
    )
    bias_terms = jnp.sum(cotangent.astype(jnp.float32), axis=(0, 2)).reshape(2, local_width)
    mask_coefficient2_derivative, mask_offset2_derivative = lax.psum(
        (jnp.stack([grad_re, grad_im]), bias_terms), ("dp", "frame")
    )
    site_count = grid_rows * lon_local
    tokens = hidden.reshape(site_count, width)
    head_count = score_scale.shape[0]
    head_size = width // head_count
    kv_width = w_keyval.shape[1] // 2
    kv_heads = kv_width // head_size
    query = jnp.dot(tokens, w_query, preferred_element_type=jnp.float32).reshape(
        site_count, head_count, head_size
    )
    qnorm = head_norm(query).astype(jnp.bfloat16).reshape(site_count, 1, width)
    keyval = jnp.dot(tokens, w_keyval, preferred_element_type=jnp.float32)
    knorm = (
        head_norm(keyval[:, :kv_width].reshape(site_count, kv_heads, head_size))
        .astype(jnp.bfloat16)
        .reshape(site_count, 1, kv_width)
    )
    values = keyval[:, kv_width:].astype(jnp.bfloat16).reshape(site_count, 1, kv_width)
    first_seen = jnp.broadcast_to(
        earliest_past_snapshot[:, None], (samples, lat_rows * lon_local)
    ).reshape(site_count)
    own_frame = lax.axis_index("frame")
    keys_all, value_rows_full = (
        lax.all_gather(knorm, "frame", axis=1, tiled=True),
        lax.all_gather(values, "frame", axis=1, tiled=True),
    )
    query_frame = jnp.reshape(own_frame, (1,))
    attended = attend(
        qnorm, keys_all, value_rows_full, query_frame, first_seen, score_scale, kv_heads, head_size
    )
    output = jnp.dot(
        attended.reshape(site_count, width), w_output, preferred_element_type=jnp.float32
    )
    predicted_output_fields = (
        (tokens.astype(jnp.float32) + output)
        .astype(jnp.bfloat16)
        .reshape(samples, 1, lat_rows, lon_local, width)
    )
    return (predicted_output_fields, mask_coefficient2_derivative, mask_offset2_derivative)


def basis_rank(window, length, modes):
    return -(-(window * (2 * modes - 1) // length + 24) // 16) * 16


def body(fields, *rest):
    width, local_width = fields.shape[-1], rest[-1].shape[-1]
    head_size = width // rest[-2].shape[0]
    fits = (
        fields.shape[0] == 1
        and lax.axis_size("frame") == 2
        and local_width % LANES == 0
        and fields.shape[2] == sum(rows for step, _, rows, _ in PLAN if step == "compress")
        and 2 * head_size == 128
        and 2 * rest[4].shape[2] == 128
        and rest[-4].shape[1] * 2 == width
    )
    sizes = [lax.axis_size(axis) for axis in ("frame", "dp")]
    fits = fits and all(size & (size - 1) == 0 for size in sizes)
    return (fused_body if fits else plain_body)(fields, *rest)


def solution(mesh):
    placed = (
        P("dp", "frame", None, "lon", None),
        P("dp", None),
        P("dp"),
        P(),
        P(),
        P(None, "lon", None, None),
        P(None, "lon"),
        P(None, "lon", None, None),
        P(None, "lon"),
        P(),
        P(),
        P(),
        P(),
        P("dp", "frame", None, None, None, "lon"),
    )
    return jax.shard_map(
        body,
        mesh=mesh,
        in_specs=placed,
        out_specs=(P("dp", "frame", None, "lon", None), P(None, "lon", None, None), P(None, "lon")),
        check_vma=False,
    )
```

```python
import functools
import math

import jax
import jax.numpy as jnp
import ml_dtypes
import numpy as np
from jax import lax
from jax.experimental import pallas as pl
from jax.experimental.pallas import tpu as pltpu
from jax.sharding import PartitionSpec as P


def window_basis(window, length, modes, rank):
    band = 2 * modes - 1
    site = np.arange(window)
    step = np.arange(1, window)
    diagonal = -np.cos(np.pi * (window - 1 - 2 * site) / length) * np.cos(np.pi * band / length)
    beside = np.sin(np.pi * step / length) * np.sin(np.pi * (window - step) / length)
    _, vectors = np.linalg.eigh(np.diag(diagonal) + np.diag(beside, 1) + np.diag(beside, -1))
    basis = vectors[:, ::-1][:, :rank]
    lead = np.argmax(np.abs(basis) > 1e-3, axis=0)
    return basis * np.sign(basis[lead, np.arange(rank)])[None, :]


def window_tables(window, length, modes, rank):
    basis = window_basis(window, length, modes, rank)
    turns = np.arange(length)[:, None] * np.arange(modes)[None, :] % length
    angles = 2.0 * np.pi * turns / length
    table = np.concatenate([np.cos(angles), -np.sin(angles)], axis=1)
    factor = np.where(np.arange(2 * modes) % modes == 0, 1.0, 2.0)
    parts = table.reshape(length // window, window, 2 * modes)
    spread = np.einsum("pnj,nr->prj", parts, basis) / math.sqrt(length)
    fold = np.transpose(spread, (2, 0, 1)).reshape(2 * modes, -1)
    unfold = spread * factor

    def small(array):
        return (np.round(array * 2.0**16) / 2.0**16).astype(ml_dtypes.bfloat16)

    return small(basis), small(basis.T), small(fold), small(unfold)


LANES = 256
F32 = jnp.float32
BF16 = jnp.bfloat16


def dot(left, right):
    return jnp.dot(left, right, preferred_element_type=F32)


def row_tiles(rows, size):
    return [(low, min(low + size, rows)) for low in range(0, rows, size)]


def latitude_row(band, block):
    rows = block.astype(F32)
    place = lax.broadcasted_iota(jnp.int32, rows.shape, 0)
    return jnp.sum(jnp.where(place == band % rows.shape[0], rows, 0.0), axis=0, keepdims=True)


def compress_kernel(start, band_ref, x_ref, lat_ref, gain_ref, basis_ref, *rest):
    *outs, normed_ref = rest
    rows, width = x_ref.shape
    embed = latitude_row(band_ref[0, start + pl.program_id(0)], lat_ref[...])
    gain = gain_ref[...]
    for low, high in row_tiles(rows, 16):
        inputs = x_ref[low:high].astype(F32) + embed
        center = jnp.sum(inputs, axis=-1, keepdims=True) * (1.0 / width)
        inputs = inputs - center
        spread = jnp.sum(inputs * inputs, axis=-1, keepdims=True) * (1.0 / width)
        normed_ref[low:high] = (inputs * lax.rsqrt(spread + 1e-05) * gain).astype(BF16)
    size = width // lax.axis_size("lon")
    for block, store in outgoing(outs):
        columns = pl.ds(pl.multiple_of(block * size, size), size)
        store(dot(basis_ref[...], normed_ref[:, columns]).astype(BF16))


def outgoing(outs):
    count = lax.axis_size("lon")
    if len(outs) == 1:
        return [(block, functools.partial(outs[0].__setitem__, block)) for block in range(count)]
    me = lax.axis_index("lon")
    return [
        (lax.rem(me + shift, count), functools.partial(out.__setitem__, ...))
        for shift, out in enumerate(outs)
    ]


def incoming(parts):
    count = lax.axis_size("lon")
    if len(parts) == 1:
        return [(owner, parts[0][owner]) for owner in range(count)]
    me = lax.axis_index("lon")
    return [(lax.rem(me + count - shift, count), part[...]) for shift, part in enumerate(parts)]


def blocks_kernel(w1_ref, w2_ref, mix1_ref, mix2_ref):
    _, blocks, size, _ = w1_ref.shape
    width = blocks * size
    for weight, mix in ((w1_ref, mix1_ref), (w2_ref, mix2_ref)):
        mix[...] = jnp.zeros(mix.shape, mix.dtype)
        for block in range(blocks):
            low = block * size
            here, there = slice(low, low + size), slice(width + low, width + low + size)
            real, imag = weight[0, block], weight[1, block]
            mix[here, here] = real
            mix[here, there] = imag
            mix[there, here] = -imag
            mix[there, there] = real


def filter_kernel(taken, *refs):
    parts, refs = refs[:taken], refs[taken:]
    fold_ref, w1_ref, b1_ref, w2_ref, b2_ref, first_ref, mixed_ref, whole_ref = refs
    rank, width = parts[0].shape[-2:]
    modes = first_ref.shape[0] // 2
    for owner, part in incoming(parts):
        whole_ref[pl.ds(pl.multiple_of(owner * rank, 16), rank)] = part
    spectrum = dot(fold_ref[...], whole_ref[...]).astype(BF16)
    spectrum = jnp.concatenate([spectrum[:modes], spectrum[modes:]], axis=1)
    first = jnp.maximum(dot(spectrum, w1_ref[...]) + both_parts(b1_ref), 0.0).astype(BF16)
    first_ref[:modes] = first[:, :width]
    first_ref[modes:] = first[:, width:]
    mixed = (dot(first, w2_ref[...]) + both_parts(b2_ref)).astype(BF16)
    mixed_ref[:modes] = mixed[:, :width]
    mixed_ref[modes:] = mixed[:, width:]


def both_parts(ref):
    return jnp.concatenate([ref[0:1], ref[1:2]], axis=1)


def unfold_kernel(mixed_ref, unfold_ref, *outs):
    sums = [(store, dot(unfold_ref[block], mixed_ref[...])) for block, store in outgoing(outs)]
    for store, part in sums:
        store(part.astype(BF16))


def gradient_kernel(size, *refs):
    *firsts, cot_ref, packed_ref = refs
    modes, width = cot_ref.shape[2:]
    contract = (((0,), (0,)), ((), ()))
    total, bias, row = 0.0, 0.0, 0
    for first_ref in firsts:
        for piece in range(first_ref.shape[0]):
            real, imag = cot_ref[row, 0], cot_ref[row, 1]
            both = jnp.concatenate([real, imag], axis=1)
            turned = jnp.concatenate([imag, -real], axis=1)
            first_re, first_im = first_ref[piece, :modes], first_ref[piece, modes:]
            total += lax.dot_general(first_re, both, contract, preferred_element_type=F32)
            total += lax.dot_general(first_im, turned, contract, preferred_element_type=F32)
            bias += jnp.sum(both.astype(F32), axis=0, keepdims=True)
            row += 1
    pair = 2 * size
    lane = lax.broadcasted_iota(jnp.int32, (size, pair), 1)
    out = 0
    for low in range(0, 2 * width, pair):
        left = low % width
        even = total[left : left + size, low : low + pair]
        odd = total[left + size : left + pair, low : low + pair]
        packed_ref[out : out + size] = jnp.where(lane < size, even, odd)
        out += size
    packed_ref[out:] = jnp.zeros((packed_ref.shape[0] - out, pair), F32)
    for place, low in enumerate(range(0, 2 * width, pair)):
        packed_ref[out + place : out + place + 1] = bias[:, low : low + pair]


def unpack_kernel(summed_ref, weight_ref, bias_ref):
    _, blocks, size, _ = weight_ref.shape
    total = summed_ref[...]
    out = 0
    for part in range(2):
        for block in range(0, blocks, 2):
            weight_ref[part, block] = total[out : out + size, :size]
            weight_ref[part, block + 1] = total[out : out + size, size:]
            out += size
    for part in range(2):
        for low in range(0, bias_ref.shape[1], 2 * size):
            bias_ref[part : part + 1, low : low + 2 * size] = total[out : out + 1]
            out += 1


def head_scale(values, ones):
    squares = (values * values).astype(BF16)
    return values * lax.rsqrt(dot(squares, ones) + 1e-06)


def head_ones(head_size, value):
    row = lax.broadcasted_iota(jnp.int32, (LANES, LANES), 0) // head_size
    column = lax.broadcasted_iota(jnp.int32, (LANES, LANES), 1) // head_size
    return jnp.where(row == column, value, 0.0).astype(BF16)


def expand_kernel(start, taken, head_size, band_ref, x_ref, lat_ref, *refs):
    parts, refs = refs[:taken], refs[taken:]
    basis_ref, w_keyval_ref, hidden_ref, *keyval_refs, whole_ref = refs
    count, _, width = whole_ref.shape
    for owner, part in incoming(parts):
        whole_ref[owner] = part
    embed = latitude_row(band_ref[0, start + pl.program_id(0)], lat_ref[...])
    grids = [dot(basis_ref[...], whole_ref[block]).astype(BF16) for block in range(count)]
    inputs = x_ref[...].astype(F32) + embed
    hidden = (inputs + jnp.concatenate(grids, axis=1).astype(F32)).astype(BF16)
    hidden_ref[...] = hidden
    keyval = dot(hidden, w_keyval_ref[...])
    ones = head_ones(head_size, 1.0 / head_size)
    half = keyval.shape[1] // 2
    keys = [head_scale(keyval[:, low : low + LANES], ones) for low in range(0, half, LANES)]
    keyval = jnp.concatenate([*keys, keyval[:, half:]], axis=1).astype(BF16)
    low = 0
    for out in keyval_refs:
        out[...] = keyval[:, low : low + out.shape[1]]
        low += out.shape[1]


def query_kernel(head_size, hidden_ref, w_query_ref, query_ref):
    ones = head_ones(head_size, 1.0 / head_size)
    tiles = [slice(low, low + LANES) for low in range(0, query_ref.shape[1], LANES)]
    queries = [dot(hidden_ref[...], w_query_ref[:, columns]) for columns in tiles]
    means = [dot((query * query).astype(BF16), ones) for query in queries]
    for columns, query, mean in zip(tiles, queries, means):
        query_ref[:, columns] = (query * lax.rsqrt(mean + 1e-06)).astype(BF16)


def repeat_head(pair, upper, head_size):
    lane = lax.broadcasted_iota(jnp.int32, pair.shape, 1)
    rolled = pltpu.roll(pair, head_size, 1)
    return jnp.where((lane < head_size) != upper, pair, rolled)


def twice(part):
    return jnp.concatenate([part, part], axis=1)


def attend_kernel(head_size, groups, past_ref, scale_ref, *refs):
    out_ref = refs[-1]
    w_ref = refs[sum(2 + 2 * taken for _, _, taken in groups)]
    for first, last, taken in groups:
        size = 2 + 2 * taken
        mine, refs = refs[:size], refs[size:]
        row = pl.program_id(0)

        @pl.when(jnp.logical_and(row >= first, row < last))
        def _(mine=mine, taken=taken):
            attend_row(head_size, taken, past_ref, scale_ref, *mine, w_ref, out_ref)


def attend_row(head_size, taken, past_ref, scale_ref, query_ref, *refs):
    own_refs, other_refs, refs = refs[:taken], refs[taken : 2 * taken], refs[2 * taken :]
    hidden_ref, w_ref, out_ref = refs
    half = sum(ref.shape[1] for ref in own_refs) // 2
    pair_width = 2 * head_size
    group = LANES // head_size
    ones = head_ones(head_size, 1.0)
    ones = jnp.concatenate([ones, ones], axis=0)
    lane_head = lax.broadcasted_iota(jnp.int32, (1, LANES), 1) // head_size
    seen = jnp.logical_and(lax.axis_index("frame") == 1, past_ref[0] <= 0)

    def load(refs, low):
        size = refs[0].shape[1]
        return refs[low // size][:, low % size : low % size + pair_width].astype(F32)

    leads, attended = [], []
    heads = range(half // head_size)
    for head in heads:
        pair = head // 2 * pair_width
        step = repeat_head(load(other_refs, pair) - load(own_refs, pair), head % 2 == 1, head_size)
        product = query_ref[:, head * LANES : head * LANES + LANES].astype(F32) * twice(step)
        high = product.astype(BF16)
        low = (product - high.astype(F32)).astype(BF16)
        leads.append(dot(jnp.concatenate([high, low], axis=1), ones))
    for head in heads:
        pair = half + head // 2 * pair_width
        value = load(own_refs, pair)
        reach = jnp.where(seen, 0.5 * (load(other_refs, pair) - value), 0.0)
        scale = jnp.zeros((1, LANES), F32)
        for place in range(group):
            scale = jnp.where(lane_head == place, scale_ref[head * group + place], scale)
        share = jnp.tanh(leads[head] * (scale * (0.5 / math.sqrt(head_size))))
        middle, reach = (twice(repeat_head(part, head % 2 == 1, head_size)) for part in (value + reach, reach))
        attended.append((middle + reach * share).astype(BF16))
    output = dot(jnp.concatenate(attended, axis=1), w_ref[...])
    out_ref[...] = (hidden_ref[...].astype(F32) + output).astype(BF16)


def fixed(array):
    return pl.BlockSpec(array.shape, lambda *_, rank=len(array.shape): (0,) * rank)


def by_row(array, low=0, lead=0):
    before, after = array.shape[:lead], array.shape[lead + 1 :]
    return pl.BlockSpec(
        (*before, None, *after), lambda i, *_: (0,) * len(before) + (low + i,) + (0,) * len(after)
    )


def within(array, start):
    rows, *rest = array.shape
    return pl.BlockSpec(
        (None, *rest), lambda i, *_: (jnp.clip(i - start, 0, rows - 1),) + (0,) * len(rest)
    )


class Order:
    def __init__(self):
        self.last = None
        self.after = []

    def __call__(self, kernel, prefetch, args, specs, outs, out_specs, scratch, flops, grid=(1,), alias=None):
        anywhere = pl.BlockSpec(memory_space=pl.ANY)
        token = jax.ShapeDtypeStruct((8, 128), F32)
        taken = self.after + ([] if self.last is None else [self.last])
        self.after = []
        skip, count = len(prefetch) + len(args), len(outs)

        def ordered(*refs):
            refs = refs[:skip] + refs[skip + len(taken) :]
            give = len(prefetch) + len(args) + count
            kernel(*refs[:give], *refs[give + 1 :])

        *results, self.last = call(
            ordered,
            prefetch,
            tuple(args) + tuple(taken),
            [*specs, *[anywhere] * len(taken)],
            [*outs, token],
            [*out_specs, anywhere],
            scratch,
            flops,
            grid,
            alias,
        )
        return results


def call(kernel, prefetch, args, specs, outs, out_specs, scratch, flops, grid=(1,), alias=None):
    moved = 2 * sum(math.prod(out.shape) * out.dtype.itemsize for out in outs)
    return pl.pallas_call(
        kernel,
        grid_spec=pltpu.PrefetchScalarGridSpec(
            num_scalar_prefetch=len(prefetch),
            grid=grid,
            in_specs=specs,
            out_specs=out_specs,
            scratch_shapes=scratch,
        ),
        out_shape=outs,
        input_output_aliases=alias or {},
        compiler_params=pltpu.CompilerParams(vmem_limit_bytes=VMEM_BYTES),
        cost_estimate=pl.CostEstimate(flops=1024, bytes_accessed=1024, transcendentals=0),
    )(*prefetch, *args)


VMEM_BYTES = 36 * 1024 * 1024


def held(array):
    return pltpu.with_memory_space_constraint(array, pltpu.HBM)


def swap_blocks(parts, count):
    if len(parts) == 1:
        return [lax.all_to_all(parts[0], "lon", 0, 0, tiled=True)]
    moved = [
        lax.ppermute(part, "lon", [(i, (i + shift) % count) for i in range(count)])
        for shift, part in enumerate(parts)
        if shift
    ]
    return [parts[0], *moved]


def exchanges(axis):
    size = lax.axis_size(axis)
    step = 1
    while step < size:
        yield axis, [(i, i ^ step) for i in range(size)]
        step *= 2


def fused_body(
    fields,
    band_rows,
    earliest_past_snapshot,
    lat_table,
    norm_gain,
    w_in1,
    b_in1,
    w_out2,
    b_out2,
    w_query,
    w_keyval,
    w_output,
    score_scale,
    spec_cot,
):
    _, _, lat_rows, window, width = fields.shape
    count = lax.axis_size("lon")
    length = window * count
    modes, local_width = spec_cot.shape[4:]
    _, blocks, block_size, _ = w_in1.shape
    head_size = width // score_scale.shape[0]
    keyval_width = w_keyval.shape[1]
    rank = basis_rank(window, length, modes)
    basis, basis_t, fold, unfold = window_tables(window, length, modes, rank)
    gain = norm_gain.reshape(1, width)

    run = Order()

    def struct(*shape, dtype=BF16):
        return jax.ShapeDtypeStruct(shape, dtype)

    def row_specs(start):
        return [
            pl.BlockSpec((None, None, None, window, width), lambda i, *_: (0, 0, start + i, 0, 0)),
            pl.BlockSpec((16, width), lambda i, band: (band[0, start + i] // 16, 0)),
        ]

    def part_outs(rows, at_once):
        if at_once:
            return [struct(count, rows, rank, local_width)]
        return [struct(rows, rank, local_width)] * count

    def compress(start, rows, at_once):
        outs = part_outs(rows, at_once)
        return run(
            functools.partial(compress_kernel, start),
            (band_rows,),
            tuple(held(a) for a in (fields, lat_table, gain, basis_t)),
            [*row_specs(start), fixed(gain), fixed(basis_t)],
            outs,
            [by_row(out, lead=len(out.shape) - 3) for out in outs],
            [pltpu.VMEM((window, width), BF16)],
            2 * rows * rank * window * width,
            grid=(rows,),
        )

    def mix(parts, low, rows):
        args = (fold, mix1, b_in1, mix2, b_out2)
        outs = [struct(rows, 2 * modes, local_width)] * 2
        return run(
            functools.partial(filter_kernel, len(parts)),
            (),
            (*parts, *args),
            [*[by_row(part, low, part.ndim - 3) for part in parts], *[fixed(a) for a in args]],
            outs,
            [by_row(out) for out in outs],
            [pltpu.VMEM((count * rank, local_width), BF16)],
            rows * (16 * modes * local_width * local_width + 4 * modes * local_width * rank * count),
            grid=(rows,),
        )

    def unmix(mixed, at_once):
        rows = mixed.shape[0]
        outs = part_outs(rows, at_once)
        return run(
            unfold_kernel,
            (),
            (mixed, unfold),
            [by_row(mixed), fixed(unfold)],
            outs,
            [by_row(out, lead=len(out.shape) - 3) for out in outs],
            [],
            rows * 4 * modes * local_width * rank * count,
            grid=(rows,),
        )

    def expand(start, parts, low, rows, split):
        args = (basis, w_keyval)
        pieces = 2 if split else 1
        outs = [struct(rows, window, width), *[struct(rows, window, keyval_width // pieces)] * pieces]
        return run(
            functools.partial(expand_kernel, start, len(parts), head_size),
            (band_rows,),
            (fields, held(lat_table), *parts, *args),
            [*row_specs(start), *[by_row(part, low, part.ndim - 3) for part in parts], *[fixed(a) for a in args]],
            outs,
            [by_row(out) for out in outs],
            [pltpu.VMEM((count, rank, local_width), BF16)],
            2 * rows * window * width * (rank + keyval_width),
            grid=(rows,),
        )

    def gradient(firsts):
        args = (*firsts, spec_cot.reshape(spec_cot.shape[2:]))
        packed = struct(blocks * block_size + 8, 2 * block_size, dtype=F32)
        return run(
            functools.partial(gradient_kernel, block_size),
            (),
            args,
            [fixed(a) for a in args],
            [packed],
            [fixed(packed)],
            [],
            8 * lat_rows * modes * local_width * local_width,
        )[0]

    def unpack(summed):
        outs = [struct(*w_out2.shape, dtype=F32), struct(*b_out2.shape, dtype=F32)]
        specs = [fixed(out) for out in outs]
        return run(unpack_kernel, (), (summed,), [fixed(summed)], outs, specs, [], 0)

    def project(hidden):
        return run(
            functools.partial(query_kernel, head_size),
            (),
            (hidden, w_query),
            [by_row(hidden), fixed(w_query)],
            [struct(*hidden.shape)],
            [by_row(hidden)],
            [],
            2 * hidden.size * width,
            grid=(hidden.shape[0],),
        )[0]

    def attention(start, rows, filled):
        args, specs, groups = [], [], []
        for low in sorted(set(cells) & set(range(start, start + rows))):
            query, own, other, hidden = cells[low]
            mine = (query, *own, *other, hidden)
            groups.append((low - start, low - start + query.shape[0], len(own)))
            args += mine
            specs += [within(a, low - start) for a in mine]
        args.append(w_output)
        specs.append(fixed(w_output))
        alias = None
        if filled is not None:
            alias = {2 + len(args): 0}
            args.append(filled)
            specs.append(pl.BlockSpec(memory_space=pl.ANY))
        return run(
            functools.partial(attend_kernel, head_size, groups),
            (earliest_past_snapshot, score_scale),
            args,
            specs,
            [struct(*fields.shape)],
            [pl.BlockSpec((None, None, None, window, width), lambda i, *_: (0, 0, start + i, 0, 0))],
            [],
            4 * rows * window * width * width,
            grid=(rows,),
            alias=alias,
        )[0]

    predicted = None
    received, mixes, firsts, homeward, cells = {}, {}, [], {}, {}
    for step, start, rows, at_once in PLAN:
        if step == "compress":
            parts = swap_blocks(compress(start, rows, at_once), count)
            received.update({start + low: (parts, low) for low in range(rows)})
        elif step == "blocks":
            weights = [w_in1, w_out2]
            mix_shape = struct(2 * local_width, 2 * local_width)
            mix1, mix2 = run(
                blocks_kernel, (), weights, [fixed(a) for a in weights], [mix_shape] * 2, [fixed(mix_shape)] * 2, [], 0
            )
        elif step == "mix":
            first, mixes[start] = mix(*received[start], rows)
            firsts.append(first)
        elif step == "unmix":
            parts = swap_blocks(unmix(mixes[start], at_once), count)
            homeward.update({start + low: (parts, low) for low in range(rows)})
        elif step == "expand":
            hidden, *keyval = expand(start, *homeward[start], rows, at_once)
            earlier = [lax.ppermute(part, "frame", [(0, 1)]) for part in keyval]
            cells[start] = (keyval, earlier, hidden)
        elif step == "received":
            run.after.append(received[start][0][rows])
        elif step == "returned":
            run.after.append(homeward[start][0][rows])
        elif step == "query":
            cells[start] = (project(cells[start][-1]), *cells[start])
        elif step == "attend":
            predicted = attention(start, rows, predicted)
        elif step == "gradient":
            summed = gradient(firsts)
            rounds = [*exchanges("frame"), *exchanges("dp")]
            crossing = lax.ppermute(summed, *rounds.pop(0))
        elif step == "add":
            summed = summed + crossing
            if rounds:
                crossing = lax.ppermute(summed, *rounds.pop(0))
                run.after.append(summed)
        elif step == "sum":
            gradients = unpack(summed)
    return (predicted, *gradients)


PLAN = (
    ("compress", 0, 2, False),
    ("received", 0, 2, False),
    ("compress", 2, 2, False),
    ("blocks", 0, 0, False),
    ("mix", 0, 2, False),
    ("unmix", 0, 2, False),
    ("mix", 2, 2, False),
    ("gradient", 0, 0, False),
    ("returned", 0, 2, False),
    ("unmix", 2, 2, False),
    ("expand", 0, 2, True),
    ("query", 0, 2, False),
    ("expand", 2, 1, False),
    ("expand", 3, 1, False),
    ("add", 0, 0, False),
    ("query", 2, 1, False),
    ("query", 3, 1, False),
    ("add", 0, 0, False),
    ("attend", 0, 2, False),
    ("attend", 2, 1, False),
    ("add", 0, 0, False),
    ("sum", 0, 0, False),
    ("attend", 3, 1, False),
)


def transform_table(length, modes):
    longitude = jnp.arange(length, dtype=jnp.int32)
    zonal_wavenumber = jnp.arange(modes, dtype=jnp.int32)
    turns_mod = longitude[:, None] * zonal_wavenumber[None, :] % length
    angles = turns_mod.astype(jnp.float32) * (2.0 * math.pi / length)
    return jnp.concatenate([jnp.cos(angles), -jnp.sin(angles)], axis=1).astype(jnp.bfloat16)


def inverse_table(forward, modes):
    zonal_wavenumber = jnp.arange(modes, dtype=jnp.int32)
    factor = jnp.where(zonal_wavenumber == 0, 1.0, 2.0).astype(jnp.float32)
    factor = jnp.concatenate([factor, factor])
    return (forward.astype(jnp.float32) * factor[None, :]).astype(jnp.bfloat16)


def block_mix(left, weight):
    return jnp.einsum("rmgc,gce->rmge", left, weight, preferred_element_type=jnp.float32)


def filter_modes(spectrum, w_in1, b_in1, w_out2, b_out2):
    spectral_real = spectrum[:, 0]
    spec_im = spectrum[:, 1]
    first_re = jax.nn.relu(
        block_mix(spectral_real, w_in1[0]) - block_mix(spec_im, w_in1[1]) + b_in1[0]
    ).astype(jnp.bfloat16)
    first_im = jax.nn.relu(
        block_mix(spectral_real, w_in1[1]) + block_mix(spec_im, w_in1[0]) + b_in1[1]
    ).astype(jnp.bfloat16)
    second_re = (
        block_mix(first_re, w_out2[0]) - block_mix(first_im, w_out2[1]) + b_out2[0]
    ).astype(jnp.bfloat16)
    second_im = (
        block_mix(first_re, w_out2[1]) + block_mix(first_im, w_out2[0]) + b_out2[1]
    ).astype(jnp.bfloat16)
    return (first_re, first_im, jnp.concatenate([second_re, second_im], axis=1))


def head_norm(values_in):
    return values_in * lax.rsqrt(jnp.mean(values_in * values_in, axis=-1, keepdims=True) + 1e-06)


def attend(
    queries, keys_all, value_rows_full, query_frame, first_seen, score_scale, kv_heads, head_size
):
    site_count, query_frames, width = queries.shape
    key_frames = keys_all.shape[1]
    groups = width // head_size // kv_heads
    q_five = queries.reshape(site_count, query_frames, kv_heads, groups, head_size)
    k_four = keys_all.reshape(site_count, key_frames, kv_heads, head_size)
    v_four = value_rows_full.reshape(site_count, key_frames, kv_heads, head_size)
    scores = jnp.einsum("sqkgd,stkd->kgqts", q_five, k_four, preferred_element_type=jnp.float32)
    scores = scores * (score_scale.reshape(kv_heads, groups, 1, 1, 1) / math.sqrt(head_size))
    key_ids = jnp.arange(key_frames, dtype=jnp.int32)[None, :, None]
    query_ids = query_frame[:, None, None]
    seen = (key_ids <= query_ids) & (
        (key_ids >= first_seen[None, None, :]) | (key_ids == query_ids)
    )
    scores = jnp.where(seen[None, None], scores, -1e30)
    top_score = jnp.max(scores, axis=-2, keepdims=True)
    weights = jnp.exp(scores - top_score)
    probs = (weights / jnp.sum(weights, axis=-2, keepdims=True)).astype(jnp.bfloat16)
    attended = jnp.einsum("kgqts,stkd->sqkgd", probs, v_four, preferred_element_type=jnp.float32)
    return attended.astype(jnp.bfloat16).reshape(site_count, query_frames, width)


def plain_body(
    fields,
    band_rows,
    earliest_past_snapshot,
    lat_table,
    norm_gain,
    w_in1,
    b_in1,
    w_out2,
    b_out2,
    w_query,
    w_keyval,
    w_output,
    score_scale,
    spec_cot,
):
    samples, _, lat_rows, lon_local, width = fields.shape
    grid_rows = samples * lat_rows
    length = lon_local * lax.axis_size("lon")
    modes = spec_cot.shape[4]
    local_width = spec_cot.shape[5]
    blocks = w_in1.shape[1]
    block_size = w_in1.shape[2]
    forward = transform_table(length, modes)
    backward = inverse_table(forward, modes)
    scale_t = 1.0 / math.sqrt(length)
    lat_count = lat_table.shape[0]
    onehot = (
        band_rows[:, :, None] == jnp.arange(lat_count, dtype=jnp.int32)[None, None, :]
    ).astype(jnp.bfloat16)
    embedding = jnp.dot(
        onehot.reshape(grid_rows, lat_count), lat_table, preferred_element_type=jnp.float32
    )
    inputs = fields[:, 0].astype(jnp.float32) + embedding.reshape(samples, lat_rows, 1, width)
    center = jnp.mean(inputs, axis=-1, keepdims=True)
    spread = jnp.mean(jnp.square(inputs - center), axis=-1, keepdims=True)
    normed = ((inputs - center) * lax.rsqrt(spread + 1e-05) * norm_gain).astype(jnp.bfloat16)
    gathered = lax.all_to_all(
        normed.reshape(grid_rows, lon_local, width), "lon", split_axis=2, concat_axis=1, tiled=True
    )
    spectrum = (
        jnp.einsum("rnc,nk->rkc", gathered, forward, preferred_element_type=jnp.float32) * scale_t
    ).astype(jnp.bfloat16)
    spectrum = spectrum.reshape(grid_rows, 2, modes, blocks, block_size)
    first_re, first_im, mixed = filter_modes(
        spectrum,
        w_in1,
        b_in1.reshape(2, blocks, block_size),
        w_out2,
        b_out2.reshape(2, blocks, block_size),
    )
    mixed = mixed.reshape(grid_rows, 2 * modes, local_width)
    grid_part = (
        jnp.einsum("rkc,nk->rnc", mixed, backward, preferred_element_type=jnp.float32) * scale_t
    ).astype(jnp.bfloat16)
    returned = lax.all_to_all(grid_part, "lon", split_axis=1, concat_axis=2, tiled=True)
    hidden = (
        inputs + returned.reshape(samples, lat_rows, lon_local, width).astype(jnp.float32)
    ).astype(jnp.bfloat16)
    cotangent = spec_cot.reshape(grid_rows, 2, modes, blocks, block_size)
    grad_re = jnp.einsum(
        "rmgc,rmge->gce", first_re, cotangent[:, 0], preferred_element_type=jnp.float32
    )
    grad_re = grad_re + jnp.einsum(
        "rmgc,rmge->gce", first_im, cotangent[:, 1], preferred_element_type=jnp.float32
    )
    grad_im = jnp.einsum(
        "rmgc,rmge->gce", first_re, cotangent[:, 1], preferred_element_type=jnp.float32
    )
    grad_im = grad_im - jnp.einsum(
        "rmgc,rmge->gce", first_im, cotangent[:, 0], preferred_element_type=jnp.float32
    )
    bias_terms = jnp.sum(cotangent.astype(jnp.float32), axis=(0, 2)).reshape(2, local_width)
    mask_coefficient2_derivative, mask_offset2_derivative = lax.psum(
        (jnp.stack([grad_re, grad_im]), bias_terms), ("dp", "frame")
    )
    site_count = grid_rows * lon_local
    tokens = hidden.reshape(site_count, width)
    head_count = score_scale.shape[0]
    head_size = width // head_count
    kv_width = w_keyval.shape[1] // 2
    kv_heads = kv_width // head_size
    query = jnp.dot(tokens, w_query, preferred_element_type=jnp.float32).reshape(
        site_count, head_count, head_size
    )
    qnorm = head_norm(query).astype(jnp.bfloat16).reshape(site_count, 1, width)
    keyval = jnp.dot(tokens, w_keyval, preferred_element_type=jnp.float32)
    knorm = (
        head_norm(keyval[:, :kv_width].reshape(site_count, kv_heads, head_size))
        .astype(jnp.bfloat16)
        .reshape(site_count, 1, kv_width)
    )
    values = keyval[:, kv_width:].astype(jnp.bfloat16).reshape(site_count, 1, kv_width)
    first_seen = jnp.broadcast_to(
        earliest_past_snapshot[:, None], (samples, lat_rows * lon_local)
    ).reshape(site_count)
    own_frame = lax.axis_index("frame")
    keys_all, value_rows_full = (
        lax.all_gather(knorm, "frame", axis=1, tiled=True),
        lax.all_gather(values, "frame", axis=1, tiled=True),
    )
    query_frame = jnp.reshape(own_frame, (1,))
    attended = attend(
        qnorm, keys_all, value_rows_full, query_frame, first_seen, score_scale, kv_heads, head_size
    )
    output = jnp.dot(
        attended.reshape(site_count, width), w_output, preferred_element_type=jnp.float32
    )
    predicted_output_fields = (
        (tokens.astype(jnp.float32) + output)
        .astype(jnp.bfloat16)
        .reshape(samples, 1, lat_rows, lon_local, width)
    )
    return (predicted_output_fields, mask_coefficient2_derivative, mask_offset2_derivative)


def basis_rank(window, length, modes):
    return -(-(window * (2 * modes - 1) // length + 24) // 16) * 16


def body(fields, *rest):
    width, local_width = fields.shape[-1], rest[-1].shape[-1]
    head_size = width // rest[-2].shape[0]
    fits = (
        fields.shape[0] == 1
        and lax.axis_size("frame") == 2
        and local_width % LANES == 0
        and fields.shape[2] == sum(rows for step, _, rows, _ in PLAN if step == "compress")
        and 2 * head_size == 128
        and 2 * rest[4].shape[2] == 128
        and rest[-4].shape[1] * 2 == width
    )
    sizes = [lax.axis_size(axis) for axis in ("frame", "dp")]
    fits = fits and all(size & (size - 1) == 0 for size in sizes)
    return (fused_body if fits else plain_body)(fields, *rest)


def solution(mesh):
    placed = (
        P("dp", "frame", None, "lon", None),
        P("dp", None),
        P("dp"),
        P(),
        P(),
        P(None, "lon", None, None),
        P(None, "lon"),
        P(None, "lon", None, None),
        P(None, "lon"),
        P(),
        P(),
        P(),
        P(),
        P("dp", "frame", None, None, None, "lon"),
    )
    return jax.shard_map(
        body,
        mesh=mesh,
        in_specs=placed,
        out_specs=(P("dp", "frame", None, "lon", None), P(None, "lon", None, None), P(None, "lon")),
        check_vma=False,
    )
```

```python
import functools
import math

import jax
import jax.numpy as jnp
import ml_dtypes
import numpy as np
from jax import lax
from jax.experimental import pallas as pl
from jax.experimental.pallas import tpu as pltpu
from jax.sharding import PartitionSpec as P


def window_basis(window, length, modes, rank):
    band = 2 * modes - 1
    site = np.arange(window)
    step = np.arange(1, window)
    diagonal = -np.cos(np.pi * (window - 1 - 2 * site) / length) * np.cos(np.pi * band / length)
    beside = np.sin(np.pi * step / length) * np.sin(np.pi * (window - step) / length)
    _, vectors = np.linalg.eigh(np.diag(diagonal) + np.diag(beside, 1) + np.diag(beside, -1))
    basis = vectors[:, ::-1][:, :rank]
    lead = np.argmax(np.abs(basis) > 1e-3, axis=0)
    return basis * np.sign(basis[lead, np.arange(rank)])[None, :]


def window_tables(window, length, modes, rank):
    basis = window_basis(window, length, modes, rank)
    turns = np.arange(length)[:, None] * np.arange(modes)[None, :] % length
    angles = 2.0 * np.pi * turns / length
    table = np.concatenate([np.cos(angles), -np.sin(angles)], axis=1)
    factor = np.where(np.arange(2 * modes) % modes == 0, 1.0, 2.0)
    parts = table.reshape(length // window, window, 2 * modes)
    spread = np.einsum("pnj,nr->prj", parts, basis) / math.sqrt(length)
    fold = np.transpose(spread, (2, 0, 1)).reshape(2 * modes, -1)
    unfold = spread * factor

    def small(array):
        return (np.round(array * 2.0**16) / 2.0**16).astype(ml_dtypes.bfloat16)

    return small(basis), small(basis.T), small(fold), small(unfold)


LANES = 256
F32 = jnp.float32
BF16 = jnp.bfloat16


def dot(left, right):
    return jnp.dot(left, right, preferred_element_type=F32)


def row_tiles(rows, size):
    return [(low, min(low + size, rows)) for low in range(0, rows, size)]


def latitude_row(band, block):
    rows = block.astype(F32)
    place = lax.broadcasted_iota(jnp.int32, rows.shape, 0)
    return jnp.sum(jnp.where(place == band % rows.shape[0], rows, 0.0), axis=0, keepdims=True)


def compress_kernel(start, band_ref, x_ref, lat_ref, gain_ref, basis_ref, *rest):
    *outs, normed_ref = rest
    rows, width = x_ref.shape
    embed = latitude_row(band_ref[0, start + pl.program_id(0)], lat_ref[...])
    gain = gain_ref[...]
    for low, high in row_tiles(rows, 16):
        inputs = x_ref[low:high].astype(F32) + embed
        center = jnp.sum(inputs, axis=-1, keepdims=True) * (1.0 / width)
        inputs = inputs - center
        spread = jnp.sum(inputs * inputs, axis=-1, keepdims=True) * (1.0 / width)
        normed_ref[low:high] = (inputs * lax.rsqrt(spread + 1e-05) * gain).astype(BF16)
    size = width // lax.axis_size("lon")
    for block, store in outgoing(outs):
        columns = pl.ds(pl.multiple_of(block * size, size), size)
        store(dot(basis_ref[...], normed_ref[:, columns]).astype(BF16))


def outgoing(outs):
    count = lax.axis_size("lon")
    if len(outs) == 1:
        return [(block, functools.partial(outs[0].__setitem__, block)) for block in range(count)]
    me = lax.axis_index("lon")
    return [
        (lax.rem(me + shift, count), functools.partial(out.__setitem__, ...))
        for shift, out in enumerate(outs)
    ]


def incoming(parts):
    count = lax.axis_size("lon")
    if len(parts) == 1:
        return [(owner, parts[0][owner]) for owner in range(count)]
    me = lax.axis_index("lon")
    return [(lax.rem(me + count - shift, count), part[...]) for shift, part in enumerate(parts)]


def blocks_kernel(w1_ref, w2_ref, mix1_ref, mix2_ref):
    _, blocks, size, _ = w1_ref.shape
    width = blocks * size
    for weight, mix in ((w1_ref, mix1_ref), (w2_ref, mix2_ref)):
        mix[...] = jnp.zeros(mix.shape, mix.dtype)
        for block in range(blocks):
            low = block * size
            here, there = slice(low, low + size), slice(width + low, width + low + size)
            real, imag = weight[0, block], weight[1, block]
            mix[here, here] = real
            mix[here, there] = imag
            mix[there, here] = -imag
            mix[there, there] = real


def filter_kernel(taken, *refs):
    parts, refs = refs[:taken], refs[taken:]
    fold_ref, w1_ref, b1_ref, w2_ref, b2_ref, first_ref, mixed_ref, whole_ref = refs
    rank, width = parts[0].shape[-2:]
    modes = first_ref.shape[0] // 2
    for owner, part in incoming(parts):
        whole_ref[pl.ds(pl.multiple_of(owner * rank, 16), rank)] = part
    spectrum = dot(fold_ref[...], whole_ref[...]).astype(BF16)
    spectrum = jnp.concatenate([spectrum[:modes], spectrum[modes:]], axis=1)
    first = jnp.maximum(dot(spectrum, w1_ref[...]) + both_parts(b1_ref), 0.0).astype(BF16)
    first_ref[:modes] = first[:, :width]
    first_ref[modes:] = first[:, width:]
    mixed = (dot(first, w2_ref[...]) + both_parts(b2_ref)).astype(BF16)
    mixed_ref[:modes] = mixed[:, :width]
    mixed_ref[modes:] = mixed[:, width:]


def both_parts(ref):
    return jnp.concatenate([ref[0:1], ref[1:2]], axis=1)


def unfold_kernel(mixed_ref, unfold_ref, *outs):
    sums = [(store, dot(unfold_ref[block], mixed_ref[...])) for block, store in outgoing(outs)]
    for store, part in sums:
        store(part.astype(BF16))


def gradient_kernel(size, *refs):
    *firsts, cot_ref, packed_ref = refs
    modes, width = cot_ref.shape[2:]
    contract = (((0,), (0,)), ((), ()))
    total, bias, row = 0.0, 0.0, 0
    for first_ref in firsts:
        for piece in range(first_ref.shape[0]):
            real, imag = cot_ref[row, 0], cot_ref[row, 1]
            both = jnp.concatenate([real, imag], axis=1)
            turned = jnp.concatenate([imag, -real], axis=1)
            first_re, first_im = first_ref[piece, :modes], first_ref[piece, modes:]
            total += lax.dot_general(first_re, both, contract, preferred_element_type=F32)
            total += lax.dot_general(first_im, turned, contract, preferred_element_type=F32)
            bias += jnp.sum(both.astype(F32), axis=0, keepdims=True)
            row += 1
    pair = 2 * size
    lane = lax.broadcasted_iota(jnp.int32, (size, pair), 1)
    out = 0
    for low in range(0, 2 * width, pair):
        left = low % width
        even = total[left : left + size, low : low + pair]
        odd = total[left + size : left + pair, low : low + pair]
        packed_ref[out : out + size] = jnp.where(lane < size, even, odd)
        out += size
    packed_ref[out:] = jnp.zeros((packed_ref.shape[0] - out, pair), F32)
    for place, low in enumerate(range(0, 2 * width, pair)):
        packed_ref[out + place : out + place + 1] = bias[:, low : low + pair]


def unpack_kernel(summed_ref, weight_ref, bias_ref):
    _, blocks, size, _ = weight_ref.shape
    total = summed_ref[...]
    out = 0
    for part in range(2):
        for block in range(0, blocks, 2):
            weight_ref[part, block] = total[out : out + size, :size]
            weight_ref[part, block + 1] = total[out : out + size, size:]
            out += size
    for part in range(2):
        for low in range(0, bias_ref.shape[1], 2 * size):
            bias_ref[part : part + 1, low : low + 2 * size] = total[out : out + 1]
            out += 1


def head_scale(values, ones):
    squares = (values * values).astype(BF16)
    return values * lax.rsqrt(dot(squares, ones) + 1e-06)


def head_ones(head_size, value):
    row = lax.broadcasted_iota(jnp.int32, (LANES, LANES), 0) // head_size
    column = lax.broadcasted_iota(jnp.int32, (LANES, LANES), 1) // head_size
    return jnp.where(row == column, value, 0.0).astype(BF16)


def expand_kernel(start, taken, head_size, band_ref, x_ref, lat_ref, *refs):
    parts, refs = refs[:taken], refs[taken:]
    basis_ref, w_keyval_ref, hidden_ref, *keyval_refs, whole_ref = refs
    count, _, width = whole_ref.shape
    for owner, part in incoming(parts):
        whole_ref[owner] = part
    embed = latitude_row(band_ref[0, start + pl.program_id(0)], lat_ref[...])
    grids = [dot(basis_ref[...], whole_ref[block]).astype(BF16) for block in range(count)]
    inputs = x_ref[...].astype(F32) + embed
    hidden = (inputs + jnp.concatenate(grids, axis=1).astype(F32)).astype(BF16)
    hidden_ref[...] = hidden
    keyval = dot(hidden, w_keyval_ref[...])
    ones = head_ones(head_size, 1.0 / head_size)
    half = keyval.shape[1] // 2
    keys = [head_scale(keyval[:, low : low + LANES], ones) for low in range(0, half, LANES)]
    keyval = jnp.concatenate([*keys, keyval[:, half:]], axis=1).astype(BF16)
    low = 0
    for out in keyval_refs:
        out[...] = keyval[:, low : low + out.shape[1]]
        low += out.shape[1]


def query_kernel(head_size, hidden_ref, w_query_ref, query_ref):
    ones = head_ones(head_size, 1.0 / head_size)
    tiles = [slice(low, low + LANES) for low in range(0, query_ref.shape[1], LANES)]
    queries = [dot(hidden_ref[...], w_query_ref[:, columns]) for columns in tiles]
    means = [dot((query * query).astype(BF16), ones) for query in queries]
    for columns, query, mean in zip(tiles, queries, means):
        query_ref[:, columns] = (query * lax.rsqrt(mean + 1e-06)).astype(BF16)


def repeat_head(pair, upper, head_size):
    lane = lax.broadcasted_iota(jnp.int32, pair.shape, 1)
    rolled = pltpu.roll(pair, head_size, 1)
    return jnp.where((lane < head_size) != upper, pair, rolled)


def twice(part):
    return jnp.concatenate([part, part], axis=1)


def attend_kernel(head_size, groups, past_ref, scale_ref, *refs):
    out_ref = refs[-1]
    w_ref = refs[sum(2 + 2 * taken for _, _, taken in groups)]
    for first, last, taken in groups:
        size = 2 + 2 * taken
        mine, refs = refs[:size], refs[size:]
        row = pl.program_id(0)

        @pl.when(jnp.logical_and(row >= first, row < last))
        def _(mine=mine, taken=taken):
            attend_row(head_size, taken, past_ref, scale_ref, *mine, w_ref, out_ref)


def attend_row(head_size, taken, past_ref, scale_ref, query_ref, *refs):
    own_refs, other_refs, refs = refs[:taken], refs[taken : 2 * taken], refs[2 * taken :]
    hidden_ref, w_ref, out_ref = refs
    half = sum(ref.shape[1] for ref in own_refs) // 2
    pair_width = 2 * head_size
    group = LANES // head_size
    ones = head_ones(head_size, 1.0)
    ones = jnp.concatenate([ones, ones], axis=0)
    lane_head = lax.broadcasted_iota(jnp.int32, (1, LANES), 1) // head_size
    seen = jnp.logical_and(lax.axis_index("frame") == 1, past_ref[0] <= 0)

    def load(refs, low):
        size = refs[0].shape[1]
        return refs[low // size][:, low % size : low % size + pair_width].astype(F32)

    leads, attended = [], []
    heads = range(half // head_size)
    for head in heads:
        pair = head // 2 * pair_width
        step = repeat_head(load(other_refs, pair) - load(own_refs, pair), head % 2 == 1, head_size)
        product = query_ref[:, head * LANES : head * LANES + LANES].astype(F32) * twice(step)
        high = product.astype(BF16)
        low = (product - high.astype(F32)).astype(BF16)
        leads.append(dot(jnp.concatenate([high, low], axis=1), ones))
    for head in heads:
        pair = half + head // 2 * pair_width
        value = load(own_refs, pair)
        reach = jnp.where(seen, 0.5 * (load(other_refs, pair) - value), 0.0)
        scale = jnp.zeros((1, LANES), F32)
        for place in range(group):
            scale = jnp.where(lane_head == place, scale_ref[head * group + place], scale)
        share = jnp.tanh(leads[head] * (scale * (0.5 / math.sqrt(head_size))))
        middle, reach = (twice(repeat_head(part, head % 2 == 1, head_size)) for part in (value + reach, reach))
        attended.append((middle + reach * share).astype(BF16))
    output = dot(jnp.concatenate(attended, axis=1), w_ref[...])
    out_ref[...] = (hidden_ref[...].astype(F32) + output).astype(BF16)


def fixed(array):
    return pl.BlockSpec(array.shape, lambda *_, rank=len(array.shape): (0,) * rank)


def by_row(array, low=0, lead=0):
    before, after = array.shape[:lead], array.shape[lead + 1 :]
    return pl.BlockSpec(
        (*before, None, *after), lambda i, *_: (0,) * len(before) + (low + i,) + (0,) * len(after)
    )


def within(array, start):
    rows, *rest = array.shape
    return pl.BlockSpec(
        (None, *rest), lambda i, *_: (jnp.clip(i - start, 0, rows - 1),) + (0,) * len(rest)
    )


class Order:
    def __init__(self):
        self.last = None
        self.after = []

    def __call__(self, kernel, prefetch, args, specs, outs, out_specs, scratch, flops, grid=(1,), alias=None):
        anywhere = pl.BlockSpec(memory_space=pl.ANY)
        token = jax.ShapeDtypeStruct((8, 128), F32)
        taken = self.after + ([] if self.last is None else [self.last])
        self.after = []
        skip, count = len(prefetch) + len(args), len(outs)

        def ordered(*refs):
            refs = refs[:skip] + refs[skip + len(taken) :]
            give = len(prefetch) + len(args) + count
            kernel(*refs[:give], *refs[give + 1 :])

        *results, self.last = call(
            ordered,
            prefetch,
            tuple(args) + tuple(taken),
            [*specs, *[anywhere] * len(taken)],
            [*outs, token],
            [*out_specs, anywhere],
            scratch,
            flops,
            grid,
            alias,
        )
        return results


def call(kernel, prefetch, args, specs, outs, out_specs, scratch, flops, grid=(1,), alias=None):
    moved = 2 * sum(math.prod(out.shape) * out.dtype.itemsize for out in outs)
    return pl.pallas_call(
        kernel,
        grid_spec=pltpu.PrefetchScalarGridSpec(
            num_scalar_prefetch=len(prefetch),
            grid=grid,
            in_specs=specs,
            out_specs=out_specs,
            scratch_shapes=scratch,
        ),
        out_shape=outs,
        input_output_aliases=alias or {},
        compiler_params=pltpu.CompilerParams(vmem_limit_bytes=VMEM_BYTES),
        cost_estimate=pl.CostEstimate(flops=1024, bytes_accessed=1024, transcendentals=0),
    )(*prefetch, *args)


VMEM_BYTES = 36 * 1024 * 1024


def held(array):
    return pltpu.with_memory_space_constraint(array, pltpu.HBM)


def swap_blocks(parts, count):
    if len(parts) == 1:
        return [lax.all_to_all(parts[0], "lon", 0, 0, tiled=True)]
    moved = [
        lax.ppermute(part, "lon", [(i, (i + shift) % count) for i in range(count)])
        for shift, part in enumerate(parts)
        if shift
    ]
    return [parts[0], *moved]


def exchanges(axis):
    size = lax.axis_size(axis)
    step = 1
    while step < size:
        yield axis, [(i, i ^ step) for i in range(size)]
        step *= 2


def fused_body(
    fields,
    band_rows,
    earliest_past_snapshot,
    lat_table,
    norm_gain,
    w_in1,
    b_in1,
    w_out2,
    b_out2,
    w_query,
    w_keyval,
    w_output,
    score_scale,
    spec_cot,
):
    _, _, lat_rows, window, width = fields.shape
    count = lax.axis_size("lon")
    length = window * count
    modes, local_width = spec_cot.shape[4:]
    _, blocks, block_size, _ = w_in1.shape
    head_size = width // score_scale.shape[0]
    keyval_width = w_keyval.shape[1]
    rank = basis_rank(window, length, modes)
    basis, basis_t, fold, unfold = window_tables(window, length, modes, rank)
    gain = norm_gain.reshape(1, width)

    run = Order()

    def struct(*shape, dtype=BF16):
        return jax.ShapeDtypeStruct(shape, dtype)

    def row_specs(start):
        return [
            pl.BlockSpec((None, None, None, window, width), lambda i, *_: (0, 0, start + i, 0, 0)),
            pl.BlockSpec((16, width), lambda i, band: (band[0, start + i] // 16, 0)),
        ]

    def part_outs(rows, at_once):
        if at_once:
            return [struct(count, rows, rank, local_width)]
        return [struct(rows, rank, local_width)] * count

    def compress(start, rows, at_once):
        outs = part_outs(rows, at_once)
        return run(
            functools.partial(compress_kernel, start),
            (band_rows,),
            tuple(held(a) for a in (fields, lat_table, gain, basis_t)),
            [*row_specs(start), fixed(gain), fixed(basis_t)],
            outs,
            [by_row(out, lead=len(out.shape) - 3) for out in outs],
            [pltpu.VMEM((window, width), BF16)],
            2 * rows * rank * window * width,
            grid=(rows,),
        )

    def mix(parts, low, rows):
        args = (fold, mix1, b_in1, mix2, b_out2)
        outs = [struct(rows, 2 * modes, local_width)] * 2
        return run(
            functools.partial(filter_kernel, len(parts)),
            (),
            (*parts, *args),
            [*[by_row(part, low, part.ndim - 3) for part in parts], *[fixed(a) for a in args]],
            outs,
            [by_row(out) for out in outs],
            [pltpu.VMEM((count * rank, local_width), BF16)],
            rows * (16 * modes * local_width * local_width + 4 * modes * local_width * rank * count),
            grid=(rows,),
        )

    def unmix(mixed, at_once):
        rows = mixed.shape[0]
        outs = part_outs(rows, at_once)
        return run(
            unfold_kernel,
            (),
            (mixed, unfold),
            [by_row(mixed), fixed(unfold)],
            outs,
            [by_row(out, lead=len(out.shape) - 3) for out in outs],
            [],
            rows * 4 * modes * local_width * rank * count,
            grid=(rows,),
        )

    def expand(start, parts, low, rows, split):
        args = (basis, w_keyval)
        pieces = 2 if split else 1
        outs = [struct(rows, window, width), *[struct(rows, window, keyval_width // pieces)] * pieces]
        return run(
            functools.partial(expand_kernel, start, len(parts), head_size),
            (band_rows,),
            (fields, held(lat_table), *parts, *args),
            [*row_specs(start), *[by_row(part, low, part.ndim - 3) for part in parts], *[fixed(a) for a in args]],
            outs,
            [by_row(out) for out in outs],
            [pltpu.VMEM((count, rank, local_width), BF16)],
            2 * rows * window * width * (rank + keyval_width),
            grid=(rows,),
        )

    def gradient(firsts):
        args = (*firsts, spec_cot.reshape(spec_cot.shape[2:]))
        packed = struct(blocks * block_size + 8, 2 * block_size, dtype=F32)
        return run(
            functools.partial(gradient_kernel, block_size),
            (),
            args,
            [fixed(a) for a in args],
            [packed],
            [fixed(packed)],
            [],
            8 * lat_rows * modes * local_width * local_width,
        )[0]

    def unpack(summed):
        outs = [struct(*w_out2.shape, dtype=F32), struct(*b_out2.shape, dtype=F32)]
        specs = [fixed(out) for out in outs]
        return run(unpack_kernel, (), (summed,), [fixed(summed)], outs, specs, [], 0)

    def project(hidden):
        return run(
            functools.partial(query_kernel, head_size),
            (),
            (hidden, w_query),
            [by_row(hidden), fixed(w_query)],
            [struct(*hidden.shape)],
            [by_row(hidden)],
            [],
            2 * hidden.size * width,
            grid=(hidden.shape[0],),
        )[0]

    def attention(start, rows, filled):
        args, specs, groups = [], [], []
        for low in sorted(set(cells) & set(range(start, start + rows))):
            query, own, other, hidden = cells[low]
            mine = (query, *own, *other, hidden)
            groups.append((low - start, low - start + query.shape[0], len(own)))
            args += mine
            specs += [within(a, low - start) for a in mine]
        args.append(w_output)
        specs.append(fixed(w_output))
        alias = None
        if filled is not None:
            alias = {2 + len(args): 0}
            args.append(filled)
            specs.append(pl.BlockSpec(memory_space=pl.ANY))
        return run(
            functools.partial(attend_kernel, head_size, groups),
            (earliest_past_snapshot, score_scale),
            args,
            specs,
            [struct(*fields.shape)],
            [pl.BlockSpec((None, None, None, window, width), lambda i, *_: (0, 0, start + i, 0, 0))],
            [],
            4 * rows * window * width * width,
            grid=(rows,),
            alias=alias,
        )[0]

    predicted = None
    received, mixes, firsts, homeward, cells = {}, {}, [], {}, {}
    for step, start, rows, at_once in PLAN:
        if step == "compress":
            parts = swap_blocks(compress(start, rows, at_once), count)
            received.update({start + low: (parts, low) for low in range(rows)})
        elif step == "blocks":
            weights = [w_in1, w_out2]
            mix_shape = struct(2 * local_width, 2 * local_width)
            mix1, mix2 = run(
                blocks_kernel, (), weights, [fixed(a) for a in weights], [mix_shape] * 2, [fixed(mix_shape)] * 2, [], 0
            )
        elif step == "mix":
            first, mixes[start] = mix(*received[start], rows)
            firsts.append(first)
        elif step == "unmix":
            parts = swap_blocks(unmix(mixes[start], at_once), count)
            homeward.update({start + low: (parts, low) for low in range(rows)})
        elif step == "expand":
            hidden, *keyval = expand(start, *homeward[start], rows, at_once)
            earlier = [lax.ppermute(part, "frame", [(0, 1)]) for part in keyval]
            cells[start] = (keyval, earlier, hidden)
        elif step == "received":
            run.after.append(received[start][0][rows])
        elif step == "returned":
            run.after.append(homeward[start][0][rows])
        elif step == "query":
            cells[start] = (project(cells[start][-1]), *cells[start])
        elif step == "attend":
            predicted = attention(start, rows, predicted)
        elif step == "gradient":
            summed = gradient(firsts)
            rounds = [*exchanges("frame"), *exchanges("dp")]
            crossing = lax.ppermute(summed, *rounds.pop(0))
        elif step == "add":
            summed = summed + crossing
            if rounds:
                crossing = lax.ppermute(summed, *rounds.pop(0))
                run.after.append(summed)
        elif step == "sum":
            gradients = unpack(summed)
    return (predicted, *gradients)


PLAN = (
    ("compress", 0, 2, False),
    ("received", 0, 1, False),
    ("compress", 2, 2, False),
    ("blocks", 0, 0, False),
    ("mix", 0, 2, False),
    ("unmix", 0, 2, False),
    ("mix", 2, 2, False),
    ("gradient", 0, 0, False),
    ("returned", 0, 2, False),
    ("unmix", 2, 2, False),
    ("expand", 0, 2, True),
    ("query", 0, 2, False),
    ("expand", 2, 1, False),
    ("expand", 3, 1, False),
    ("query", 2, 1, False),
    ("query", 3, 1, False),
    ("add", 0, 0, False),
    ("attend", 0, 2, False),
    ("add", 0, 0, False),
    ("attend", 2, 1, False),
    ("add", 0, 0, False),
    ("sum", 0, 0, False),
    ("attend", 3, 1, False),
)


def transform_table(length, modes):
    longitude = jnp.arange(length, dtype=jnp.int32)
    zonal_wavenumber = jnp.arange(modes, dtype=jnp.int32)
    turns_mod = longitude[:, None] * zonal_wavenumber[None, :] % length
    angles = turns_mod.astype(jnp.float32) * (2.0 * math.pi / length)
    return jnp.concatenate([jnp.cos(angles), -jnp.sin(angles)], axis=1).astype(jnp.bfloat16)


def inverse_table(forward, modes):
    zonal_wavenumber = jnp.arange(modes, dtype=jnp.int32)
    factor = jnp.where(zonal_wavenumber == 0, 1.0, 2.0).astype(jnp.float32)
    factor = jnp.concatenate([factor, factor])
    return (forward.astype(jnp.float32) * factor[None, :]).astype(jnp.bfloat16)


def block_mix(left, weight):
    return jnp.einsum("rmgc,gce->rmge", left, weight, preferred_element_type=jnp.float32)


def filter_modes(spectrum, w_in1, b_in1, w_out2, b_out2):
    spectral_real = spectrum[:, 0]
    spec_im = spectrum[:, 1]
    first_re = jax.nn.relu(
        block_mix(spectral_real, w_in1[0]) - block_mix(spec_im, w_in1[1]) + b_in1[0]
    ).astype(jnp.bfloat16)
    first_im = jax.nn.relu(
        block_mix(spectral_real, w_in1[1]) + block_mix(spec_im, w_in1[0]) + b_in1[1]
    ).astype(jnp.bfloat16)
    second_re = (
        block_mix(first_re, w_out2[0]) - block_mix(first_im, w_out2[1]) + b_out2[0]
    ).astype(jnp.bfloat16)
    second_im = (
        block_mix(first_re, w_out2[1]) + block_mix(first_im, w_out2[0]) + b_out2[1]
    ).astype(jnp.bfloat16)
    return (first_re, first_im, jnp.concatenate([second_re, second_im], axis=1))


def head_norm(values_in):
    return values_in * lax.rsqrt(jnp.mean(values_in * values_in, axis=-1, keepdims=True) + 1e-06)


def attend(
    queries, keys_all, value_rows_full, query_frame, first_seen, score_scale, kv_heads, head_size
):
    site_count, query_frames, width = queries.shape
    key_frames = keys_all.shape[1]
    groups = width // head_size // kv_heads
    q_five = queries.reshape(site_count, query_frames, kv_heads, groups, head_size)
    k_four = keys_all.reshape(site_count, key_frames, kv_heads, head_size)
    v_four = value_rows_full.reshape(site_count, key_frames, kv_heads, head_size)
    scores = jnp.einsum("sqkgd,stkd->kgqts", q_five, k_four, preferred_element_type=jnp.float32)
    scores = scores * (score_scale.reshape(kv_heads, groups, 1, 1, 1) / math.sqrt(head_size))
    key_ids = jnp.arange(key_frames, dtype=jnp.int32)[None, :, None]
    query_ids = query_frame[:, None, None]
    seen = (key_ids <= query_ids) & (
        (key_ids >= first_seen[None, None, :]) | (key_ids == query_ids)
    )
    scores = jnp.where(seen[None, None], scores, -1e30)
    top_score = jnp.max(scores, axis=-2, keepdims=True)
    weights = jnp.exp(scores - top_score)
    probs = (weights / jnp.sum(weights, axis=-2, keepdims=True)).astype(jnp.bfloat16)
    attended = jnp.einsum("kgqts,stkd->sqkgd", probs, v_four, preferred_element_type=jnp.float32)
    return attended.astype(jnp.bfloat16).reshape(site_count, query_frames, width)


def plain_body(
    fields,
    band_rows,
    earliest_past_snapshot,
    lat_table,
    norm_gain,
    w_in1,
    b_in1,
    w_out2,
    b_out2,
    w_query,
    w_keyval,
    w_output,
    score_scale,
    spec_cot,
):
    samples, _, lat_rows, lon_local, width = fields.shape
    grid_rows = samples * lat_rows
    length = lon_local * lax.axis_size("lon")
    modes = spec_cot.shape[4]
    local_width = spec_cot.shape[5]
    blocks = w_in1.shape[1]
    block_size = w_in1.shape[2]
    forward = transform_table(length, modes)
    backward = inverse_table(forward, modes)
    scale_t = 1.0 / math.sqrt(length)
    lat_count = lat_table.shape[0]
    onehot = (
        band_rows[:, :, None] == jnp.arange(lat_count, dtype=jnp.int32)[None, None, :]
    ).astype(jnp.bfloat16)
    embedding = jnp.dot(
        onehot.reshape(grid_rows, lat_count), lat_table, preferred_element_type=jnp.float32
    )
    inputs = fields[:, 0].astype(jnp.float32) + embedding.reshape(samples, lat_rows, 1, width)
    center = jnp.mean(inputs, axis=-1, keepdims=True)
    spread = jnp.mean(jnp.square(inputs - center), axis=-1, keepdims=True)
    normed = ((inputs - center) * lax.rsqrt(spread + 1e-05) * norm_gain).astype(jnp.bfloat16)
    gathered = lax.all_to_all(
        normed.reshape(grid_rows, lon_local, width), "lon", split_axis=2, concat_axis=1, tiled=True
    )
    spectrum = (
        jnp.einsum("rnc,nk->rkc", gathered, forward, preferred_element_type=jnp.float32) * scale_t
    ).astype(jnp.bfloat16)
    spectrum = spectrum.reshape(grid_rows, 2, modes, blocks, block_size)
    first_re, first_im, mixed = filter_modes(
        spectrum,
        w_in1,
        b_in1.reshape(2, blocks, block_size),
        w_out2,
        b_out2.reshape(2, blocks, block_size),
    )
    mixed = mixed.reshape(grid_rows, 2 * modes, local_width)
    grid_part = (
        jnp.einsum("rkc,nk->rnc", mixed, backward, preferred_element_type=jnp.float32) * scale_t
    ).astype(jnp.bfloat16)
    returned = lax.all_to_all(grid_part, "lon", split_axis=1, concat_axis=2, tiled=True)
    hidden = (
        inputs + returned.reshape(samples, lat_rows, lon_local, width).astype(jnp.float32)
    ).astype(jnp.bfloat16)
    cotangent = spec_cot.reshape(grid_rows, 2, modes, blocks, block_size)
    grad_re = jnp.einsum(
        "rmgc,rmge->gce", first_re, cotangent[:, 0], preferred_element_type=jnp.float32
    )
    grad_re = grad_re + jnp.einsum(
        "rmgc,rmge->gce", first_im, cotangent[:, 1], preferred_element_type=jnp.float32
    )
    grad_im = jnp.einsum(
        "rmgc,rmge->gce", first_re, cotangent[:, 1], preferred_element_type=jnp.float32
    )
    grad_im = grad_im - jnp.einsum(
        "rmgc,rmge->gce", first_im, cotangent[:, 0], preferred_element_type=jnp.float32
    )
    bias_terms = jnp.sum(cotangent.astype(jnp.float32), axis=(0, 2)).reshape(2, local_width)
    mask_coefficient2_derivative, mask_offset2_derivative = lax.psum(
        (jnp.stack([grad_re, grad_im]), bias_terms), ("dp", "frame")
    )
    site_count = grid_rows * lon_local
    tokens = hidden.reshape(site_count, width)
    head_count = score_scale.shape[0]
    head_size = width // head_count
    kv_width = w_keyval.shape[1] // 2
    kv_heads = kv_width // head_size
    query = jnp.dot(tokens, w_query, preferred_element_type=jnp.float32).reshape(
        site_count, head_count, head_size
    )
    qnorm = head_norm(query).astype(jnp.bfloat16).reshape(site_count, 1, width)
    keyval = jnp.dot(tokens, w_keyval, preferred_element_type=jnp.float32)
    knorm = (
        head_norm(keyval[:, :kv_width].reshape(site_count, kv_heads, head_size))
        .astype(jnp.bfloat16)
        .reshape(site_count, 1, kv_width)
    )
    values = keyval[:, kv_width:].astype(jnp.bfloat16).reshape(site_count, 1, kv_width)
    first_seen = jnp.broadcast_to(
        earliest_past_snapshot[:, None], (samples, lat_rows * lon_local)
    ).reshape(site_count)
    own_frame = lax.axis_index("frame")
    keys_all, value_rows_full = (
        lax.all_gather(knorm, "frame", axis=1, tiled=True),
        lax.all_gather(values, "frame", axis=1, tiled=True),
    )
    query_frame = jnp.reshape(own_frame, (1,))
    attended = attend(
        qnorm, keys_all, value_rows_full, query_frame, first_seen, score_scale, kv_heads, head_size
    )
    output = jnp.dot(
        attended.reshape(site_count, width), w_output, preferred_element_type=jnp.float32
    )
    predicted_output_fields = (
        (tokens.astype(jnp.float32) + output)
        .astype(jnp.bfloat16)
        .reshape(samples, 1, lat_rows, lon_local, width)
    )
    return (predicted_output_fields, mask_coefficient2_derivative, mask_offset2_derivative)


def basis_rank(window, length, modes):
    return -(-(window * (2 * modes - 1) // length + 24) // 16) * 16


def body(fields, *rest):
    width, local_width = fields.shape[-1], rest[-1].shape[-1]
    head_size = width // rest[-2].shape[0]
    fits = (
        fields.shape[0] == 1
        and lax.axis_size("frame") == 2
        and local_width % LANES == 0
        and fields.shape[2] == sum(rows for step, _, rows, _ in PLAN if step == "compress")
        and 2 * head_size == 128
        and 2 * rest[4].shape[2] == 128
        and rest[-4].shape[1] * 2 == width
    )
    sizes = [lax.axis_size(axis) for axis in ("frame", "dp")]
    fits = fits and all(size & (size - 1) == 0 for size in sizes)
    return (fused_body if fits else plain_body)(fields, *rest)


def solution(mesh):
    placed = (
        P("dp", "frame", None, "lon", None),
        P("dp", None),
        P("dp"),
        P(),
        P(),
        P(None, "lon", None, None),
        P(None, "lon"),
        P(None, "lon", None, None),
        P(None, "lon"),
        P(),
        P(),
        P(),
        P(),
        P("dp", "frame", None, None, None, "lon"),
    )
    return jax.shard_map(
        body,
        mesh=mesh,
        in_specs=placed,
        out_specs=(P("dp", "frame", None, "lon", None), P(None, "lon", None, None), P(None, "lon")),
        check_vma=False,
    )
```

```python
import functools
import math

import jax
import jax.numpy as jnp
import ml_dtypes
import numpy as np
from jax import lax
from jax.experimental import pallas as pl
from jax.experimental.pallas import tpu as pltpu
from jax.sharding import PartitionSpec as P


def window_basis(window, length, modes, rank):
    band = 2 * modes - 1
    site = np.arange(window)
    step = np.arange(1, window)
    diagonal = -np.cos(np.pi * (window - 1 - 2 * site) / length) * np.cos(np.pi * band / length)
    beside = np.sin(np.pi * step / length) * np.sin(np.pi * (window - step) / length)
    _, vectors = np.linalg.eigh(np.diag(diagonal) + np.diag(beside, 1) + np.diag(beside, -1))
    basis = vectors[:, ::-1][:, :rank]
    lead = np.argmax(np.abs(basis) > 1e-3, axis=0)
    return basis * np.sign(basis[lead, np.arange(rank)])[None, :]


def window_tables(window, length, modes, rank):
    basis = window_basis(window, length, modes, rank)
    turns = np.arange(length)[:, None] * np.arange(modes)[None, :] % length
    angles = 2.0 * np.pi * turns / length
    table = np.concatenate([np.cos(angles), -np.sin(angles)], axis=1)
    factor = np.where(np.arange(2 * modes) % modes == 0, 1.0, 2.0)
    parts = table.reshape(length // window, window, 2 * modes)
    spread = np.einsum("pnj,nr->prj", parts, basis) / math.sqrt(length)
    fold = np.transpose(spread, (2, 0, 1)).reshape(2 * modes, -1)
    unfold = spread * factor

    def small(array):
        return (np.round(array * 2.0**16) / 2.0**16).astype(ml_dtypes.bfloat16)

    return small(basis), small(basis.T), small(fold), small(unfold)


LANES = 256
F32 = jnp.float32
BF16 = jnp.bfloat16


def dot(left, right):
    return jnp.dot(left, right, preferred_element_type=F32)


def row_tiles(rows, size):
    return [(low, min(low + size, rows)) for low in range(0, rows, size)]


def latitude_row(band, block):
    rows = block.astype(F32)
    place = lax.broadcasted_iota(jnp.int32, rows.shape, 0)
    return jnp.sum(jnp.where(place == band % rows.shape[0], rows, 0.0), axis=0, keepdims=True)


def compress_kernel(start, band_ref, x_ref, lat_ref, gain_ref, basis_ref, *rest):
    *outs, normed_ref = rest
    rows, width = x_ref.shape
    embed = latitude_row(band_ref[0, start + pl.program_id(0)], lat_ref[...])
    gain = gain_ref[...]
    for low, high in row_tiles(rows, 16):
        inputs = x_ref[low:high].astype(F32) + embed
        center = jnp.sum(inputs, axis=-1, keepdims=True) * (1.0 / width)
        inputs = inputs - center
        spread = jnp.sum(inputs * inputs, axis=-1, keepdims=True) * (1.0 / width)
        normed_ref[low:high] = (inputs * lax.rsqrt(spread + 1e-05) * gain).astype(BF16)
    size = width // lax.axis_size("lon")
    for block, store in outgoing(outs):
        columns = pl.ds(pl.multiple_of(block * size, size), size)
        store(dot(basis_ref[...], normed_ref[:, columns]).astype(BF16))


def outgoing(outs):
    count = lax.axis_size("lon")
    if len(outs) == 1:
        return [(block, functools.partial(outs[0].__setitem__, block)) for block in range(count)]
    me = lax.axis_index("lon")
    return [
        (lax.rem(me + shift, count), functools.partial(out.__setitem__, ...))
        for shift, out in enumerate(outs)
    ]


def incoming(parts):
    count = lax.axis_size("lon")
    if len(parts) == 1:
        return [(owner, parts[0][owner]) for owner in range(count)]
    me = lax.axis_index("lon")
    return [(lax.rem(me + count - shift, count), part[...]) for shift, part in enumerate(parts)]


def blocks_kernel(w1_ref, w2_ref, mix1_ref, mix2_ref):
    _, blocks, size, _ = w1_ref.shape
    width = blocks * size
    for weight, mix in ((w1_ref, mix1_ref), (w2_ref, mix2_ref)):
        mix[...] = jnp.zeros(mix.shape, mix.dtype)
        for block in range(blocks):
            low = block * size
            here, there = slice(low, low + size), slice(width + low, width + low + size)
            real, imag = weight[0, block], weight[1, block]
            mix[here, here] = real
            mix[here, there] = imag
            mix[there, here] = -imag
            mix[there, there] = real


def filter_kernel(taken, *refs):
    parts, refs = refs[:taken], refs[taken:]
    fold_ref, w1_ref, b1_ref, w2_ref, b2_ref, first_ref, mixed_ref, whole_ref = refs
    rank, width = parts[0].shape[-2:]
    modes = first_ref.shape[0] // 2
    for owner, part in incoming(parts):
        whole_ref[pl.ds(pl.multiple_of(owner * rank, 16), rank)] = part
    spectrum = dot(fold_ref[...], whole_ref[...]).astype(BF16)
    spectrum = jnp.concatenate([spectrum[:modes], spectrum[modes:]], axis=1)
    first = jnp.maximum(dot(spectrum, w1_ref[...]) + both_parts(b1_ref), 0.0).astype(BF16)
    first_ref[:modes] = first[:, :width]
    first_ref[modes:] = first[:, width:]
    mixed = (dot(first, w2_ref[...]) + both_parts(b2_ref)).astype(BF16)
    mixed_ref[:modes] = mixed[:, :width]
    mixed_ref[modes:] = mixed[:, width:]


def both_parts(ref):
    return jnp.concatenate([ref[0:1], ref[1:2]], axis=1)


def unfold_kernel(mixed_ref, unfold_ref, *outs):
    sums = [(store, dot(unfold_ref[block], mixed_ref[...])) for block, store in outgoing(outs)]
    for store, part in sums:
        store(part.astype(BF16))


def gradient_kernel(size, *refs):
    *firsts, cot_ref, packed_ref = refs
    modes, width = cot_ref.shape[2:]
    contract = (((0,), (0,)), ((), ()))
    total, bias, row = 0.0, 0.0, 0
    for first_ref in firsts:
        for piece in range(first_ref.shape[0]):
            real, imag = cot_ref[row, 0], cot_ref[row, 1]
            both = jnp.concatenate([real, imag], axis=1)
            turned = jnp.concatenate([imag, -real], axis=1)
            first_re, first_im = first_ref[piece, :modes], first_ref[piece, modes:]
            total += lax.dot_general(first_re, both, contract, preferred_element_type=F32)
            total += lax.dot_general(first_im, turned, contract, preferred_element_type=F32)
            bias += jnp.sum(both.astype(F32), axis=0, keepdims=True)
            row += 1
    pair = 2 * size
    lane = lax.broadcasted_iota(jnp.int32, (size, pair), 1)
    out = 0
    for low in range(0, 2 * width, pair):
        left = low % width
        even = total[left : left + size, low : low + pair]
        odd = total[left + size : left + pair, low : low + pair]
        packed_ref[out : out + size] = jnp.where(lane < size, even, odd)
        out += size
    packed_ref[out:] = jnp.zeros((packed_ref.shape[0] - out, pair), F32)
    for place, low in enumerate(range(0, 2 * width, pair)):
        packed_ref[out + place : out + place + 1] = bias[:, low : low + pair]


def unpack_kernel(summed_ref, weight_ref, bias_ref):
    _, blocks, size, _ = weight_ref.shape
    total = summed_ref[...]
    out = 0
    for part in range(2):
        for block in range(0, blocks, 2):
            weight_ref[part, block] = total[out : out + size, :size]
            weight_ref[part, block + 1] = total[out : out + size, size:]
            out += size
    for part in range(2):
        for low in range(0, bias_ref.shape[1], 2 * size):
            bias_ref[part : part + 1, low : low + 2 * size] = total[out : out + 1]
            out += 1


def head_scale(values, ones):
    squares = (values * values).astype(BF16)
    return values * lax.rsqrt(dot(squares, ones) + 1e-06)


def head_ones(head_size, value):
    row = lax.broadcasted_iota(jnp.int32, (LANES, LANES), 0) // head_size
    column = lax.broadcasted_iota(jnp.int32, (LANES, LANES), 1) // head_size
    return jnp.where(row == column, value, 0.0).astype(BF16)


def expand_kernel(start, taken, head_size, band_ref, x_ref, lat_ref, *refs):
    parts, refs = refs[:taken], refs[taken:]
    basis_ref, w_keyval_ref, hidden_ref, *keyval_refs, whole_ref = refs
    count, _, width = whole_ref.shape
    for owner, part in incoming(parts):
        whole_ref[owner] = part
    embed = latitude_row(band_ref[0, start + pl.program_id(0)], lat_ref[...])
    grids = [dot(basis_ref[...], whole_ref[block]).astype(BF16) for block in range(count)]
    inputs = x_ref[...].astype(F32) + embed
    hidden = (inputs + jnp.concatenate(grids, axis=1).astype(F32)).astype(BF16)
    hidden_ref[...] = hidden
    keyval = dot(hidden, w_keyval_ref[...])
    ones = head_ones(head_size, 1.0 / head_size)
    half = keyval.shape[1] // 2
    keys = [head_scale(keyval[:, low : low + LANES], ones) for low in range(0, half, LANES)]
    keyval = jnp.concatenate([*keys, keyval[:, half:]], axis=1).astype(BF16)
    low = 0
    for out in keyval_refs:
        out[...] = keyval[:, low : low + out.shape[1]]
        low += out.shape[1]


def query_kernel(head_size, hidden_ref, w_query_ref, query_ref):
    ones = head_ones(head_size, 1.0 / head_size)
    tiles = [slice(low, low + LANES) for low in range(0, query_ref.shape[1], LANES)]
    queries = [dot(hidden_ref[...], w_query_ref[:, columns]) for columns in tiles]
    means = [dot((query * query).astype(BF16), ones) for query in queries]
    for columns, query, mean in zip(tiles, queries, means):
        query_ref[:, columns] = (query * lax.rsqrt(mean + 1e-06)).astype(BF16)


def repeat_head(pair, upper, head_size):
    lane = lax.broadcasted_iota(jnp.int32, pair.shape, 1)
    rolled = pltpu.roll(pair, head_size, 1)
    return jnp.where((lane < head_size) != upper, pair, rolled)


def twice(part):
    return jnp.concatenate([part, part], axis=1)


def attend_kernel(head_size, groups, past_ref, scale_ref, *refs):
    out_ref = refs[-1]
    w_ref = refs[sum(2 + 2 * taken for _, _, taken in groups)]
    for first, last, taken in groups:
        size = 2 + 2 * taken
        mine, refs = refs[:size], refs[size:]
        row = pl.program_id(0)

        @pl.when(jnp.logical_and(row >= first, row < last))
        def _(mine=mine, taken=taken):
            attend_row(head_size, taken, past_ref, scale_ref, *mine, w_ref, out_ref)


def attend_row(head_size, taken, past_ref, scale_ref, query_ref, *refs):
    own_refs, other_refs, refs = refs[:taken], refs[taken : 2 * taken], refs[2 * taken :]
    hidden_ref, w_ref, out_ref = refs
    half = sum(ref.shape[1] for ref in own_refs) // 2
    pair_width = 2 * head_size
    group = LANES // head_size
    ones = head_ones(head_size, 1.0)
    ones = jnp.concatenate([ones, ones], axis=0)
    lane_head = lax.broadcasted_iota(jnp.int32, (1, LANES), 1) // head_size
    seen = jnp.logical_and(lax.axis_index("frame") == 1, past_ref[0] <= 0)

    def load(refs, low):
        size = refs[0].shape[1]
        return refs[low // size][:, low % size : low % size + pair_width].astype(F32)

    leads, attended = [], []
    heads = range(half // head_size)
    for head in heads:
        pair = head // 2 * pair_width
        step = repeat_head(load(other_refs, pair) - load(own_refs, pair), head % 2 == 1, head_size)
        product = query_ref[:, head * LANES : head * LANES + LANES].astype(F32) * twice(step)
        high = product.astype(BF16)
        low = (product - high.astype(F32)).astype(BF16)
        leads.append(dot(jnp.concatenate([high, low], axis=1), ones))
    for head in heads:
        pair = half + head // 2 * pair_width
        value = load(own_refs, pair)
        reach = jnp.where(seen, 0.5 * (load(other_refs, pair) - value), 0.0)
        scale = jnp.zeros((1, LANES), F32)
        for place in range(group):
            scale = jnp.where(lane_head == place, scale_ref[head * group + place], scale)
        share = jnp.tanh(leads[head] * (scale * (0.5 / math.sqrt(head_size))))
        middle, reach = (twice(repeat_head(part, head % 2 == 1, head_size)) for part in (value + reach, reach))
        attended.append((middle + reach * share).astype(BF16))
    output = dot(jnp.concatenate(attended, axis=1), w_ref[...])
    out_ref[...] = (hidden_ref[...].astype(F32) + output).astype(BF16)


def fixed(array):
    return pl.BlockSpec(array.shape, lambda *_, rank=len(array.shape): (0,) * rank)


def by_row(array, low=0, lead=0):
    before, after = array.shape[:lead], array.shape[lead + 1 :]
    return pl.BlockSpec(
        (*before, None, *after), lambda i, *_: (0,) * len(before) + (low + i,) + (0,) * len(after)
    )


def within(array, start):
    rows, *rest = array.shape
    return pl.BlockSpec(
        (None, *rest), lambda i, *_: (jnp.clip(i - start, 0, rows - 1),) + (0,) * len(rest)
    )


class Order:
    def __init__(self):
        self.last = None
        self.after = []

    def __call__(self, kernel, prefetch, args, specs, outs, out_specs, scratch, flops, grid=(1,), alias=None):
        anywhere = pl.BlockSpec(memory_space=pl.ANY)
        token = jax.ShapeDtypeStruct((8, 128), F32)
        taken = self.after + ([] if self.last is None else [self.last])
        self.after = []
        skip, count = len(prefetch) + len(args), len(outs)

        def ordered(*refs):
            refs = refs[:skip] + refs[skip + len(taken) :]
            give = len(prefetch) + len(args) + count
            kernel(*refs[:give], *refs[give + 1 :])

        *results, self.last = call(
            ordered,
            prefetch,
            tuple(args) + tuple(taken),
            [*specs, *[anywhere] * len(taken)],
            [*outs, token],
            [*out_specs, anywhere],
            scratch,
            flops,
            grid,
            alias,
        )
        return results


def call(kernel, prefetch, args, specs, outs, out_specs, scratch, flops, grid=(1,), alias=None):
    moved = 2 * sum(math.prod(out.shape) * out.dtype.itemsize for out in outs)
    return pl.pallas_call(
        kernel,
        grid_spec=pltpu.PrefetchScalarGridSpec(
            num_scalar_prefetch=len(prefetch),
            grid=grid,
            in_specs=specs,
            out_specs=out_specs,
            scratch_shapes=scratch,
        ),
        out_shape=outs,
        input_output_aliases=alias or {},
        compiler_params=pltpu.CompilerParams(vmem_limit_bytes=VMEM_BYTES),
        cost_estimate=pl.CostEstimate(flops=1024, bytes_accessed=1024, transcendentals=0),
    )(*prefetch, *args)


VMEM_BYTES = 24 * 1024 * 1024


def held(array):
    return pltpu.with_memory_space_constraint(array, pltpu.HBM)


def swap_blocks(parts, count):
    if len(parts) == 1:
        return [lax.all_to_all(parts[0], "lon", 0, 0, tiled=True)]
    moved = [
        lax.ppermute(part, "lon", [(i, (i + shift) % count) for i in range(count)])
        for shift, part in enumerate(parts)
        if shift
    ]
    return [parts[0], *moved]


def exchanges(axis):
    size = lax.axis_size(axis)
    step = 1
    while step < size:
        yield axis, [(i, i ^ step) for i in range(size)]
        step *= 2


def fused_body(
    fields,
    band_rows,
    earliest_past_snapshot,
    lat_table,
    norm_gain,
    w_in1,
    b_in1,
    w_out2,
    b_out2,
    w_query,
    w_keyval,
    w_output,
    score_scale,
    spec_cot,
):
    _, _, lat_rows, window, width = fields.shape
    count = lax.axis_size("lon")
    length = window * count
    modes, local_width = spec_cot.shape[4:]
    _, blocks, block_size, _ = w_in1.shape
    head_size = width // score_scale.shape[0]
    keyval_width = w_keyval.shape[1]
    rank = basis_rank(window, length, modes)
    basis, basis_t, fold, unfold = window_tables(window, length, modes, rank)
    gain = norm_gain.reshape(1, width)

    run = Order()

    def struct(*shape, dtype=BF16):
        return jax.ShapeDtypeStruct(shape, dtype)

    def row_specs(start):
        return [
            pl.BlockSpec((None, None, None, window, width), lambda i, *_: (0, 0, start + i, 0, 0)),
            pl.BlockSpec((16, width), lambda i, band: (band[0, start + i] // 16, 0)),
        ]

    def part_outs(rows, at_once):
        if at_once:
            return [struct(count, rows, rank, local_width)]
        return [struct(rows, rank, local_width)] * count

    def compress(start, rows, at_once):
        outs = part_outs(rows, at_once)
        return run(
            functools.partial(compress_kernel, start),
            (band_rows,),
            tuple(held(a) for a in (fields, lat_table, gain, basis_t)),
            [*row_specs(start), fixed(gain), fixed(basis_t)],
            outs,
            [by_row(out, lead=len(out.shape) - 3) for out in outs],
            [pltpu.VMEM((window, width), BF16)],
            2 * rows * rank * window * width,
            grid=(rows,),
        )

    def mix(parts, low, rows):
        args = (fold, mix1, b_in1, mix2, b_out2)
        outs = [struct(rows, 2 * modes, local_width)] * 2
        return run(
            functools.partial(filter_kernel, len(parts)),
            (),
            (*parts, *args),
            [*[by_row(part, low, part.ndim - 3) for part in parts], *[fixed(a) for a in args]],
            outs,
            [by_row(out) for out in outs],
            [pltpu.VMEM((count * rank, local_width), BF16)],
            rows * (16 * modes * local_width * local_width + 4 * modes * local_width * rank * count),
            grid=(rows,),
        )

    def unmix(mixed, at_once):
        rows = mixed.shape[0]
        outs = part_outs(rows, at_once)
        return run(
            unfold_kernel,
            (),
            (mixed, unfold),
            [by_row(mixed), fixed(unfold)],
            outs,
            [by_row(out, lead=len(out.shape) - 3) for out in outs],
            [],
            rows * 4 * modes * local_width * rank * count,
            grid=(rows,),
        )

    def expand(start, parts, low, rows, split):
        args = (basis, w_keyval)
        pieces = 2 if split else 1
        outs = [struct(rows, window, width), *[struct(rows, window, keyval_width // pieces)] * pieces]
        return run(
            functools.partial(expand_kernel, start, len(parts), head_size),
            (band_rows,),
            (fields, held(lat_table), *parts, *args),
            [*row_specs(start), *[by_row(part, low, part.ndim - 3) for part in parts], *[fixed(a) for a in args]],
            outs,
            [by_row(out) for out in outs],
            [pltpu.VMEM((count, rank, local_width), BF16)],
            2 * rows * window * width * (rank + keyval_width),
            grid=(rows,),
        )

    def gradient(firsts):
        args = (*firsts, spec_cot.reshape(spec_cot.shape[2:]))
        packed = struct(blocks * block_size + 8, 2 * block_size, dtype=F32)
        return run(
            functools.partial(gradient_kernel, block_size),
            (),
            args,
            [fixed(a) for a in args],
            [packed],
            [fixed(packed)],
            [],
            8 * lat_rows * modes * local_width * local_width,
        )[0]

    def unpack(summed):
        outs = [struct(*w_out2.shape, dtype=F32), struct(*b_out2.shape, dtype=F32)]
        specs = [fixed(out) for out in outs]
        return run(unpack_kernel, (), (summed,), [fixed(summed)], outs, specs, [], 0)

    def project(hidden):
        return run(
            functools.partial(query_kernel, head_size),
            (),
            (hidden, w_query),
            [by_row(hidden), fixed(w_query)],
            [struct(*hidden.shape)],
            [by_row(hidden)],
            [],
            2 * hidden.size * width,
            grid=(hidden.shape[0],),
        )[0]

    def attention(start, rows, filled):
        args, specs, groups = [], [], []
        for low in sorted(set(cells) & set(range(start, start + rows))):
            query, own, other, hidden = cells[low]
            mine = (query, *own, *other, hidden)
            groups.append((low - start, low - start + query.shape[0], len(own)))
            args += mine
            specs += [within(a, low - start) for a in mine]
        args.append(w_output)
        specs.append(fixed(w_output))
        alias = None
        if filled is not None:
            alias = {2 + len(args): 0}
            args.append(filled)
            specs.append(pl.BlockSpec(memory_space=pl.ANY))
        return run(
            functools.partial(attend_kernel, head_size, groups),
            (earliest_past_snapshot, score_scale),
            args,
            specs,
            [struct(*fields.shape)],
            [pl.BlockSpec((None, None, None, window, width), lambda i, *_: (0, 0, start + i, 0, 0))],
            [],
            4 * rows * window * width * width,
            grid=(rows,),
            alias=alias,
        )[0]

    predicted = None
    received, mixes, firsts, homeward, cells = {}, {}, [], {}, {}
    for step, start, rows, at_once in PLAN:
        if step == "compress":
            parts = swap_blocks(compress(start, rows, at_once), count)
            received.update({start + low: (parts, low) for low in range(rows)})
        elif step == "blocks":
            weights = [w_in1, w_out2]
            mix_shape = struct(2 * local_width, 2 * local_width)
            mix1, mix2 = run(
                blocks_kernel, (), weights, [fixed(a) for a in weights], [mix_shape] * 2, [fixed(mix_shape)] * 2, [], 0
            )
        elif step == "mix":
            first, mixes[start] = mix(*received[start], rows)
            firsts.append(first)
        elif step == "unmix":
            parts = swap_blocks(unmix(mixes[start], at_once), count)
            homeward.update({start + low: (parts, low) for low in range(rows)})
        elif step == "expand":
            hidden, *keyval = expand(start, *homeward[start], rows, at_once)
            earlier = [lax.ppermute(part, "frame", [(0, 1)]) for part in keyval]
            cells[start] = (keyval, earlier, hidden)
        elif step == "received":
            run.after.append(received[start][0][rows])
        elif step == "returned":
            run.after.append(homeward[start][0][rows])
        elif step == "query":
            cells[start] = (project(cells[start][-1]), *cells[start])
        elif step == "attend":
            predicted = attention(start, rows, predicted)
        elif step == "gradient":
            summed = gradient(firsts)
            rounds = [*exchanges("frame"), *exchanges("dp")]
            crossing = lax.ppermute(summed, *rounds.pop(0))
        elif step == "add":
            summed = summed + crossing
            if rounds:
                crossing = lax.ppermute(summed, *rounds.pop(0))
                run.after.append(summed)
        elif step == "sum":
            gradients = unpack(summed)
    return (predicted, *gradients)


PLAN = (
    ("compress", 0, 2, False),
    ("received", 0, 1, False),
    ("compress", 2, 2, False),
    ("blocks", 0, 0, False),
    ("mix", 0, 2, False),
    ("unmix", 0, 2, False),
    ("mix", 2, 2, False),
    ("gradient", 0, 0, False),
    ("returned", 0, 2, False),
    ("unmix", 2, 2, False),
    ("expand", 0, 2, True),
    ("query", 0, 2, False),
    ("expand", 2, 1, False),
    ("expand", 3, 1, False),
    ("query", 2, 1, False),
    ("query", 3, 1, False),
    ("add", 0, 0, False),
    ("attend", 0, 3, False),
    ("add", 0, 0, False),
    ("attend", 3, 1, False),
    ("add", 0, 0, False),
    ("sum", 0, 0, False),
)


def transform_table(length, modes):
    longitude = jnp.arange(length, dtype=jnp.int32)
    zonal_wavenumber = jnp.arange(modes, dtype=jnp.int32)
    turns_mod = longitude[:, None] * zonal_wavenumber[None, :] % length
    angles = turns_mod.astype(jnp.float32) * (2.0 * math.pi / length)
    return jnp.concatenate([jnp.cos(angles), -jnp.sin(angles)], axis=1).astype(jnp.bfloat16)


def inverse_table(forward, modes):
    zonal_wavenumber = jnp.arange(modes, dtype=jnp.int32)
    factor = jnp.where(zonal_wavenumber == 0, 1.0, 2.0).astype(jnp.float32)
    factor = jnp.concatenate([factor, factor])
    return (forward.astype(jnp.float32) * factor[None, :]).astype(jnp.bfloat16)


def block_mix(left, weight):
    return jnp.einsum("rmgc,gce->rmge", left, weight, preferred_element_type=jnp.float32)


def filter_modes(spectrum, w_in1, b_in1, w_out2, b_out2):
    spectral_real = spectrum[:, 0]
    spec_im = spectrum[:, 1]
    first_re = jax.nn.relu(
        block_mix(spectral_real, w_in1[0]) - block_mix(spec_im, w_in1[1]) + b_in1[0]
    ).astype(jnp.bfloat16)
    first_im = jax.nn.relu(
        block_mix(spectral_real, w_in1[1]) + block_mix(spec_im, w_in1[0]) + b_in1[1]
    ).astype(jnp.bfloat16)
    second_re = (
        block_mix(first_re, w_out2[0]) - block_mix(first_im, w_out2[1]) + b_out2[0]
    ).astype(jnp.bfloat16)
    second_im = (
        block_mix(first_re, w_out2[1]) + block_mix(first_im, w_out2[0]) + b_out2[1]
    ).astype(jnp.bfloat16)
    return (first_re, first_im, jnp.concatenate([second_re, second_im], axis=1))


def head_norm(values_in):
    return values_in * lax.rsqrt(jnp.mean(values_in * values_in, axis=-1, keepdims=True) + 1e-06)


def attend(
    queries, keys_all, value_rows_full, query_frame, first_seen, score_scale, kv_heads, head_size
):
    site_count, query_frames, width = queries.shape
    key_frames = keys_all.shape[1]
    groups = width // head_size // kv_heads
    q_five = queries.reshape(site_count, query_frames, kv_heads, groups, head_size)
    k_four = keys_all.reshape(site_count, key_frames, kv_heads, head_size)
    v_four = value_rows_full.reshape(site_count, key_frames, kv_heads, head_size)
    scores = jnp.einsum("sqkgd,stkd->kgqts", q_five, k_four, preferred_element_type=jnp.float32)
    scores = scores * (score_scale.reshape(kv_heads, groups, 1, 1, 1) / math.sqrt(head_size))
    key_ids = jnp.arange(key_frames, dtype=jnp.int32)[None, :, None]
    query_ids = query_frame[:, None, None]
    seen = (key_ids <= query_ids) & (
        (key_ids >= first_seen[None, None, :]) | (key_ids == query_ids)
    )
    scores = jnp.where(seen[None, None], scores, -1e30)
    top_score = jnp.max(scores, axis=-2, keepdims=True)
    weights = jnp.exp(scores - top_score)
    probs = (weights / jnp.sum(weights, axis=-2, keepdims=True)).astype(jnp.bfloat16)
    attended = jnp.einsum("kgqts,stkd->sqkgd", probs, v_four, preferred_element_type=jnp.float32)
    return attended.astype(jnp.bfloat16).reshape(site_count, query_frames, width)


def plain_body(
    fields,
    band_rows,
    earliest_past_snapshot,
    lat_table,
    norm_gain,
    w_in1,
    b_in1,
    w_out2,
    b_out2,
    w_query,
    w_keyval,
    w_output,
    score_scale,
    spec_cot,
):
    samples, _, lat_rows, lon_local, width = fields.shape
    grid_rows = samples * lat_rows
    length = lon_local * lax.axis_size("lon")
    modes = spec_cot.shape[4]
    local_width = spec_cot.shape[5]
    blocks = w_in1.shape[1]
    block_size = w_in1.shape[2]
    forward = transform_table(length, modes)
    backward = inverse_table(forward, modes)
    scale_t = 1.0 / math.sqrt(length)
    lat_count = lat_table.shape[0]
    onehot = (
        band_rows[:, :, None] == jnp.arange(lat_count, dtype=jnp.int32)[None, None, :]
    ).astype(jnp.bfloat16)
    embedding = jnp.dot(
        onehot.reshape(grid_rows, lat_count), lat_table, preferred_element_type=jnp.float32
    )
    inputs = fields[:, 0].astype(jnp.float32) + embedding.reshape(samples, lat_rows, 1, width)
    center = jnp.mean(inputs, axis=-1, keepdims=True)
    spread = jnp.mean(jnp.square(inputs - center), axis=-1, keepdims=True)
    normed = ((inputs - center) * lax.rsqrt(spread + 1e-05) * norm_gain).astype(jnp.bfloat16)
    gathered = lax.all_to_all(
        normed.reshape(grid_rows, lon_local, width), "lon", split_axis=2, concat_axis=1, tiled=True
    )
    spectrum = (
        jnp.einsum("rnc,nk->rkc", gathered, forward, preferred_element_type=jnp.float32) * scale_t
    ).astype(jnp.bfloat16)
    spectrum = spectrum.reshape(grid_rows, 2, modes, blocks, block_size)
    first_re, first_im, mixed = filter_modes(
        spectrum,
        w_in1,
        b_in1.reshape(2, blocks, block_size),
        w_out2,
        b_out2.reshape(2, blocks, block_size),
    )
    mixed = mixed.reshape(grid_rows, 2 * modes, local_width)
    grid_part = (
        jnp.einsum("rkc,nk->rnc", mixed, backward, preferred_element_type=jnp.float32) * scale_t
    ).astype(jnp.bfloat16)
    returned = lax.all_to_all(grid_part, "lon", split_axis=1, concat_axis=2, tiled=True)
    hidden = (
        inputs + returned.reshape(samples, lat_rows, lon_local, width).astype(jnp.float32)
    ).astype(jnp.bfloat16)
    cotangent = spec_cot.reshape(grid_rows, 2, modes, blocks, block_size)
    grad_re = jnp.einsum(
        "rmgc,rmge->gce", first_re, cotangent[:, 0], preferred_element_type=jnp.float32
    )
    grad_re = grad_re + jnp.einsum(
        "rmgc,rmge->gce", first_im, cotangent[:, 1], preferred_element_type=jnp.float32
    )
    grad_im = jnp.einsum(
        "rmgc,rmge->gce", first_re, cotangent[:, 1], preferred_element_type=jnp.float32
    )
    grad_im = grad_im - jnp.einsum(
        "rmgc,rmge->gce", first_im, cotangent[:, 0], preferred_element_type=jnp.float32
    )
    bias_terms = jnp.sum(cotangent.astype(jnp.float32), axis=(0, 2)).reshape(2, local_width)
    mask_coefficient2_derivative, mask_offset2_derivative = lax.psum(
        (jnp.stack([grad_re, grad_im]), bias_terms), ("dp", "frame")
    )
    site_count = grid_rows * lon_local
    tokens = hidden.reshape(site_count, width)
    head_count = score_scale.shape[0]
    head_size = width // head_count
    kv_width = w_keyval.shape[1] // 2
    kv_heads = kv_width // head_size
    query = jnp.dot(tokens, w_query, preferred_element_type=jnp.float32).reshape(
        site_count, head_count, head_size
    )
    qnorm = head_norm(query).astype(jnp.bfloat16).reshape(site_count, 1, width)
    keyval = jnp.dot(tokens, w_keyval, preferred_element_type=jnp.float32)
    knorm = (
        head_norm(keyval[:, :kv_width].reshape(site_count, kv_heads, head_size))
        .astype(jnp.bfloat16)
        .reshape(site_count, 1, kv_width)
    )
    values = keyval[:, kv_width:].astype(jnp.bfloat16).reshape(site_count, 1, kv_width)
    first_seen = jnp.broadcast_to(
        earliest_past_snapshot[:, None], (samples, lat_rows * lon_local)
    ).reshape(site_count)
    own_frame = lax.axis_index("frame")
    keys_all, value_rows_full = (
        lax.all_gather(knorm, "frame", axis=1, tiled=True),
        lax.all_gather(values, "frame", axis=1, tiled=True),
    )
    query_frame = jnp.reshape(own_frame, (1,))
    attended = attend(
        qnorm, keys_all, value_rows_full, query_frame, first_seen, score_scale, kv_heads, head_size
    )
    output = jnp.dot(
        attended.reshape(site_count, width), w_output, preferred_element_type=jnp.float32
    )
    predicted_output_fields = (
        (tokens.astype(jnp.float32) + output)
        .astype(jnp.bfloat16)
        .reshape(samples, 1, lat_rows, lon_local, width)
    )
    return (predicted_output_fields, mask_coefficient2_derivative, mask_offset2_derivative)


def basis_rank(window, length, modes):
    return -(-(window * (2 * modes - 1) // length + 24) // 16) * 16


def body(fields, *rest):
    width, local_width = fields.shape[-1], rest[-1].shape[-1]
    head_size = width // rest[-2].shape[0]
    fits = (
        fields.shape[0] == 1
        and lax.axis_size("frame") == 2
        and local_width % LANES == 0
        and fields.shape[2] == sum(rows for step, _, rows, _ in PLAN if step == "compress")
        and 2 * head_size == 128
        and 2 * rest[4].shape[2] == 128
        and rest[-4].shape[1] * 2 == width
    )
    sizes = [lax.axis_size(axis) for axis in ("frame", "dp")]
    fits = fits and all(size & (size - 1) == 0 for size in sizes)
    return (fused_body if fits else plain_body)(fields, *rest)


def solution(mesh):
    placed = (
        P("dp", "frame", None, "lon", None),
        P("dp", None),
        P("dp"),
        P(),
        P(),
        P(None, "lon", None, None),
        P(None, "lon"),
        P(None, "lon", None, None),
        P(None, "lon"),
        P(),
        P(),
        P(),
        P(),
        P("dp", "frame", None, None, None, "lon"),
    )
    return jax.shard_map(
        body,
        mesh=mesh,
        in_specs=placed,
        out_specs=(P("dp", "frame", None, "lon", None), P(None, "lon", None, None), P(None, "lon")),
        check_vma=False,
    )
```

```python
import functools
import math

import jax
import jax.numpy as jnp
import ml_dtypes
import numpy as np
from jax import lax
from jax.experimental import pallas as pl
from jax.experimental.pallas import tpu as pltpu
from jax.sharding import PartitionSpec as P


def window_basis(window, length, modes, rank):
    band = 2 * modes - 1
    site = np.arange(window)
    step = np.arange(1, window)
    diagonal = -np.cos(np.pi * (window - 1 - 2 * site) / length) * np.cos(np.pi * band / length)
    beside = np.sin(np.pi * step / length) * np.sin(np.pi * (window - step) / length)
    _, vectors = np.linalg.eigh(np.diag(diagonal) + np.diag(beside, 1) + np.diag(beside, -1))
    basis = vectors[:, ::-1][:, :rank]
    lead = np.argmax(np.abs(basis) > 1e-3, axis=0)
    return basis * np.sign(basis[lead, np.arange(rank)])[None, :]


def window_tables(window, length, modes, rank):
    basis = window_basis(window, length, modes, rank)
    turns = np.arange(length)[:, None] * np.arange(modes)[None, :] % length
    angles = 2.0 * np.pi * turns / length
    table = np.concatenate([np.cos(angles), -np.sin(angles)], axis=1)
    factor = np.where(np.arange(2 * modes) % modes == 0, 1.0, 2.0)
    parts = table.reshape(length // window, window, 2 * modes)
    spread = np.einsum("pnj,nr->prj", parts, basis) / math.sqrt(length)
    fold = np.transpose(spread, (2, 0, 1)).reshape(2 * modes, -1)
    unfold = spread * factor

    def small(array):
        return (np.round(array * 2.0**16) / 2.0**16).astype(ml_dtypes.bfloat16)

    return small(basis), small(basis.T), small(fold), small(unfold)


LANES = 256
F32 = jnp.float32
BF16 = jnp.bfloat16


def dot(left, right):
    return jnp.dot(left, right, preferred_element_type=F32)


def row_tiles(rows, size):
    return [(low, min(low + size, rows)) for low in range(0, rows, size)]


def latitude_row(band, block):
    rows = block.astype(F32)
    place = lax.broadcasted_iota(jnp.int32, rows.shape, 0)
    return jnp.sum(jnp.where(place == band % rows.shape[0], rows, 0.0), axis=0, keepdims=True)


def compress_kernel(start, band_ref, x_ref, lat_ref, gain_ref, basis_ref, *rest):
    *outs, normed_ref = rest
    rows, width = x_ref.shape
    embed = latitude_row(band_ref[0, start + pl.program_id(0)], lat_ref[...])
    gain = gain_ref[...]
    for low, high in row_tiles(rows, 16):
        inputs = x_ref[low:high].astype(F32) + embed
        center = jnp.sum(inputs, axis=-1, keepdims=True) * (1.0 / width)
        inputs = inputs - center
        spread = jnp.sum(inputs * inputs, axis=-1, keepdims=True) * (1.0 / width)
        normed_ref[low:high] = (inputs * lax.rsqrt(spread + 1e-05) * gain).astype(BF16)
    size = width // lax.axis_size("lon")
    for block, store in outgoing(outs):
        columns = pl.ds(pl.multiple_of(block * size, size), size)
        store(dot(basis_ref[...], normed_ref[:, columns]).astype(BF16))


def outgoing(outs):
    count = lax.axis_size("lon")
    if len(outs) == 1:
        return [(block, functools.partial(outs[0].__setitem__, block)) for block in range(count)]
    me = lax.axis_index("lon")
    return [
        (lax.rem(me + shift, count), functools.partial(out.__setitem__, ...))
        for shift, out in enumerate(outs)
    ]


def incoming(parts):
    count = lax.axis_size("lon")
    if len(parts) == 1:
        return [(owner, parts[0][owner]) for owner in range(count)]
    me = lax.axis_index("lon")
    return [(lax.rem(me + count - shift, count), part[...]) for shift, part in enumerate(parts)]


def blocks_kernel(w1_ref, w2_ref, mix1_ref, mix2_ref):
    _, blocks, size, _ = w1_ref.shape
    width = blocks * size
    for weight, mix in ((w1_ref, mix1_ref), (w2_ref, mix2_ref)):
        mix[...] = jnp.zeros(mix.shape, mix.dtype)
        for block in range(blocks):
            low = block * size
            here, there = slice(low, low + size), slice(width + low, width + low + size)
            real, imag = weight[0, block], weight[1, block]
            mix[here, here] = real
            mix[here, there] = imag
            mix[there, here] = -imag
            mix[there, there] = real


def filter_kernel(taken, *refs):
    parts, refs = refs[:taken], refs[taken:]
    fold_ref, w1_ref, b1_ref, w2_ref, b2_ref, first_ref, mixed_ref, whole_ref = refs
    rank, width = parts[0].shape[-2:]
    modes = first_ref.shape[0] // 2
    for owner, part in incoming(parts):
        whole_ref[pl.ds(pl.multiple_of(owner * rank, 16), rank)] = part
    spectrum = dot(fold_ref[...], whole_ref[...]).astype(BF16)
    spectrum = jnp.concatenate([spectrum[:modes], spectrum[modes:]], axis=1)
    first = jnp.maximum(dot(spectrum, w1_ref[...]) + both_parts(b1_ref), 0.0).astype(BF16)
    first_ref[:modes] = first[:, :width]
    first_ref[modes:] = first[:, width:]
    mixed = (dot(first, w2_ref[...]) + both_parts(b2_ref)).astype(BF16)
    mixed_ref[:modes] = mixed[:, :width]
    mixed_ref[modes:] = mixed[:, width:]


def both_parts(ref):
    return jnp.concatenate([ref[0:1], ref[1:2]], axis=1)


def unfold_kernel(mixed_ref, unfold_ref, *outs):
    sums = [(store, dot(unfold_ref[block], mixed_ref[...])) for block, store in outgoing(outs)]
    for store, part in sums:
        store(part.astype(BF16))


def gradient_kernel(size, *refs):
    *firsts, cot_ref, packed_ref = refs
    modes, width = cot_ref.shape[2:]
    contract = (((0,), (0,)), ((), ()))
    total, bias, row = 0.0, 0.0, 0
    for first_ref in firsts:
        for piece in range(first_ref.shape[0]):
            real, imag = cot_ref[row, 0], cot_ref[row, 1]
            both = jnp.concatenate([real, imag], axis=1)
            turned = jnp.concatenate([imag, -real], axis=1)
            first_re, first_im = first_ref[piece, :modes], first_ref[piece, modes:]
            total += lax.dot_general(first_re, both, contract, preferred_element_type=F32)
            total += lax.dot_general(first_im, turned, contract, preferred_element_type=F32)
            bias += jnp.sum(both.astype(F32), axis=0, keepdims=True)
            row += 1
    pair = 2 * size
    lane = lax.broadcasted_iota(jnp.int32, (size, pair), 1)
    out = 0
    for low in range(0, 2 * width, pair):
        left = low % width
        even = total[left : left + size, low : low + pair]
        odd = total[left + size : left + pair, low : low + pair]
        packed_ref[out : out + size] = jnp.where(lane < size, even, odd)
        out += size
    packed_ref[out:] = jnp.zeros((packed_ref.shape[0] - out, pair), F32)
    for place, low in enumerate(range(0, 2 * width, pair)):
        packed_ref[out + place : out + place + 1] = bias[:, low : low + pair]


def unpack_kernel(summed_ref, weight_ref, bias_ref):
    _, blocks, size, _ = weight_ref.shape
    total = summed_ref[...]
    out = 0
    for part in range(2):
        for block in range(0, blocks, 2):
            weight_ref[part, block] = total[out : out + size, :size]
            weight_ref[part, block + 1] = total[out : out + size, size:]
            out += size
    for part in range(2):
        for low in range(0, bias_ref.shape[1], 2 * size):
            bias_ref[part : part + 1, low : low + 2 * size] = total[out : out + 1]
            out += 1


def head_scale(values, ones):
    squares = (values * values).astype(BF16)
    return values * lax.rsqrt(dot(squares, ones) + 1e-06)


def head_ones(head_size, value):
    row = lax.broadcasted_iota(jnp.int32, (LANES, LANES), 0) // head_size
    column = lax.broadcasted_iota(jnp.int32, (LANES, LANES), 1) // head_size
    return jnp.where(row == column, value, 0.0).astype(BF16)


def expand_kernel(start, taken, head_size, band_ref, x_ref, lat_ref, *refs):
    parts, refs = refs[:taken], refs[taken:]
    basis_ref, w_keyval_ref, hidden_ref, *keyval_refs, whole_ref = refs
    count, _, width = whole_ref.shape
    for owner, part in incoming(parts):
        whole_ref[owner] = part
    embed = latitude_row(band_ref[0, start + pl.program_id(0)], lat_ref[...])
    grids = [dot(basis_ref[...], whole_ref[block]).astype(BF16) for block in range(count)]
    inputs = x_ref[...].astype(F32) + embed
    hidden = (inputs + jnp.concatenate(grids, axis=1).astype(F32)).astype(BF16)
    hidden_ref[...] = hidden
    keyval = dot(hidden, w_keyval_ref[...])
    ones = head_ones(head_size, 1.0 / head_size)
    half = keyval.shape[1] // 2
    keys = [head_scale(keyval[:, low : low + LANES], ones) for low in range(0, half, LANES)]
    keyval = jnp.concatenate([*keys, keyval[:, half:]], axis=1).astype(BF16)
    low = 0
    for out in keyval_refs:
        out[...] = keyval[:, low : low + out.shape[1]]
        low += out.shape[1]


def query_kernel(head_size, hidden_ref, w_query_ref, query_ref):
    ones = head_ones(head_size, 1.0 / head_size)
    tiles = [slice(low, low + LANES) for low in range(0, query_ref.shape[1], LANES)]
    queries = [dot(hidden_ref[...], w_query_ref[:, columns]) for columns in tiles]
    means = [dot((query * query).astype(BF16), ones) for query in queries]
    for columns, query, mean in zip(tiles, queries, means):
        query_ref[:, columns] = (query * lax.rsqrt(mean + 1e-06)).astype(BF16)


def repeat_head(pair, upper, head_size):
    lane = lax.broadcasted_iota(jnp.int32, pair.shape, 1)
    rolled = pltpu.roll(pair, head_size, 1)
    return jnp.where((lane < head_size) != upper, pair, rolled)


def twice(part):
    return jnp.concatenate([part, part], axis=1)


def attend_kernel(head_size, groups, past_ref, scale_ref, *refs):
    out_ref = refs[-1]
    w_ref = refs[sum(2 + 2 * taken for _, _, taken in groups)]
    for first, last, taken in groups:
        size = 2 + 2 * taken
        mine, refs = refs[:size], refs[size:]
        row = pl.program_id(0)

        @pl.when(jnp.logical_and(row >= first, row < last))
        def _(mine=mine, taken=taken):
            attend_row(head_size, taken, past_ref, scale_ref, *mine, w_ref, out_ref)


def attend_row(head_size, taken, past_ref, scale_ref, query_ref, *refs):
    own_refs, other_refs, refs = refs[:taken], refs[taken : 2 * taken], refs[2 * taken :]
    hidden_ref, w_ref, out_ref = refs
    half = sum(ref.shape[1] for ref in own_refs) // 2
    pair_width = 2 * head_size
    group = LANES // head_size
    ones = head_ones(head_size, 1.0)
    ones = jnp.concatenate([ones, ones], axis=0)
    lane_head = lax.broadcasted_iota(jnp.int32, (1, LANES), 1) // head_size
    seen = jnp.logical_and(lax.axis_index("frame") == 1, past_ref[0] <= 0)

    def load(refs, low):
        size = refs[0].shape[1]
        return refs[low // size][:, low % size : low % size + pair_width].astype(F32)

    leads, attended = [], []
    heads = range(half // head_size)
    for head in heads:
        pair = head // 2 * pair_width
        step = repeat_head(load(other_refs, pair) - load(own_refs, pair), head % 2 == 1, head_size)
        product = query_ref[:, head * LANES : head * LANES + LANES].astype(F32) * twice(step)
        high = product.astype(BF16)
        low = (product - high.astype(F32)).astype(BF16)
        leads.append(dot(jnp.concatenate([high, low], axis=1), ones))
    for head in heads:
        pair = half + head // 2 * pair_width
        value = load(own_refs, pair)
        reach = jnp.where(seen, 0.5 * (load(other_refs, pair) - value), 0.0)
        scale = jnp.zeros((1, LANES), F32)
        for place in range(group):
            scale = jnp.where(lane_head == place, scale_ref[head * group + place], scale)
        share = jnp.tanh(leads[head] * (scale * (0.5 / math.sqrt(head_size))))
        middle, reach = (twice(repeat_head(part, head % 2 == 1, head_size)) for part in (value + reach, reach))
        attended.append((middle + reach * share).astype(BF16))
    output = dot(jnp.concatenate(attended, axis=1), w_ref[...])
    out_ref[...] = (hidden_ref[...].astype(F32) + output).astype(BF16)


def fixed(array):
    return pl.BlockSpec(array.shape, lambda *_, rank=len(array.shape): (0,) * rank)


def by_row(array, low=0, lead=0):
    before, after = array.shape[:lead], array.shape[lead + 1 :]
    return pl.BlockSpec(
        (*before, None, *after), lambda i, *_: (0,) * len(before) + (low + i,) + (0,) * len(after)
    )


def within(array, start):
    rows, *rest = array.shape
    return pl.BlockSpec(
        (None, *rest), lambda i, *_: (jnp.clip(i - start, 0, rows - 1),) + (0,) * len(rest)
    )


class Order:
    def __init__(self):
        self.last = None
        self.after = []

    def __call__(self, kernel, prefetch, args, specs, outs, out_specs, scratch, flops, grid=(1,), alias=None):
        anywhere = pl.BlockSpec(memory_space=pl.ANY)
        token = jax.ShapeDtypeStruct((8, 128), F32)
        taken = self.after + ([] if self.last is None else [self.last])
        self.after = []
        skip, count = len(prefetch) + len(args), len(outs)

        def ordered(*refs):
            refs = refs[:skip] + refs[skip + len(taken) :]
            give = len(prefetch) + len(args) + count
            kernel(*refs[:give], *refs[give + 1 :])

        *results, self.last = call(
            ordered,
            prefetch,
            tuple(args) + tuple(taken),
            [*specs, *[anywhere] * len(taken)],
            [*outs, token],
            [*out_specs, anywhere],
            scratch,
            flops,
            grid,
            alias,
        )
        return results


def call(kernel, prefetch, args, specs, outs, out_specs, scratch, flops, grid=(1,), alias=None):
    moved = 2 * sum(math.prod(out.shape) * out.dtype.itemsize for out in outs)
    return pl.pallas_call(
        kernel,
        grid_spec=pltpu.PrefetchScalarGridSpec(
            num_scalar_prefetch=len(prefetch),
            grid=grid,
            in_specs=specs,
            out_specs=out_specs,
            scratch_shapes=scratch,
        ),
        out_shape=outs,
        input_output_aliases=alias or {},
        compiler_params=pltpu.CompilerParams(vmem_limit_bytes=VMEM_BYTES),
        cost_estimate=pl.CostEstimate(flops=1024, bytes_accessed=1024, transcendentals=0),
    )(*prefetch, *args)


VMEM_BYTES = 24 * 1024 * 1024


def held(array):
    return pltpu.with_memory_space_constraint(array, pltpu.HBM)


def swap_blocks(parts, count):
    if len(parts) == 1:
        return [lax.all_to_all(parts[0], "lon", 0, 0, tiled=True)]
    moved = [
        lax.ppermute(part, "lon", [(i, (i + shift) % count) for i in range(count)])
        for shift, part in enumerate(parts)
        if shift
    ]
    return [parts[0], *moved]


def exchanges(axis):
    size = lax.axis_size(axis)
    step = 1
    while step < size:
        yield axis, [(i, i ^ step) for i in range(size)]
        step *= 2


def fused_body(
    fields,
    band_rows,
    earliest_past_snapshot,
    lat_table,
    norm_gain,
    w_in1,
    b_in1,
    w_out2,
    b_out2,
    w_query,
    w_keyval,
    w_output,
    score_scale,
    spec_cot,
):
    _, _, lat_rows, window, width = fields.shape
    count = lax.axis_size("lon")
    length = window * count
    modes, local_width = spec_cot.shape[4:]
    _, blocks, block_size, _ = w_in1.shape
    head_size = width // score_scale.shape[0]
    keyval_width = w_keyval.shape[1]
    rank = basis_rank(window, length, modes)
    basis, basis_t, fold, unfold = window_tables(window, length, modes, rank)
    gain = norm_gain.reshape(1, width)

    run = Order()

    def struct(*shape, dtype=BF16):
        return jax.ShapeDtypeStruct(shape, dtype)

    def row_specs(start):
        return [
            pl.BlockSpec((None, None, None, window, width), lambda i, *_: (0, 0, start + i, 0, 0)),
            pl.BlockSpec((16, width), lambda i, band: (band[0, start + i] // 16, 0)),
        ]

    def part_outs(rows, at_once):
        if at_once:
            return [struct(count, rows, rank, local_width)]
        return [struct(rows, rank, local_width)] * count

    def compress(start, rows, at_once):
        outs = part_outs(rows, at_once)
        return run(
            functools.partial(compress_kernel, start),
            (band_rows,),
            tuple(held(a) for a in (fields, lat_table, gain, basis_t)),
            [*row_specs(start), fixed(gain), fixed(basis_t)],
            outs,
            [by_row(out, lead=len(out.shape) - 3) for out in outs],
            [pltpu.VMEM((window, width), BF16)],
            2 * rows * rank * window * width,
            grid=(rows,),
        )

    def mix(parts, low, rows):
        args = (fold, mix1, b_in1, mix2, b_out2)
        outs = [struct(rows, 2 * modes, local_width)] * 2
        return run(
            functools.partial(filter_kernel, len(parts)),
            (),
            (*parts, *args),
            [*[by_row(part, low, part.ndim - 3) for part in parts], *[fixed(a) for a in args]],
            outs,
            [by_row(out) for out in outs],
            [pltpu.VMEM((count * rank, local_width), BF16)],
            rows * (16 * modes * local_width * local_width + 4 * modes * local_width * rank * count),
            grid=(rows,),
        )

    def unmix(mixed, at_once):
        rows = mixed.shape[0]
        outs = part_outs(rows, at_once)
        return run(
            unfold_kernel,
            (),
            (mixed, unfold),
            [by_row(mixed), fixed(unfold)],
            outs,
            [by_row(out, lead=len(out.shape) - 3) for out in outs],
            [],
            rows * 4 * modes * local_width * rank * count,
            grid=(rows,),
        )

    def expand(start, parts, low, rows, split):
        args = (basis, w_keyval)
        pieces = 2 if split else 1
        outs = [struct(rows, window, width), *[struct(rows, window, keyval_width // pieces)] * pieces]
        return run(
            functools.partial(expand_kernel, start, len(parts), head_size),
            (band_rows,),
            (fields, held(lat_table), *parts, *args),
            [*row_specs(start), *[by_row(part, low, part.ndim - 3) for part in parts], *[fixed(a) for a in args]],
            outs,
            [by_row(out) for out in outs],
            [pltpu.VMEM((count, rank, local_width), BF16)],
            2 * rows * window * width * (rank + keyval_width),
            grid=(rows,),
        )

    def gradient(firsts):
        args = (*firsts, spec_cot.reshape(spec_cot.shape[2:]))
        packed = struct(blocks * block_size + 8, 2 * block_size, dtype=F32)
        return run(
            functools.partial(gradient_kernel, block_size),
            (),
            args,
            [fixed(a) for a in args],
            [packed],
            [fixed(packed)],
            [],
            8 * lat_rows * modes * local_width * local_width,
        )[0]

    def unpack(summed):
        outs = [struct(*w_out2.shape, dtype=F32), struct(*b_out2.shape, dtype=F32)]
        specs = [fixed(out) for out in outs]
        return run(unpack_kernel, (), (summed,), [fixed(summed)], outs, specs, [], 0)

    def project(hidden):
        return run(
            functools.partial(query_kernel, head_size),
            (),
            (hidden, w_query),
            [by_row(hidden), fixed(w_query)],
            [struct(*hidden.shape)],
            [by_row(hidden)],
            [],
            2 * hidden.size * width,
            grid=(hidden.shape[0],),
        )[0]

    def attention(start, rows, filled):
        args, specs, groups = [], [], []
        for low in sorted(set(cells) & set(range(start, start + rows))):
            query, own, other, hidden = cells[low]
            mine = (query, *own, *other, hidden)
            groups.append((low - start, low - start + query.shape[0], len(own)))
            args += mine
            specs += [within(a, low - start) for a in mine]
        args.append(w_output)
        specs.append(fixed(w_output))
        alias = None
        if filled is not None:
            alias = {2 + len(args): 0}
            args.append(filled)
            specs.append(pl.BlockSpec(memory_space=pl.ANY))
        return run(
            functools.partial(attend_kernel, head_size, groups),
            (earliest_past_snapshot, score_scale),
            args,
            specs,
            [struct(*fields.shape)],
            [pl.BlockSpec((None, None, None, window, width), lambda i, *_: (0, 0, start + i, 0, 0))],
            [],
            4 * rows * window * width * width,
            grid=(rows,),
            alias=alias,
        )[0]

    predicted = None
    received, mixes, firsts, homeward, cells = {}, {}, [], {}, {}
    for step, start, rows, at_once in PLAN:
        if step == "compress":
            parts = swap_blocks(compress(start, rows, at_once), count)
            received.update({start + low: (parts, low) for low in range(rows)})
        elif step == "blocks":
            weights = [w_in1, w_out2]
            mix_shape = struct(2 * local_width, 2 * local_width)
            mix1, mix2 = run(
                blocks_kernel, (), weights, [fixed(a) for a in weights], [mix_shape] * 2, [fixed(mix_shape)] * 2, [], 0
            )
        elif step == "mix":
            first, mixes[start] = mix(*received[start], rows)
            firsts.append(first)
        elif step == "unmix":
            parts = swap_blocks(unmix(mixes[start], at_once), count)
            homeward.update({start + low: (parts, low) for low in range(rows)})
        elif step == "expand":
            hidden, *keyval = expand(start, *homeward[start], rows, at_once)
            earlier = [lax.ppermute(part, "frame", [(0, 1)]) for part in keyval]
            cells[start] = (keyval, earlier, hidden)
        elif step == "received":
            run.after.append(received[start][0][rows])
        elif step == "returned":
            run.after.append(homeward[start][0][rows])
        elif step == "query":
            cells[start] = (project(cells[start][-1]), *cells[start])
        elif step == "attend":
            predicted = attention(start, rows, predicted)
        elif step == "gradient":
            summed = gradient(firsts)
            rounds = [*exchanges("frame"), *exchanges("dp")]
            crossing = lax.ppermute(summed, *rounds.pop(0))
        elif step == "add":
            summed = summed + crossing
            if rounds:
                crossing = lax.ppermute(summed, *rounds.pop(0))
                run.after.append(summed)
        elif step == "sum":
            gradients = unpack(summed)
    return (predicted, *gradients)


PLAN = (
    ("compress", 0, 2, False),
    ("received", 0, 1, False),
    ("compress", 2, 2, False),
    ("blocks", 0, 0, False),
    ("mix", 0, 2, False),
    ("unmix", 0, 2, False),
    ("mix", 2, 2, False),
    ("gradient", 0, 0, False),
    ("returned", 0, 2, False),
    ("unmix", 2, 2, False),
    ("expand", 0, 2, True),
    ("query", 0, 2, False),
    ("expand", 2, 1, False),
    ("expand", 3, 1, False),
    ("query", 2, 1, False),
    ("add", 0, 0, False),
    ("query", 3, 1, False),
    ("attend", 0, 3, False),
    ("add", 0, 0, False),
    ("add", 0, 0, False),
    ("sum", 0, 0, False),
    ("attend", 3, 1, False),
)


def transform_table(length, modes):
    longitude = jnp.arange(length, dtype=jnp.int32)
    zonal_wavenumber = jnp.arange(modes, dtype=jnp.int32)
    turns_mod = longitude[:, None] * zonal_wavenumber[None, :] % length
    angles = turns_mod.astype(jnp.float32) * (2.0 * math.pi / length)
    return jnp.concatenate([jnp.cos(angles), -jnp.sin(angles)], axis=1).astype(jnp.bfloat16)


def inverse_table(forward, modes):
    zonal_wavenumber = jnp.arange(modes, dtype=jnp.int32)
    factor = jnp.where(zonal_wavenumber == 0, 1.0, 2.0).astype(jnp.float32)
    factor = jnp.concatenate([factor, factor])
    return (forward.astype(jnp.float32) * factor[None, :]).astype(jnp.bfloat16)


def block_mix(left, weight):
    return jnp.einsum("rmgc,gce->rmge", left, weight, preferred_element_type=jnp.float32)


def filter_modes(spectrum, w_in1, b_in1, w_out2, b_out2):
    spectral_real = spectrum[:, 0]
    spec_im = spectrum[:, 1]
    first_re = jax.nn.relu(
        block_mix(spectral_real, w_in1[0]) - block_mix(spec_im, w_in1[1]) + b_in1[0]
    ).astype(jnp.bfloat16)
    first_im = jax.nn.relu(
        block_mix(spectral_real, w_in1[1]) + block_mix(spec_im, w_in1[0]) + b_in1[1]
    ).astype(jnp.bfloat16)
    second_re = (
        block_mix(first_re, w_out2[0]) - block_mix(first_im, w_out2[1]) + b_out2[0]
    ).astype(jnp.bfloat16)
    second_im = (
        block_mix(first_re, w_out2[1]) + block_mix(first_im, w_out2[0]) + b_out2[1]
    ).astype(jnp.bfloat16)
    return (first_re, first_im, jnp.concatenate([second_re, second_im], axis=1))


def head_norm(values_in):
    return values_in * lax.rsqrt(jnp.mean(values_in * values_in, axis=-1, keepdims=True) + 1e-06)


def attend(
    queries, keys_all, value_rows_full, query_frame, first_seen, score_scale, kv_heads, head_size
):
    site_count, query_frames, width = queries.shape
    key_frames = keys_all.shape[1]
    groups = width // head_size // kv_heads
    q_five = queries.reshape(site_count, query_frames, kv_heads, groups, head_size)
    k_four = keys_all.reshape(site_count, key_frames, kv_heads, head_size)
    v_four = value_rows_full.reshape(site_count, key_frames, kv_heads, head_size)
    scores = jnp.einsum("sqkgd,stkd->kgqts", q_five, k_four, preferred_element_type=jnp.float32)
    scores = scores * (score_scale.reshape(kv_heads, groups, 1, 1, 1) / math.sqrt(head_size))
    key_ids = jnp.arange(key_frames, dtype=jnp.int32)[None, :, None]
    query_ids = query_frame[:, None, None]
    seen = (key_ids <= query_ids) & (
        (key_ids >= first_seen[None, None, :]) | (key_ids == query_ids)
    )
    scores = jnp.where(seen[None, None], scores, -1e30)
    top_score = jnp.max(scores, axis=-2, keepdims=True)
    weights = jnp.exp(scores - top_score)
    probs = (weights / jnp.sum(weights, axis=-2, keepdims=True)).astype(jnp.bfloat16)
    attended = jnp.einsum("kgqts,stkd->sqkgd", probs, v_four, preferred_element_type=jnp.float32)
    return attended.astype(jnp.bfloat16).reshape(site_count, query_frames, width)


def plain_body(
    fields,
    band_rows,
    earliest_past_snapshot,
    lat_table,
    norm_gain,
    w_in1,
    b_in1,
    w_out2,
    b_out2,
    w_query,
    w_keyval,
    w_output,
    score_scale,
    spec_cot,
):
    samples, _, lat_rows, lon_local, width = fields.shape
    grid_rows = samples * lat_rows
    length = lon_local * lax.axis_size("lon")
    modes = spec_cot.shape[4]
    local_width = spec_cot.shape[5]
    blocks = w_in1.shape[1]
    block_size = w_in1.shape[2]
    forward = transform_table(length, modes)
    backward = inverse_table(forward, modes)
    scale_t = 1.0 / math.sqrt(length)
    lat_count = lat_table.shape[0]
    onehot = (
        band_rows[:, :, None] == jnp.arange(lat_count, dtype=jnp.int32)[None, None, :]
    ).astype(jnp.bfloat16)
    embedding = jnp.dot(
        onehot.reshape(grid_rows, lat_count), lat_table, preferred_element_type=jnp.float32
    )
    inputs = fields[:, 0].astype(jnp.float32) + embedding.reshape(samples, lat_rows, 1, width)
    center = jnp.mean(inputs, axis=-1, keepdims=True)
    spread = jnp.mean(jnp.square(inputs - center), axis=-1, keepdims=True)
    normed = ((inputs - center) * lax.rsqrt(spread + 1e-05) * norm_gain).astype(jnp.bfloat16)
    gathered = lax.all_to_all(
        normed.reshape(grid_rows, lon_local, width), "lon", split_axis=2, concat_axis=1, tiled=True
    )
    spectrum = (
        jnp.einsum("rnc,nk->rkc", gathered, forward, preferred_element_type=jnp.float32) * scale_t
    ).astype(jnp.bfloat16)
    spectrum = spectrum.reshape(grid_rows, 2, modes, blocks, block_size)
    first_re, first_im, mixed = filter_modes(
        spectrum,
        w_in1,
        b_in1.reshape(2, blocks, block_size),
        w_out2,
        b_out2.reshape(2, blocks, block_size),
    )
    mixed = mixed.reshape(grid_rows, 2 * modes, local_width)
    grid_part = (
        jnp.einsum("rkc,nk->rnc", mixed, backward, preferred_element_type=jnp.float32) * scale_t
    ).astype(jnp.bfloat16)
    returned = lax.all_to_all(grid_part, "lon", split_axis=1, concat_axis=2, tiled=True)
    hidden = (
        inputs + returned.reshape(samples, lat_rows, lon_local, width).astype(jnp.float32)
    ).astype(jnp.bfloat16)
    cotangent = spec_cot.reshape(grid_rows, 2, modes, blocks, block_size)
    grad_re = jnp.einsum(
        "rmgc,rmge->gce", first_re, cotangent[:, 0], preferred_element_type=jnp.float32
    )
    grad_re = grad_re + jnp.einsum(
        "rmgc,rmge->gce", first_im, cotangent[:, 1], preferred_element_type=jnp.float32
    )
    grad_im = jnp.einsum(
        "rmgc,rmge->gce", first_re, cotangent[:, 1], preferred_element_type=jnp.float32
    )
    grad_im = grad_im - jnp.einsum(
        "rmgc,rmge->gce", first_im, cotangent[:, 0], preferred_element_type=jnp.float32
    )
    bias_terms = jnp.sum(cotangent.astype(jnp.float32), axis=(0, 2)).reshape(2, local_width)
    mask_coefficient2_derivative, mask_offset2_derivative = lax.psum(
        (jnp.stack([grad_re, grad_im]), bias_terms), ("dp", "frame")
    )
    site_count = grid_rows * lon_local
    tokens = hidden.reshape(site_count, width)
    head_count = score_scale.shape[0]
    head_size = width // head_count
    kv_width = w_keyval.shape[1] // 2
    kv_heads = kv_width // head_size
    query = jnp.dot(tokens, w_query, preferred_element_type=jnp.float32).reshape(
        site_count, head_count, head_size
    )
    qnorm = head_norm(query).astype(jnp.bfloat16).reshape(site_count, 1, width)
    keyval = jnp.dot(tokens, w_keyval, preferred_element_type=jnp.float32)
    knorm = (
        head_norm(keyval[:, :kv_width].reshape(site_count, kv_heads, head_size))
        .astype(jnp.bfloat16)
        .reshape(site_count, 1, kv_width)
    )
    values = keyval[:, kv_width:].astype(jnp.bfloat16).reshape(site_count, 1, kv_width)
    first_seen = jnp.broadcast_to(
        earliest_past_snapshot[:, None], (samples, lat_rows * lon_local)
    ).reshape(site_count)
    own_frame = lax.axis_index("frame")
    keys_all, value_rows_full = (
        lax.all_gather(knorm, "frame", axis=1, tiled=True),
        lax.all_gather(values, "frame", axis=1, tiled=True),
    )
    query_frame = jnp.reshape(own_frame, (1,))
    attended = attend(
        qnorm, keys_all, value_rows_full, query_frame, first_seen, score_scale, kv_heads, head_size
    )
    output = jnp.dot(
        attended.reshape(site_count, width), w_output, preferred_element_type=jnp.float32
    )
    predicted_output_fields = (
        (tokens.astype(jnp.float32) + output)
        .astype(jnp.bfloat16)
        .reshape(samples, 1, lat_rows, lon_local, width)
    )
    return (predicted_output_fields, mask_coefficient2_derivative, mask_offset2_derivative)


def basis_rank(window, length, modes):
    return -(-(window * (2 * modes - 1) // length + 24) // 16) * 16


def body(fields, *rest):
    width, local_width = fields.shape[-1], rest[-1].shape[-1]
    head_size = width // rest[-2].shape[0]
    fits = (
        fields.shape[0] == 1
        and lax.axis_size("frame") == 2
        and local_width % LANES == 0
        and fields.shape[2] == sum(rows for step, _, rows, _ in PLAN if step == "compress")
        and 2 * head_size == 128
        and 2 * rest[4].shape[2] == 128
        and rest[-4].shape[1] * 2 == width
    )
    sizes = [lax.axis_size(axis) for axis in ("frame", "dp")]
    fits = fits and all(size & (size - 1) == 0 for size in sizes)
    return (fused_body if fits else plain_body)(fields, *rest)


def solution(mesh):
    placed = (
        P("dp", "frame", None, "lon", None),
        P("dp", None),
        P("dp"),
        P(),
        P(),
        P(None, "lon", None, None),
        P(None, "lon"),
        P(None, "lon", None, None),
        P(None, "lon"),
        P(),
        P(),
        P(),
        P(),
        P("dp", "frame", None, None, None, "lon"),
    )
    return jax.shard_map(
        body,
        mesh=mesh,
        in_specs=placed,
        out_specs=(P("dp", "frame", None, "lon", None), P(None, "lon", None, None), P(None, "lon")),
        check_vma=False,
    )
```
